32 devices in a mesh: seq: 8 (over y, x, core), fsdp: 4 (over z).
Axes of the slice: x: 2, y: 2, z: 4, core: 2. Of those that a mesh axis runs over, the one named last changes fastest.
Arguments:
- tokens: bfloat16 [4, 1024, 1536], P('fsdp', 'seq'), may hold values from -6 to 6
- cotangent: bfloat16 [4, 1024, 1536], P('fsdp', 'seq'), may hold values from -6 to 6
- doc_starts: int32 [4, 8], P('fsdp'), may hold values from 0 to 1023, as said below
- mix_gain: float32 [1536], replicated, may hold values from 0.5 to 1.5
- input_proj: bfloat16 [1536, 2048], P('fsdp'), may hold values from -0.15625 to 0.15625
- gelu_proj: bfloat16 [1536, 2048], P('fsdp'), may hold values from -0.15625 to 0.15625
- conv_taps: float32 [4, 2048], replicated, may hold values from -3 to 3
- conv_bias: float32 [2048], replicated, may hold values from -3 to 3
- decay_gate: bfloat16 [2048, 256], P('fsdp'), may hold values from -0.375 to 0.375
- decay_bias: float32 [2048], replicated, may hold values from -4 to 4
- input_gate: bfloat16 [2048, 256], P('fsdp'), may hold values from -0.375 to 0.375
- input_bias: float32 [2048], replicated, may hold values from -4 to 4
- decay_param: float32 [2048], replicated, may hold values from 4 to 11
- output_proj: bfloat16 [2048, 1536], P('fsdp'), may hold values from -0.375 to 0.375
- mlp_gain: float32 [1536], replicated, may hold values from 0.5 to 1.5
- mlp_gate: bfloat16 [1536, 4608], P('fsdp'), may hold values from -0.15625 to 0.15625
- mlp_up: bfloat16 [1536, 4608], P('fsdp'), may hold values from -0.15625 to 0.15625
- mlp_down: bfloat16 [4608, 1536], P('fsdp'), may hold values from -0.1875 to 0.1875
Outputs:
- mixed: bfloat16 [4, 1024, 1536], P('fsdp', 'seq')
- tokens_grad: bfloat16 [4, 1024, 1536], P('fsdp', 'seq')
- mix_gain_grad: float32 [1536], replicated
- input_proj_grad: float32 [1536, 2048], P('fsdp', 'seq')
- gelu_proj_grad: float32 [1536, 2048], P('fsdp', 'seq')
- conv_taps_grad: float32 [4, 2048], replicated
- conv_bias_grad: float32 [2048], replicated
- decay_gate_grad: float32 [2048, 256], P('fsdp', 'seq')
- decay_bias_grad: float32 [2048], replicated
- input_gate_grad: float32 [2048, 256], P('fsdp', 'seq')
- input_bias_grad: float32 [2048], replicated
- decay_param_grad: float32 [2048], replicated
- output_proj_grad: float32 [2048, 1536], P('fsdp', 'seq')
- mlp_gain_grad: float32 [1536], replicated
- mlp_gate_grad: float32 [1536, 4608], P('fsdp', 'seq')
- mlp_up_grad: float32 [1536, 4608], P('fsdp', 'seq')
- mlp_down_grad: float32 [4608, 1536], P('fsdp', 'seq')
The draws below stay inside these ranges and needn't reach their ends.
Inputs may be any that keep to these rules, and one draw needn't show every extreme that they name: `doc_starts`: each row starts with 0 and rises strictly; its entries are the first positions of the documents of that sequence.
All inputs are finite; a program needn't handle non-finite values.
Results may differ from the reference program's by a relative error of at most 0.015.
Values may be sent and summed in bfloat16 or wider, within the bound.
No kernel may reach another device: no remote copies, remote signals or barrier semaphores. Data moves between devices by JAX's collectives and lax.ppermute only.
A program may use at most 448 MiB of HBM per device.

```python
import jax
import jax.numpy as jnp
from jax import lax

D = 1536
R = 2048
F = 4608
BLOCK = 256
CONV = 4
DOCS = 8
LEN = 1024
SEQS = 4


def draw_doc_starts(key, part):
    key = jax.random.fold_in(key, 11)
    row_keys = jax.random.split(key, SEQS)

    def one_row(row_key):
        picks = jax.random.permutation(row_key, LEN - 1)[:DOCS - 1] + 1
        return jnp.concatenate([jnp.zeros((1,), jnp.int32), jnp.sort(picks).astype(jnp.int32)])
    return jax.vmap(one_row)(row_keys)


def steps_of(own_key, shape, shards, least, largest):
    def one(dim, parts):
        steps = jax.random.uniform(jax.random.fold_in(jax.random.fold_in(own_key, 6), dim), (parts,), jnp.float32, least / len(shards), largest / len(shards))
        return jnp.repeat(jnp.exp(steps), shape[dim] // parts).reshape((-1,) + (1,) * (len(shape) - dim - 1))

    level = one(*shards[0])
    for cut in shards[1:]:
        level = level * one(*cut)
    return level


def scatter_about(own_key, dims, deviation, bound, pieces=(), held_as=jnp.bfloat16):
    factor_of = steps_of(own_key, dims, pieces, -0.22, 0.18) if pieces else 1.0
    entries = jax.random.normal(own_key, dims, jnp.float32) * deviation * factor_of
    return jnp.minimum(jnp.maximum(entries, -bound), bound).astype(held_as)


def setup_inputs(seed: int = 0) -> dict:
    key_of = jax.random.split(jax.random.key(seed), 19)
    return {
        "tokens": scatter_about(key_of[0], (SEQS, LEN, D), 1.0, 6.0, ((0, 4), (1, 8))),
        "cotangent": scatter_about(key_of[1], (SEQS, LEN, D), 1.0, 6.0, ((0, 4), (1, 8))),
        "doc_starts": draw_doc_starts(jax.random.fold_in(key_of[18], 71), 0),
        "mix_gain": jnp.clip(1.0 + 0.1 * jax.random.normal(key_of[3], (D,), jnp.float32), 0.5, 1.5),
        "input_proj": scatter_about(key_of[4], (D, R), D ** -0.5, 0.15625, ((0, 4),)),
        "gelu_proj": scatter_about(key_of[5], (D, R), D ** -0.5, 0.15625, ((0, 4),)),
        "conv_taps": scatter_about(key_of[6], (CONV, R), 0.5, 3.0, (), jnp.float32),
        "conv_bias": scatter_about(key_of[7], (R,), 0.5, 3.0, (), jnp.float32),
        "decay_gate": scatter_about(key_of[8], (R, BLOCK), BLOCK ** -0.5, 0.375, ((0, 4),)),
        "decay_bias": scatter_about(key_of[9], (R,), 1.0, 4.0, (), jnp.float32),
        "input_gate": scatter_about(key_of[10], (R, BLOCK), BLOCK ** -0.5, 0.375, ((0, 4),)),
        "input_bias": scatter_about(key_of[11], (R,), 1.0, 4.0, (), jnp.float32),
        "decay_param": jnp.clip(jax.random.uniform(key_of[12], (R,), jnp.float32, 4.0, 11.0), 4.0, 11.0),
        "output_proj": scatter_about(key_of[13], (R, D), (R // 8) ** -0.5, 0.375, ((0, 4),)),
        "mlp_gain": jnp.clip(1.0 + 0.1 * jax.random.normal(key_of[14], (D,), jnp.float32), 0.5, 1.5),
        "mlp_gate": scatter_about(key_of[15], (D, F), D ** -0.5, 0.15625, ((0, 4),)),
        "mlp_up": scatter_about(key_of[16], (D, F), D ** -0.5, 0.15625, ((0, 4),)),
        "mlp_down": scatter_about(key_of[17], (F, D), (F // 4) ** -0.5, 0.1875, ((0, 4),)),
    }


norm_eps = 1e-06
mult_floor = 0.0001
highest = lax.Precision.HIGHEST

@jax.custom_vjp
def low(v):
    return lax.optimization_barrier(v.astype(jnp.bfloat16)).astype(jnp.float32)

@jax.custom_vjp
def low_back(v):
    return v

def low_keep(v):
    return (low(v), None)

def low_pass(kept, grad):
    return (grad,)

def back_keep(v):
    return (v, None)

def back_low(kept, grad):
    return (low(grad),)
low.defvjp(low_keep, low_pass)
low_back.defvjp(back_keep, back_low)

def product(left, right):
    return jnp.dot(left, right, precision=highest)

def block_product(left, weight):
    width = weight.shape[1]
    blocks = weight.shape[0] // width
    result = jnp.einsum('nhk,hkj->nhj', left.reshape(left.shape[0], blocks, width), weight.reshape(blocks, width, width), precision=highest)
    return result.reshape(left.shape[0], -1)

def rms_scale(values, gain):
    scale = lax.rsqrt(lax.optimization_barrier(jnp.mean(values * values, axis=-1, keepdims=True)) + norm_eps)
    return values * scale * gain

def smooth_gelu(values):
    return jax.nn.gelu(values, approximate=True)

def affine_pair(earlier, later):
    return (earlier[0] * later[0], earlier[1] * later[0] + later[1])

def decay_terms(conv_out, decay_pre, input_pre, decay_param, resets):
    log_a = -8.0 * jax.nn.sigmoid(decay_pre) * jax.nn.softplus(-decay_param)
    room = jnp.maximum(-jnp.expm1(2.0 * log_a), mult_floor)
    factor = jnp.where(resets, 1.0, jnp.sqrt(room))
    decay = jnp.where(resets, 0.0, jnp.exp(log_a))
    return (decay, jax.nn.sigmoid(input_pre) * conv_out * factor)

def conv_apply(extended, taps_w, bias, masks):
    taps = taps_w.shape[0]
    rows = masks.shape[1]
    total = jnp.zeros((rows, taps_w.shape[1]), extended.dtype) + bias
    for shift_k in range(taps):
        begin_row = taps - 1 - shift_k
        total = total + taps_w[shift_k] * extended[begin_row:begin_row + rows] * masks[shift_k]
    return total

def doc_masks(starts, positions, taps):
    begin = lax.optimization_barrier(jnp.max(jnp.where(starts[None, :] <= positions[:, None], starts[None, :], 0), axis=1))
    resets = (begin == positions)[:, None]
    masks = jnp.stack([(positions - k >= begin)[:, None] for k in range(taps)]).astype(jnp.float32)
    return (resets, masks)

def forward(values, params, starts):
    mix_gain, input_proj, gelu_proj, conv_taps, conv_bias, decay_gate, decay_bias, input_gate, input_bias, decay_param, output_proj, mlp_gain, mlp_gate, mlp_up, mlp_down = params
    positions = jnp.arange(LEN, dtype=jnp.int32)
    resets, masks = doc_masks(starts.astype(jnp.int32), positions, CONV)
    normed = low(rms_scale(values, mix_gain))
    branch = low_back(low(product(normed, input_proj)))
    gelu_pre = low_back(product(normed, gelu_proj))
    gelu_out = smooth_gelu(gelu_pre)
    padded = jnp.concatenate([jnp.zeros((CONV - 1, R), jnp.float32), branch], axis=0)
    conv_out = low(conv_apply(padded, conv_taps, conv_bias, masks))
    decay_pre = low_back(block_product(conv_out, decay_gate) + decay_bias)
    input_pre = low_back(block_product(conv_out, input_gate) + input_bias)
    decay, driven = decay_terms(conv_out, decay_pre, input_pre, decay_param, resets)
    states = lax.associative_scan(affine_pair, (decay, driven), axis=0)[1]
    states = low_back(low(states))
    merged = low(states * gelu_out)
    middle = values + low_back(product(merged, output_proj))
    normed2 = low(rms_scale(middle, mlp_gain))
    gate = low_back(product(normed2, mlp_gate))
    up_val = low_back(product(normed2, mlp_up))
    hidden = low(smooth_gelu(gate) * up_val)
    return middle + low_back(product(hidden, mlp_down))

def reference(tokens, cotangent, doc_starts, mix_gain, input_proj, gelu_proj, conv_taps, conv_bias, decay_gate, decay_bias, input_gate, input_bias, decay_param, output_proj, mlp_gain, mlp_gate, mlp_up, mlp_down):
    params = tuple((item.astype(jnp.float32) for item in (mix_gain, input_proj, gelu_proj, conv_taps, conv_bias, decay_gate, decay_bias, input_gate, input_bias, decay_param, output_proj, mlp_gain, mlp_gate, mlp_up, mlp_down)))

    def one_sequence(totals, items):
        seq_tokens, seq_cot, starts = items
        result, pull = jax.vjp(lambda v, p: forward(v, p, starts), seq_tokens.astype(jnp.float32), params)
        tok_grad, param_grads = pull(seq_cot.astype(jnp.float32))
        totals = jax.tree.map(lambda left, right: left + right, totals, param_grads)
        return (totals, (result.astype(jnp.bfloat16), tok_grad.astype(jnp.bfloat16)))
    zeros = jax.tree.map(jnp.zeros_like, params)
    totals, (mixed, tokens_grad) = lax.scan(one_sequence, zeros, (tokens, cotangent, doc_starts))
    return (mixed, tokens_grad, totals[0], totals[1], totals[2], totals[3], totals[4], totals[5], totals[6], totals[7], totals[8], totals[9], totals[10], totals[11], totals[12], totals[13], totals[14])
```

```python
import functools

import jax
import jax.numpy as jnp
from jax import lax
from jax.experimental import pallas as pl
from jax.experimental.pallas import tpu as pltpu
from jax.sharding import PartitionSpec as P

norm_eps = 1e-06
mult_floor = 0.0001


def from_behind(x, axis, by):
    devices = lax.axis_size(axis)
    pairs = [(i, i + by) for i in range(devices) if 0 <= i + by < devices]
    return lax.ppermute(x, axis, pairs)


def rms_scale(values, gain):
    scale = lax.rsqrt(jnp.mean(values * values, axis=-1, keepdims=True) + norm_eps)
    return values * scale * gain


def smooth_gelu(values):
    return jax.nn.gelu(values, approximate=True)


def gated_unit(gate, up_val):
    return smooth_gelu(gate) * up_val


def affine_pair(earlier, later):
    return (earlier[0] * later[0], earlier[1] * later[0] + later[1])


def decay_terms(conv_out, decay_pre, input_pre, decay_param, resets):
    log_a = -8.0 * jax.nn.sigmoid(decay_pre) * jax.nn.softplus(-decay_param)
    room = jnp.maximum(-jnp.expm1(2.0 * log_a), mult_floor)
    factor = jnp.where(resets, 1.0, jnp.sqrt(room))
    decay = jnp.where(resets, 0.0, jnp.exp(log_a))
    return (decay, jax.nn.sigmoid(input_pre) * conv_out * factor)


def conv_apply(extended, taps_w, bias, masks):
    taps = taps_w.shape[0]
    rows = masks.shape[1]
    total = jnp.zeros((rows, taps_w.shape[1]), jnp.float32) + bias
    for shift_k in range(taps):
        begin_row = taps - 1 - shift_k
        total = total + taps_w[shift_k] * extended[begin_row : begin_row + rows] * masks[shift_k]
    return total


def block_product(left, weight):
    width = weight.shape[1]
    blocks = weight.shape[0] // width
    result = jnp.einsum(
        "nhk,hkj->nhj",
        left.reshape(left.shape[0], blocks, width),
        weight.reshape(blocks, width, width),
        preferred_element_type=jnp.float32,
    )
    return result.reshape(left.shape[0], -1)


def block_back(grad, weight):
    width = weight.shape[1]
    blocks = weight.shape[0] // width
    result = jnp.einsum(
        "nhj,hkj->nhk",
        grad.reshape(grad.shape[0], blocks, width),
        weight.reshape(blocks, width, width),
        preferred_element_type=jnp.float32,
    )
    return result.reshape(grad.shape[0], -1)


def block_weight_grad(left, grad, width):
    blocks = left.shape[1] // width
    result = jnp.einsum(
        "nhk,nhj->hkj",
        left.reshape(left.shape[0], blocks, width),
        grad.reshape(grad.shape[0], blocks, width),
        preferred_element_type=jnp.float32,
    )
    return result.reshape(blocks * width, width)


def wide_shards(
    tokens,
    cotangent,
    doc_starts,
    mix_gain,
    input_proj,
    gelu_proj,
    conv_taps,
    conv_bias,
    decay_gate,
    decay_bias,
    input_gate,
    input_bias,
    decay_param,
    output_proj,
    mlp_gain,
    mlp_gate,
    mlp_up,
    mlp_down,
):
    rows = tokens.shape[1]
    taps = conv_taps.shape[0]
    width = decay_gate.shape[1]
    input_w, gelu_w, output_w, decay_w, inputg_w, gate_w, up_w, down_w = (
        lax.all_gather(input_proj, "fsdp", axis=0, tiled=True),
        lax.all_gather(gelu_proj, "fsdp", axis=0, tiled=True),
        lax.all_gather(output_proj, "fsdp", axis=0, tiled=True),
        lax.all_gather(decay_gate, "fsdp", axis=0, tiled=True),
        lax.all_gather(input_gate, "fsdp", axis=0, tiled=True),
        lax.all_gather(mlp_gate, "fsdp", axis=0, tiled=True),
        lax.all_gather(mlp_up, "fsdp", axis=0, tiled=True),
        lax.all_gather(mlp_down, "fsdp", axis=0, tiled=True),
    )
    channels = input_w.shape[1]
    first = lax.axis_index("seq") * rows
    positions = first + jnp.arange(rows, dtype=jnp.int32)
    starts = doc_starts[0]
    begin = jnp.max(jnp.where(starts[None, :] <= positions[:, None], starts[None, :], 0), axis=1)
    resets = (begin == positions)[:, None]
    masks = jnp.stack([(positions - k >= begin)[:, None] for k in range(taps)]).astype(jnp.float32)
    values = tokens[0].astype(jnp.float32)
    normed = rms_scale(values, mix_gain).astype(jnp.bfloat16)
    branch = jnp.dot(normed, input_w, preferred_element_type=jnp.float32).astype(jnp.bfloat16)
    gelu_pre = jnp.dot(normed, gelu_w, preferred_element_type=jnp.float32)
    gelu_out = smooth_gelu(gelu_pre)
    previous = from_behind(branch[rows - (taps - 1) :], "seq", 1)
    extended = jnp.concatenate([previous, branch], axis=0).astype(jnp.float32)
    conv_f = conv_apply(extended, conv_taps, conv_bias, masks).astype(jnp.bfloat16)
    conv_val = conv_f.astype(jnp.float32)
    decay_pre = block_product(conv_f, decay_w) + decay_bias
    input_pre = block_product(conv_f, inputg_w) + input_bias
    decay, driven = decay_terms(conv_val, decay_pre, input_pre, decay_param, resets)
    decay_cols, driven_cols = (
        lax.all_to_all(decay, "seq", split_axis=1, concat_axis=0, tiled=True),
        lax.all_to_all(driven, "seq", split_axis=1, concat_axis=0, tiled=True),
    )
    states_cols = lax.associative_scan(affine_pair, (decay_cols, driven_cols), axis=0)[1]
    states_low = lax.all_to_all(
        states_cols.astype(jnp.bfloat16), "seq", split_axis=0, concat_axis=1, tiled=True
    )
    states_val = states_low.astype(jnp.float32)
    merged = (states_val * gelu_out).astype(jnp.bfloat16)
    middle = values + jnp.dot(merged, output_w, preferred_element_type=jnp.float32)
    normed2 = rms_scale(middle, mlp_gain).astype(jnp.bfloat16)
    gate = jnp.dot(normed2, gate_w, preferred_element_type=jnp.float32)
    up_val = jnp.dot(normed2, up_w, preferred_element_type=jnp.float32)
    hidden = gated_unit(gate, up_val).astype(jnp.bfloat16)
    mixed = (middle + jnp.dot(hidden, down_w, preferred_element_type=jnp.float32)).astype(
        jnp.bfloat16
    )
    out_grad = cotangent[0]
    down_grad = jnp.einsum("tf,td->fd", hidden, out_grad, preferred_element_type=jnp.float32)
    hidden_grad = jnp.einsum("td,fd->tf", out_grad, down_w, preferred_element_type=jnp.float32)
    unit_pull = jax.vjp(gated_unit, gate, up_val)[1]
    gate_grad, up_grad = unit_pull(hidden_grad)
    gate_low = gate_grad.astype(jnp.bfloat16)
    up_low = up_grad.astype(jnp.bfloat16)
    gate_w_grad = jnp.einsum("td,tf->df", normed2, gate_low, preferred_element_type=jnp.float32)
    up_w_grad = jnp.einsum("td,tf->df", normed2, up_low, preferred_element_type=jnp.float32)
    mlp_terms = (
        lax.psum_scatter(gate_w_grad, "seq", scatter_dimension=1, tiled=True),
        lax.psum_scatter(up_w_grad, "seq", scatter_dimension=1, tiled=True),
        lax.psum_scatter(down_grad, "seq", scatter_dimension=1, tiled=True),
    )
    mlp_gate_grad, mlp_up_grad, mlp_down_grad = (
        lax.psum_scatter(mlp_terms[0], "fsdp", scatter_dimension=0, tiled=True),
        lax.psum_scatter(mlp_terms[1], "fsdp", scatter_dimension=0, tiled=True),
        lax.psum_scatter(mlp_terms[2], "fsdp", scatter_dimension=0, tiled=True),
    )
    normed2_grad = jnp.einsum(
        "tf,df->td", gate_low, gate_w, preferred_element_type=jnp.float32
    ) + jnp.einsum("tf,df->td", up_low, up_w, preferred_element_type=jnp.float32)
    norm2_pull = jax.vjp(rms_scale, middle, mlp_gain)[1]
    middle_part, mlp_gain_term = norm2_pull(normed2_grad)
    middle_grad = out_grad.astype(jnp.float32) + middle_part
    mixer_grad = middle_grad.astype(jnp.bfloat16)
    output_w_grad = jnp.einsum("tr,td->rd", merged, mixer_grad, preferred_element_type=jnp.float32)
    merged_grad = jnp.einsum("td,rd->tr", mixer_grad, output_w, preferred_element_type=jnp.float32)
    state_low = (merged_grad * gelu_out).astype(jnp.bfloat16)
    gelu_pull = jax.vjp(smooth_gelu, gelu_pre)[1]
    gelu_pre_low = gelu_pull(merged_grad * states_val)[0].astype(jnp.bfloat16)
    grad_cols = lax.all_to_all(state_low, "seq", split_axis=1, concat_axis=0, tiled=True).astype(
        jnp.float32
    )
    width_cols = grad_cols.shape[1]
    next_decay = jnp.concatenate([decay_cols[1:], jnp.zeros((1, width_cols), jnp.float32)], axis=0)
    carried = lax.associative_scan(affine_pair, (next_decay, grad_cols), reverse=True, axis=0)[1]
    prior = jnp.concatenate([jnp.zeros((1, width_cols), jnp.float32), states_cols[:-1]], axis=0)
    decay_grad, driven_grad = (
        lax.all_to_all(carried * prior, "seq", split_axis=0, concat_axis=1, tiled=True),
        lax.all_to_all(carried, "seq", split_axis=0, concat_axis=1, tiled=True),
    )
    terms_pull = jax.vjp(
        lambda conv_in, dpre, ipre, dparam: decay_terms(conv_in, dpre, ipre, dparam, resets),
        conv_val,
        decay_pre,
        input_pre,
        decay_param,
    )[1]
    gate_conv_grad, dpre_grad, ipre_grad, decay_param_term = terms_pull((decay_grad, driven_grad))
    dpre_low = dpre_grad.astype(jnp.bfloat16)
    ipre_low = ipre_grad.astype(jnp.bfloat16)
    decay_w_grad = block_weight_grad(conv_f, dpre_low, width)
    inputg_w_grad = block_weight_grad(conv_f, ipre_low, width)
    conv_grad = gate_conv_grad + block_back(dpre_low, decay_w) + block_back(ipre_low, inputg_w)
    conv_pull = jax.vjp(
        lambda ext, taps_w, bias: conv_apply(ext, taps_w, bias, masks),
        extended,
        conv_taps,
        conv_bias,
    )[1]
    extended_grad, taps_term, conv_bias_term = conv_pull(conv_grad)
    returned = from_behind(extended_grad[: taps - 1], "seq", -1)
    branch_grad = extended_grad[taps - 1 :] + jnp.concatenate(
        [jnp.zeros((rows - (taps - 1), channels), jnp.float32), returned], axis=0
    )
    branch_low = branch_grad.astype(jnp.bfloat16)
    input_w_grad = jnp.einsum("td,tr->dr", normed, branch_low, preferred_element_type=jnp.float32)
    gelu_w_grad = jnp.einsum("td,tr->dr", normed, gelu_pre_low, preferred_element_type=jnp.float32)
    mix_terms = (
        lax.psum_scatter(input_w_grad, "seq", scatter_dimension=1, tiled=True),
        lax.psum_scatter(gelu_w_grad, "seq", scatter_dimension=1, tiled=True),
        lax.psum_scatter(output_w_grad, "seq", scatter_dimension=1, tiled=True),
        lax.psum_scatter(decay_w_grad, "seq", scatter_dimension=1, tiled=True),
        lax.psum_scatter(inputg_w_grad, "seq", scatter_dimension=1, tiled=True),
    )
    input_proj_grad, gelu_proj_grad, output_proj_grad, decay_gate_grad, input_gate_grad = (
        lax.psum_scatter(mix_terms[0], "fsdp", scatter_dimension=0, tiled=True),
        lax.psum_scatter(mix_terms[1], "fsdp", scatter_dimension=0, tiled=True),
        lax.psum_scatter(mix_terms[2], "fsdp", scatter_dimension=0, tiled=True),
        lax.psum_scatter(mix_terms[3], "fsdp", scatter_dimension=0, tiled=True),
        lax.psum_scatter(mix_terms[4], "fsdp", scatter_dimension=0, tiled=True),
    )
    normed_grad = jnp.einsum(
        "tr,dr->td", branch_low, input_w, preferred_element_type=jnp.float32
    ) + jnp.einsum("tr,dr->td", gelu_pre_low, gelu_w, preferred_element_type=jnp.float32)
    norm1_pull = jax.vjp(rms_scale, values, mix_gain)[1]
    values_part, mix_gain_term = norm1_pull(normed_grad)
    tokens_grad = (middle_grad + values_part).astype(jnp.bfloat16)
    (
        mix_gain_grad,
        conv_taps_grad,
        conv_bias_grad,
        decay_bias_grad,
        input_bias_grad,
        decay_param_grad,
        mlp_gain_grad,
    ) = lax.psum(
        (
            mix_gain_term,
            taps_term,
            conv_bias_term,
            jnp.sum(dpre_low.astype(jnp.float32), axis=0),
            jnp.sum(ipre_low.astype(jnp.float32), axis=0),
            decay_param_term,
            mlp_gain_term,
        ),
        ("seq", "fsdp"),
    )
    return (
        mixed[None],
        tokens_grad[None],
        mix_gain_grad,
        input_proj_grad,
        gelu_proj_grad,
        conv_taps_grad,
        conv_bias_grad,
        decay_gate_grad,
        decay_bias_grad,
        input_gate_grad,
        input_bias_grad,
        decay_param_grad,
        output_proj_grad,
        mlp_gain_grad,
        mlp_gate_grad,
        mlp_up_grad,
        mlp_down_grad,
    )


def chip_swap(x, k):
    devices = lax.axis_size("seq")
    return lax.ppermute(x, "seq", [(i, i ^ (2 * k)) for i in range(devices)])


def core_swap(x):
    devices = lax.axis_size("seq")
    return lax.ppermute(x, "seq", [(i, i ^ 1) for i in range(devices)])


def gather_blocks(x):
    chips = lax.axis_size("seq") // 2
    near = [x] + [chip_swap(x, k) for k in range(1, chips)]
    return near, [core_swap(block) for block in near]


def scatter_blocks(near, far):
    chips = near.shape[0]
    pair = near.astype(jnp.float32) + core_swap(far.astype(jnp.bfloat16)).astype(jnp.float32)
    low = pair.astype(jnp.bfloat16)
    total = pair[0]
    for k in range(1, chips):
        total = total + chip_swap(low[k], k).astype(jnp.float32)
    return total


def exchange(x, chip, core):
    chips = x.shape[0]
    parts = [lax.dynamic_index_in_dim(x, chip ^ k, 0, keepdims=False) for k in range(chips)]
    got = jnp.stack([parts[0]] + [chip_swap(parts[k], k) for k in range(1, chips)])
    keep = lax.dynamic_index_in_dim(got, core, 1, keepdims=False)
    give = lax.dynamic_index_in_dim(got, 1 - core, 1, keepdims=False)
    return keep, core_swap(give)


def reorder(parts, index):
    bit = 1
    while bit < len(parts):
        flip = (index & bit) != 0
        parts = [jnp.where(flip, parts[i ^ bit], parts[i]) for i in range(len(parts))]
        bit *= 2
    return parts


def total_over(x, axes):
    for axis in axes:
        devices = lax.axis_size(axis)
        bit = 1
        while bit < devices:
            x = x + lax.ppermute(x, axis, [(i, i ^ bit) for i in range(devices)])
            bit *= 2
    return x


def gelu_parts(v):
    inner = 0.7978845608028654 * (v + 0.044715 * v * v * v)
    th = jnp.tanh(inner)
    value = 0.5 * v * (1.0 + th)
    slope = 0.5 * (1.0 + th) + 0.5 * v * (1.0 - th * th) * (
        0.7978845608028654 * (1.0 + 0.134145 * v * v)
    )
    return value, slope


def sigmoid(v):
    return 1.0 / (1.0 + jnp.exp(-v))


def one_less_exp(v):
    series = -v * (1.0 + v * (0.5 + v * (1.0 / 6.0 + v * (1.0 / 24.0 + v * (1.0 / 120.0)))))
    return jnp.where(v > -0.1, series, 1.0 - jnp.exp(v))


def dot_nn(a, b):
    return lax.dot_general(a, b, (((1,), (0,)), ((), ())), preferred_element_type=jnp.float32)


def dot_nt(a, b):
    return lax.dot_general(a, b, (((1,), (1,)), ((), ())), preferred_element_type=jnp.float32)


def dot_tn(a, b):
    return lax.dot_general(a, b, (((0,), (0,)), ((), ())), preferred_element_type=jnp.float32)


def scan_rows(a, b, later):
    rows = a.shape[0]
    row = lax.broadcasted_iota(jnp.int32, a.shape, 0)
    step = 1
    while step < rows:
        turn = rows - step if later else step
        there = (row < rows - step) if later else (row >= step)
        a_next = jnp.where(there, pltpu.roll(a, turn, 0), 1.0)
        b_next = jnp.where(there, pltpu.roll(b, turn, 0), 0.0)
        b = a * b_next + b
        a = a * a_next
        step *= 2
    return a, b


def in_time(value, core):
    rows = value.shape[0] // 2
    near, far = value[:rows], value[rows:]
    odd = core == 1
    return jnp.concatenate([jnp.where(odd, far, near), jnp.where(odd, near, far)], axis=0)


def by_core(value, ref, core):
    rows = value.shape[0] // 2
    first, second = value[:rows], value[rows:]
    odd = core == 1
    ref[0] = jnp.where(odd, second, first).astype(ref.dtype)
    ref[1] = jnp.where(odd, first, second).astype(ref.dtype)


def mix_forward_kernel(chips, *refs):
    place = refs[0][0]
    blocks = refs[1 : 1 + 2 * chips]
    age_ref, chan_ref, in_ref, keep_ref, got_ref = refs[1 + 2 * chips : 6 + 2 * chips]
    (
        merged_ref,
        normed_ref,
        branch_ref,
        gelu_pre_ref,
        conv_ref,
        decay_pre_ref,
        input_pre_ref,
        prior_ref,
        low_ref,
        weights_ref,
        held,
        extended,
        carry,
    ) = refs[-13:]
    step = pl.program_id(0)
    chip, core = place // 2, place % 2
    rows, width = branch_ref.shape
    planes, near_model, both = in_ref.shape
    model = planes * near_model
    parts = weights_ref.shape[1] // both
    piece = keep_ref.shape[1] // parts

    @pl.when(step == 0)
    def _():
        extended[pl.ds(0, 8), :] = jnp.zeros((8, width), jnp.float32)
        carry[...] = jnp.zeros_like(carry)
        for k in range(chips):
            held[0, k] = blocks[k][...]
            held[1, k] = blocks[chips + k][...]
            home = pl.multiple_of(piece * 2 * (chip ^ k) + piece * core, piece)
            away = pl.multiple_of(piece * 2 * (chip ^ k) + piece * (1 - core), piece)
            for j in range(parts):
                where = pl.ds(j * both, both)
                weights_ref[pl.ds(home, piece), where] = keep_ref[k, pl.ds(j * piece, piece), :]
                weights_ref[pl.ds(away, piece), where] = got_ref[k, pl.ds(j * piece, piece), :]

    @pl.when(step > 0)
    def _():
        extended[pl.ds(0, 8), :] = extended[pl.ds(rows, 8), :]

    turn = step ^ chip
    near, far = held[0, turn], held[1, turn]
    normed_ref[0] = near
    normed_ref[1] = far
    normed = jnp.concatenate([near, far], axis=0)
    pre = dot_nn(normed[:, :near_model], in_ref[0])
    for z in range(1, planes):
        pre = pre + dot_nn(normed[:, z * near_model : (z + 1) * near_model], in_ref[z])
    pre = in_time(pre, core)
    branch = pre[:, :width].astype(jnp.bfloat16)
    gelu_pre = pre[:, width:]
    branch_ref[...] = branch
    gelu_pre_ref[...] = gelu_pre
    extended[pl.ds(8, rows), :] = branch.astype(jnp.float32)
    age = age_ref[...]
    total = jnp.zeros((rows, width), jnp.float32) + chan_ref[4:5, :]
    for k in range(4):
        shifted = extended[pl.ds(8 - k, rows), :]
        total = total + chan_ref[k : k + 1, :] * shifted * jnp.where(age >= k, 1.0, 0.0)
    conv_low = total.astype(jnp.bfloat16)
    conv = conv_low.astype(jnp.float32)
    conv_ref[...] = conv_low
    decay_pre = dot_nn(conv_low, weights_ref[:, model : model + width]) + chan_ref[5:6, :]
    input_pre = dot_nn(conv_low, weights_ref[:, model + width :]) + chan_ref[6:7, :]
    decay_pre_ref[...] = decay_pre
    input_pre_ref[...] = input_pre
    log_a = -8.0 * sigmoid(decay_pre) * chan_ref[7:8, :]
    reset = age < 0.5
    room = jnp.maximum(one_less_exp(2.0 * log_a), mult_floor)
    factor = jnp.where(reset, 1.0, jnp.sqrt(room))
    decay = jnp.where(reset, 0.0, jnp.exp(log_a))
    driven = sigmoid(input_pre) * conv * factor
    grown, states = scan_rows(decay, driven, False)
    before = carry[0:1, :]
    states = states + grown * before
    carry[0:1, :] = states[rows - 1 :, :]
    row = lax.broadcasted_iota(jnp.int32, states.shape, 0)
    prior_ref[...] = jnp.where(row == 0, before, pltpu.roll(states, 1, 0))
    low = states.astype(jnp.bfloat16)
    low_ref[...] = low
    merged = low.astype(jnp.float32) * gelu_parts(gelu_pre)[0]
    by_core(merged, merged_ref, core)


def mix_forward(place, near, far, age, chan, pack, keep, got, ahead_of):
    chips = len(near)
    rows, model = near[0].shape
    planes, _, both = pack.shape
    width = both // 2
    length = 2 * chips * rows
    chunk = 2 * rows
    columns = keep.shape[1] * both // (width // (2 * chips))
    time_block = lambda i, s: (i, 0)
    token_block = lambda i, s: (0, i ^ (s[0] // 2), 0, 0)
    saved = lambda dtype: jax.ShapeDtypeStruct((length, width), dtype)
    spec = pl.BlockSpec((chunk, width), time_block)
    fixed = lambda shape: pl.BlockSpec(shape, lambda i, s: (0,) * len(shape))
    return pl.pallas_call(
        functools.partial(mix_forward_kernel, chips),
        grid_spec=pltpu.PrefetchScalarGridSpec(
            num_scalar_prefetch=1,
            grid=(chips,),
            in_specs=[fixed((rows, model))] * (2 * chips)
            + [
                pl.BlockSpec((chunk, 1), time_block),
                pl.BlockSpec((chan.shape[0], width), lambda i, s: (0, s[0])),
                fixed((planes, model // planes, both)),
                fixed(keep.shape),
                fixed(got.shape),
            ]
            + [pl.BlockSpec(memory_space=pl.ANY)] * len(ahead_of),
            out_specs=[
                pl.BlockSpec((2, None, rows, width), token_block),
                pl.BlockSpec((2, None, rows, model), token_block),
            ]
            + [spec] * 7
            + [fixed((width, columns))],
            scratch_shapes=[
                pltpu.VMEM((2, chips, rows, model), jnp.bfloat16),
                pltpu.VMEM((chunk + 8, width), jnp.float32),
                pltpu.VMEM((8, width), jnp.float32),
            ],
        ),
        out_shape=[
            jax.ShapeDtypeStruct((2, chips, rows, width), jnp.bfloat16),
            jax.ShapeDtypeStruct((2, chips, rows, model), jnp.bfloat16),
            saved(jnp.bfloat16),
            saved(jnp.float32),
            saved(jnp.bfloat16),
            saved(jnp.float32),
            saved(jnp.float32),
            saved(jnp.float32),
            saved(jnp.bfloat16),
            jax.ShapeDtypeStruct((width, columns), jnp.bfloat16),
        ],
        compiler_params=pltpu.CompilerParams(vmem_limit_bytes=48 * 1024 * 1024),
        name="mix_forward",
    )(place, *near, *far, age, chan, pack, keep, got, *ahead_of)


def mix_backward_kernel(chips, *refs):
    place = refs[0][0]
    blocks = refs[1 : 1 + 2 * chips]
    (
        age_ref,
        chan_ref,
        weights_ref,
        branch_ref,
        gelu_pre_ref,
        conv_ref,
        decay_pre_ref,
        input_pre_ref,
        prior_ref,
        low_ref,
        both_ref,
        small_ref,
        gate_grads_ref,
        out_grad_ref,
        held,
        ahead,
        carry,
    ) = refs[1 + 2 * chips :]
    step = pl.program_id(0)
    chip, core = place // 2, place % 2
    rows, width = branch_ref.shape
    model = held.shape[-1]

    @pl.when(step == 0)
    def _():
        carry[...] = jnp.zeros_like(carry)
        ahead[:, pl.ds(rows, 8), :] = jnp.zeros((3, 8, width), jnp.float32)
        small_ref[...] = jnp.zeros_like(small_ref)
        gate_grads_ref[...] = jnp.zeros_like(gate_grads_ref)
        out_grad_ref[...] = jnp.zeros_like(out_grad_ref)
        for k in range(chips):
            held[0, k] = blocks[k][...]
            held[1, k] = blocks[chips + k][...]

    @pl.when(step > 0)
    def _():
        ahead[:, pl.ds(rows, 8), :] = ahead[:, pl.ds(0, 8), :]

    turn = (chips - 1 - step) ^ chip
    mixer_grad = jnp.concatenate([held[0, turn], held[1, turn]], axis=0)
    merged_grad = in_time(dot_nt(mixer_grad, weights_ref[:, :model]), core)
    age = age_ref[...]
    gelu_out, slope = gelu_parts(gelu_pre_ref[...])
    state_grad = (merged_grad * gelu_out).astype(jnp.bfloat16).astype(jnp.float32)
    low = low_ref[...].astype(jnp.float32)
    gelu_pre_grad = merged_grad * low * slope
    merged = in_time(low * gelu_out, core).astype(jnp.bfloat16)
    out_grad_ref[...] += dot_tn(mixer_grad, merged)
    reset = age < 0.5
    sig_d = sigmoid(decay_pre_ref[...])
    sig_i = sigmoid(input_pre_ref[...])
    soft = chan_ref[7:8, :]
    log_a = -8.0 * sig_d * soft
    a = jnp.exp(log_a)
    open_room = one_less_exp(2.0 * log_a)
    room = jnp.maximum(open_room, mult_floor)
    root = jnp.sqrt(room)
    factor = jnp.where(reset, 1.0, root)
    decay = jnp.where(reset, 0.0, a)
    conv_low = conv_ref[...]
    conv = conv_low.astype(jnp.float32)
    row = lax.broadcasted_iota(jnp.int32, (rows, width), 0)
    next_decay = jnp.where(row == rows - 1, carry[0:1, :], pltpu.roll(decay, rows - 1, 0))
    grown, carried = scan_rows(next_decay, state_grad, True)
    carried = carried + grown * carry[1:2, :]
    carry[0:1, :] = decay[0:1, :]
    carry[1:2, :] = carried[0:1, :]
    decay_grad = carried * prior_ref[...]
    input_pre_grad = carried * conv * factor * sig_i * (1.0 - sig_i)
    gate_conv_grad = carried * sig_i * factor
    room_grad = jnp.where(open_room > mult_floor, carried * sig_i * conv * 0.5 / root, 0.0)
    log_a_grad = jnp.where(reset, 0.0, decay_grad * a - 2.0 * a * a * room_grad)
    sig_grad = log_a_grad * sig_d
    decay_pre_grad = -8.0 * soft * sig_grad * (1.0 - sig_d)
    decay_low = decay_pre_grad.astype(jnp.bfloat16)
    input_low = input_pre_grad.astype(jnp.bfloat16)
    conv_grad = (
        gate_conv_grad
        + dot_nt(decay_low, weights_ref[:, model : model + width])
        + dot_nt(input_low, weights_ref[:, model + width :])
    )
    gate_grads_ref[0] += dot_tn(decay_low, conv_low)
    gate_grads_ref[1] += dot_tn(input_low, conv_low)
    branch = branch_ref[...].astype(jnp.float32)
    branch_grad = chan_ref[0:1, :] * conv_grad
    small_ref[0:1, :] += jnp.sum(conv_grad * branch, axis=0, keepdims=True)
    for k in range(1, 4):
        ahead[k - 1, pl.ds(0, rows), :] = conv_grad * jnp.where(age >= k, 1.0, 0.0)
        shifted = ahead[k - 1, pl.ds(k, rows), :]
        branch_grad = branch_grad + chan_ref[k : k + 1, :] * shifted
        small_ref[k : k + 1, :] += jnp.sum(shifted * branch, axis=0, keepdims=True)
    small_ref[4:5, :] += jnp.sum(conv_grad, axis=0, keepdims=True)
    small_ref[5:6, :] += jnp.sum(decay_low.astype(jnp.float32), axis=0, keepdims=True)
    small_ref[6:7, :] += jnp.sum(input_low.astype(jnp.float32), axis=0, keepdims=True)
    small_ref[7:8, :] += 8.0 * chan_ref[8:9, :] * jnp.sum(sig_grad, axis=0, keepdims=True)
    by_core(jnp.concatenate([branch_grad, gelu_pre_grad], axis=1), both_ref, core)


def mix_backward(place, near, far, age, chan, weights, saved):
    chips = len(near)
    rows, model = near[0].shape
    width, columns = weights.shape
    chunk = 2 * rows
    last = chips - 1
    time_block = lambda i, s: (last - i, 0)
    token_block = lambda i, s: (0, (last - i) ^ (s[0] // 2), 0, 0)
    spec = pl.BlockSpec((chunk, width), time_block)
    fixed = lambda shape: pl.BlockSpec(shape, lambda i, s: (0,) * len(shape))
    return pl.pallas_call(
        functools.partial(mix_backward_kernel, chips),
        grid_spec=pltpu.PrefetchScalarGridSpec(
            num_scalar_prefetch=1,
            grid=(chips,),
            in_specs=[fixed((rows, model))] * (2 * chips)
            + [
                pl.BlockSpec((chunk, 1), time_block),
                pl.BlockSpec((chan.shape[0], width), lambda i, s: (0, s[0])),
                fixed((width, columns)),
            ]
            + [spec] * 7,
            out_specs=[
                pl.BlockSpec((2, None, rows, 2 * width), token_block),
                fixed((8, width)),
                fixed((2, width, width)),
                fixed((model, width)),
            ],
            scratch_shapes=[
                pltpu.VMEM((2, chips, rows, model), jnp.bfloat16),
                pltpu.VMEM((3, chunk + 8, width), jnp.float32),
                pltpu.VMEM((8, width), jnp.float32),
            ],
        ),
        out_shape=[
            jax.ShapeDtypeStruct((2, chips, rows, 2 * width), jnp.bfloat16),
            jax.ShapeDtypeStruct((8, width), jnp.float32),
            jax.ShapeDtypeStruct((2, width, width), jnp.float32),
            jax.ShapeDtypeStruct((model, width), jnp.float32),
        ],
        compiler_params=pltpu.CompilerParams(vmem_limit_bytes=48 * 1024 * 1024),
        name="mix_backward",
    )(place, *near, *far, age, chan, weights, *saved)


def unit_kernel(chips, *refs):
    blocks, cots = refs[: 2 * chips], refs[2 * chips : 4 * chips]
    pack_ref, pair_ref, hidden_ref, grads_ref, down_ref, normed, cot, gate_up, down = refs[4 * chips :]
    rows = blocks[0].shape[0]
    planes, tall, near_model = pack_ref.shape
    both = pair_ref.shape[1]
    part = both // 2
    span = part // planes
    side = near_model // 2
    for k in range(2 * chips):
        normed[pl.ds(k * rows, rows), :] = blocks[k][...]
        cot[pl.ds(k * rows, rows), :] = cots[k][...]
    for z in range(planes):
        for j in range(3):
            gate_up[pl.ds(z * near_model, near_model), pl.ds(j * near_model, near_model)] = pack_ref[
                z, pl.ds(j * near_model, near_model), :
            ]
        for j in range(planes):
            down[pl.ds(z * span, span), pl.ds(j * near_model, near_model)] = pack_ref[
                z, pl.ds(3 * near_model + j * span, span), :
            ]
    down[pl.ds(part, side), :] = down[pl.ds(part - side, side), :]
    down_ref[...] = down[pl.ds(0, part), :]
    chunk = 2 * rows

    def tokens_step(i, nothing):
        here = pl.ds(pl.multiple_of(i * chunk, chunk), chunk)
        pre = dot_nn(normed[here, :], gate_up[...])
        hidden_grad = dot_nt(cot[here, :], down[...])
        gate, mid, up = pre[:, :near_model], pre[:, near_model:-near_model], pre[:, -near_model:]
        value, slope = gelu_parts(gate)
        above = hidden_grad[:, :near_model]
        hidden_ref[here, pl.ds(0, near_model)] = (value * up).astype(jnp.bfloat16)
        pair_ref[here, pl.ds(0, near_model)] = (above * up * slope).astype(jnp.bfloat16)
        pair_ref[here, pl.ds(2 * near_model, near_model)] = (above * value).astype(jnp.bfloat16)
        first = lax.broadcasted_iota(jnp.int32, mid.shape, 1) < side
        turned = pltpu.roll(mid, side, 1)
        gate, up = jnp.where(first, mid, turned), jnp.where(first, turned, mid)
        value, slope = gelu_parts(gate)
        above = hidden_grad[:, near_model:]
        hidden_ref[here, pl.ds(near_model, side)] = (value * up)[:, :side].astype(jnp.bfloat16)
        pair_ref[here, pl.ds(near_model, near_model)] = jnp.where(
            first, above * up * slope, above * value
        ).astype(jnp.bfloat16)
        return nothing

    lax.fori_loop(0, chips, tokens_step, 0)
    for z in range(planes):
        here = pl.ds(z * near_model, near_model)
        grad = dot_tn(normed[:, here], pair_ref[...]).astype(jnp.bfloat16)
        for j in range(3):
            grads_ref[z, pl.ds(j * near_model, near_model), :] = grad[
                :, j * near_model : (j + 1) * near_model
            ]
        grad = dot_tn(hidden_ref[...], cot[:, here]).astype(jnp.bfloat16)
        for j in range(planes):
            grads_ref[j, pl.ds(3 * near_model + z * span, span), :] = grad[
                j * span : (j + 1) * span
            ]


def unit_back_and_forth(near, far, cot_near, cot_far, pack, part):
    chips = len(near)
    rows, model = near[0].shape
    length = 2 * chips * rows
    _, _, near_model = pack.shape
    bf16 = jnp.bfloat16
    whole = pl.BlockSpec(memory_space=pltpu.VMEM)
    return pl.pallas_call(
        functools.partial(unit_kernel, chips),
        in_specs=[whole] * (4 * chips + 1),
        out_specs=[whole] * 4,
        scratch_shapes=[
            pltpu.VMEM((length, model), bf16),
            pltpu.VMEM((length, model), bf16),
            pltpu.VMEM((model, 2 * part), bf16),
            pltpu.VMEM((part + near_model // 2, model), bf16),
        ],
        out_shape=[
            jax.ShapeDtypeStruct((length, 2 * part), bf16),
            jax.ShapeDtypeStruct((length, part), bf16),
            jax.ShapeDtypeStruct(pack.shape, bf16),
            jax.ShapeDtypeStruct((part, model), bf16),
        ],
        compiler_params=pltpu.CompilerParams(vmem_limit_bytes=58 * 1024 * 1024),
        name="unit_back_and_forth",
    )(*near, *far, *cot_near, *cot_far, pack)


def pair_back_kernel(pair_ref, pack_ref, out_ref):
    near_model = pack_ref.shape[1]
    total = dot_nt(pair_ref[:, :near_model], pack_ref[:near_model, :])
    for j in (1, 2):
        here = slice(j * near_model, (j + 1) * near_model)
        total = total + dot_nt(pair_ref[:, here], pack_ref[here, :])
    out_ref[...] = total.astype(out_ref.dtype)


def pair_back(pair, pack, half):
    length, both = pair.shape
    planes, _, near_model = pack.shape
    rows = length // 2
    return pl.pallas_call(
        pair_back_kernel,
        grid=(planes,),
        in_specs=[
            pl.BlockSpec((rows, both), lambda z: (half, 0)),
            pl.BlockSpec((None, 3 * near_model, near_model), lambda z: (z, 0, 0)),
        ],
        out_specs=pl.BlockSpec((rows, near_model), lambda z: (0, z)),
        out_shape=jax.ShapeDtypeStruct((rows, planes * near_model), jnp.bfloat16),
        compiler_params=pltpu.CompilerParams(vmem_limit_bytes=32 * 1024 * 1024),
        name="pair_back",
    )(pair, pack)


def norm_back(values, scale, gain, grad):
    inner = jnp.mean(gain * grad * values, axis=-1, keepdims=True)
    return scale * gain * grad - values * (scale * scale * scale) * inner


def narrow_shards(
    tokens,
    cotangent,
    doc_starts,
    mix_gain,
    input_proj,
    gelu_proj,
    conv_taps,
    conv_bias,
    decay_gate,
    decay_bias,
    input_gate,
    input_bias,
    decay_param,
    output_proj,
    mlp_gain,
    mlp_gate,
    mlp_up,
    mlp_down,
):
    f32, bf16 = jnp.float32, jnp.bfloat16
    devices, planes = lax.axis_size("seq"), lax.axis_size("fsdp")
    chips = devices // 2
    place = lax.axis_index("seq")
    chip, core = place // 2, place % 2
    rows, model = tokens.shape[1:]
    length = rows * devices
    channels = conv_taps.shape[1]
    width = decay_gate.shape[1]
    deep = mlp_gate.shape[1]
    heads = output_proj.shape[0] // width
    piece = width // devices
    span = deep // (planes * devices)
    part = deep // devices
    near_model = model // planes

    def along_fsdp(x):
        return lax.all_gather(x, "fsdp", axis=0, tiled=True)

    def columns(x, start, size):
        return lax.dynamic_slice_in_dim(x, start, size, axis=1)

    def own_rows(x):
        mine = lax.dynamic_slice_in_dim(
            x.reshape(heads, width, x.shape[1]), place * piece, piece, 1
        )
        return jnp.swapaxes(mine.reshape(heads, piece, -1, 2 * width), 1, 2)

    rowset = jnp.concatenate(
        [own_rows(output_proj), own_rows(jnp.concatenate([decay_gate, input_gate], axis=1))], axis=1
    ).reshape(-1, 2 * width)
    in_own = jnp.concatenate(
        [columns(input_proj, place * width, width), columns(gelu_proj, place * width, width)],
        axis=1,
    )
    mix_pack = lax.all_gather(jnp.concatenate([in_own, rowset], axis=0), "fsdp", axis=0)

    def own_spans(x):
        return jnp.concatenate(
            [columns(x, z * (deep // planes) + place * span, span) for z in range(planes)], axis=1
        )

    gate_own, up_own = own_spans(mlp_gate), own_spans(mlp_up)
    down_own = lax.dynamic_slice_in_dim(mlp_down, place * span, span, 0)
    unit_pack = lax.all_gather(
        jnp.concatenate(
            [
                gate_own[:, :near_model],
                jnp.concatenate([gate_own[:, near_model:], up_own[:, near_model:]], axis=1),
                up_own[:, :near_model],
                jnp.swapaxes(down_own.reshape(span, planes, near_model), 0, 1).reshape(
                    planes * span, near_model
                ),
            ],
            axis=0,
        ),
        "fsdp",
        axis=0,
    )

    values = tokens[0].astype(f32)
    scale1 = lax.rsqrt(jnp.mean(values * values, axis=-1, keepdims=True) + norm_eps)
    normed_near, normed_far = gather_blocks((values * scale1 * mix_gain).astype(bf16))
    out_grad = cotangent[0]
    cot_near, cot_far = gather_blocks(out_grad)

    positions = jnp.arange(length, dtype=jnp.int32)
    starts = doc_starts[0]
    begin = jnp.max(jnp.where(starts[None, :] <= positions[:, None], starts[None, :], 0), axis=1)
    age = (positions - begin).astype(f32)[:, None]
    chan = jnp.concatenate(
        [
            conv_taps,
            conv_bias[None],
            decay_bias[None],
            input_bias[None],
            jax.nn.softplus(-decay_param)[None],
            jax.nn.sigmoid(-decay_param)[None],
            jnp.zeros((7, channels), f32),
        ],
        axis=0,
    )
    place_arg = place.astype(jnp.int32)[None]

    keep, got = exchange(mix_pack[:, near_model:].reshape(chips, 2, -1, 2 * width), chip, core)
    merged, normed, *saved, weights = mix_forward(
        place_arg, normed_near, normed_far, age, chan, mix_pack, keep, got, cot_near + cot_far
    )
    out_weights = weights[:, :model]
    in_weights = mix_pack[:, :near_model].reshape(model, 2 * width)
    far = dot_nn(merged[1].reshape(-1, width), out_weights).astype(bf16)
    near = dot_nn(merged[0].reshape(-1, width), out_weights)
    middle = values + scatter_blocks(
        near.reshape(chips, rows, model), far.reshape(chips, rows, model)
    )

    scale2 = lax.rsqrt(jnp.mean(middle * middle, axis=-1, keepdims=True) + norm_eps)
    near, far = gather_blocks((middle * scale2 * mlp_gain).astype(bf16))
    pair, hidden, unit_grads, down = unit_back_and_forth(
        near, far, cot_near, cot_far, unit_pack, part
    )
    unit_sum = lax.psum_scatter(unit_grads, "fsdp", scatter_dimension=0, tiled=False)
    far = pair_back(pair, unit_pack, 1)
    near = pair_back(pair, unit_pack, 0)
    normed2_grad = scatter_blocks(
        near.reshape(chips, rows, model), far.reshape(chips, rows, model)
    )
    split = length // 2

    mlp_gain_term = jnp.sum(normed2_grad * middle * scale2, axis=0)
    middle_grad = out_grad.astype(f32) + norm_back(middle, scale2, mlp_gain, normed2_grad)
    near, far = gather_blocks(middle_grad.astype(bf16))

    both, small, gate_grads, out_w_grad = mix_backward(
        place_arg, near, far, age, chan, weights, saved
    )
    normed = normed.reshape(length, model)
    both = both.reshape(length, 2 * width)
    far = dot_nt(both[split:], in_weights).astype(bf16)
    near = dot_nt(both[:split], in_weights)
    normed_grad = scatter_blocks(
        near.reshape(chips, rows, model), far.reshape(chips, rows, model)
    )
    in_grad = dot_tn(normed, both)
    turned = jnp.concatenate(
        [
            out_w_grad.astype(bf16).reshape(devices, model // devices, width),
            gate_grads[0].astype(bf16).reshape(devices, piece, width),
            gate_grads[1].astype(bf16).reshape(devices, piece, width),
        ],
        axis=1,
    )
    tall = turned.shape[1]
    keep, got = exchange(turned.reshape(chips, 2, tall, width), chip, core)
    home = reorder([keep[k] for k in range(chips)], chip)
    away = reorder([got[k] for k in range(chips)], chip)
    by_head = [
        jnp.concatenate(
            [jnp.where(core == 0, home[k], away[k]), jnp.where(core == 0, away[k], home[k])], axis=1
        )
        for k in range(chips)
    ]
    share = chips // planes
    row_pack = jnp.stack(
        [jnp.concatenate(by_head[z * share : (z + 1) * share], axis=1) for z in range(planes)]
    )
    grad_pack = jnp.concatenate(
        [in_grad.astype(bf16).reshape(planes, near_model, 2 * width), row_pack], axis=1
    )
    grad_pack, unit_sum = lax.optimization_barrier((grad_pack, unit_sum))
    mix_sum = lax.psum_scatter(grad_pack, "fsdp", scatter_dimension=0, tiled=False).astype(f32)
    input_proj_grad = mix_sum[:near_model, :width]
    gelu_proj_grad = mix_sum[:near_model, width:]
    turned_sum = mix_sum[near_model:].T
    slim = model // devices
    output_proj_grad = turned_sum[:, :slim]
    decay_gate_grad = turned_sum[:, slim : slim + piece]
    input_gate_grad = turned_sum[:, slim + piece :]

    first, mid, last, bottom = (
        unit_sum[:near_model],
        unit_sum[near_model : 2 * near_model],
        unit_sum[2 * near_model : 3 * near_model],
        unit_sum[3 * near_model :],
    )
    side = near_model // 2
    gate_sum = jnp.concatenate([first, mid[:, :side]], axis=1)
    up_sum = jnp.concatenate([last, mid[:, side:]], axis=1)
    mlp_gate_grad, mlp_up_grad, mlp_down_grad = final_exchange(
        jnp.stack([gate_sum.T, up_sum.T]).reshape(2, planes, span, near_model).swapaxes(0, 1),
        bottom.reshape(planes, span, near_model),
        chip,
        core,
        chips,
    )

    held = lax.optimization_barrier((hidden, down, both))
    hidden, down = held[:2]
    far = dot_nn(hidden[split:], down).astype(bf16)
    near = dot_nn(hidden[:split], down)
    mixed = (
        middle
        + scatter_blocks(near.reshape(chips, rows, model), far.reshape(chips, rows, model))
    ).astype(bf16)

    values_part = norm_back(values, scale1, mix_gain, normed_grad)
    tokens_grad = (middle_grad + values_part).astype(bf16)
    mix_gain_term = jnp.sum(in_grad * in_weights.astype(f32), axis=1) / mix_gain
    where_mine = (jnp.arange(devices) == place)[None, :, None]
    spread = jnp.where(where_mine, small[:, None, :], 0.0).reshape(8, channels)
    gains = jnp.pad(jnp.stack([mix_gain_term, mlp_gain_term]), ((0, 0), (0, channels - model)))
    sums = total_over(jnp.concatenate([spread, gains], axis=0), ("fsdp", "seq"))
    return (
        mixed[None],
        tokens_grad[None],
        sums[8, :model],
        input_proj_grad,
        gelu_proj_grad,
        sums[:4],
        sums[4],
        decay_gate_grad,
        sums[5],
        input_gate_grad,
        sums[6],
        sums[7],
        output_proj_grad,
        sums[9, :model],
        mlp_gate_grad,
        mlp_up_grad,
        mlp_down_grad,
    )


def final_exchange(gate_up_sum, down_sum, chip, core, chips):
    f32 = jnp.float32
    span, cols = down_sum.shape[1:]
    half = cols // 2
    sent = jnp.concatenate([gate_up_sum, down_sum[:, None]], axis=1)
    parts = [lax.dynamic_index_in_dim(sent, chip ^ k, 0, keepdims=False) for k in range(chips)]
    got = [parts[0]] + [chip_swap(parts[k], k) for k in range(1, chips)]
    turn = core ^ (chip // 2)
    low, high = jnp.stack(got[:2]), jnp.stack(got[2:])
    keep_gu = jnp.where(turn == 0, low[:, :2], high[:, :2])
    give_gu = jnp.where(turn == 0, high[:, :2], low[:, :2])
    downs = jnp.stack([g[2] for g in got])
    keep_d = jnp.where(core == 0, downs[:, :, :half], downs[:, :, half:])
    give_d = jnp.where(core == 0, downs[:, :, half:], downs[:, :, :half])
    got_gu, got_d = core_swap(give_gu), core_swap(give_d)
    home = reorder([keep_gu[0], keep_gu[1]], chip & 1)
    away = reorder([got_gu[0], got_gu[1]], chip & 1)
    blocks = []
    for x in range(2):
        blocks.append(jnp.where(core == 0, home[x], away[x]))
        blocks.append(jnp.where(core == 0, away[x], home[x]))
    gate_up = jnp.concatenate(blocks, axis=1).astype(f32)
    home = reorder([keep_d[k] for k in range(chips)], chip)
    away = reorder([got_d[k] for k in range(chips)], chip)
    blocks = []
    for k in range(chips):
        blocks.append(jnp.where(core == 0, home[k], away[k]))
        blocks.append(jnp.where(core == 0, away[k], home[k]))
    return gate_up[0].T, gate_up[1].T, jnp.concatenate(blocks, axis=0).astype(f32)


def choose_plan(mesh):
    devices, planes = mesh.shape["seq"], mesh.shape["fsdp"]

    def plan(*args):
        channels, width = args[6].shape[1], args[8].shape[1]
        if channels == width * devices and devices == 2 * planes and planes == 4:
            return narrow_shards(*args)
        return wide_shards(*args)

    return plan


def solution(mesh):
    return jax.shard_map(
        choose_plan(mesh),
        mesh=mesh,
        in_specs=(
            P("fsdp", "seq", None),
            P("fsdp", "seq", None),
            P("fsdp", None),
            P(),
            P("fsdp", None),
            P("fsdp", None),
            P(),
            P(),
            P("fsdp", None),
            P(),
            P("fsdp", None),
            P(),
            P(),
            P("fsdp", None),
            P(),
            P("fsdp", None),
            P("fsdp", None),
            P("fsdp", None),
        ),
        out_specs=(
            P("fsdp", "seq", None),
            P("fsdp", "seq", None),
            P(),
            P("fsdp", "seq"),
            P("fsdp", "seq"),
            P(),
            P(),
            P("fsdp", "seq"),
            P(),
            P("fsdp", "seq"),
            P(),
            P(),
            P("fsdp", "seq"),
            P(),
            P("fsdp", "seq"),
            P("fsdp", "seq"),
            P("fsdp", "seq"),
        ),
        check_vma=False,
    )
```

```python
import functools

import jax
import jax.numpy as jnp
from jax import lax
from jax.experimental import pallas as pl
from jax.experimental.pallas import tpu as pltpu
from jax.sharding import PartitionSpec as P

norm_eps = 1e-06
mult_floor = 0.0001


def from_behind(x, axis, by):
    devices = lax.axis_size(axis)
    pairs = [(i, i + by) for i in range(devices) if 0 <= i + by < devices]
    return lax.ppermute(x, axis, pairs)


def rms_scale(values, gain):
    scale = lax.rsqrt(jnp.mean(values * values, axis=-1, keepdims=True) + norm_eps)
    return values * scale * gain


def smooth_gelu(values):
    return jax.nn.gelu(values, approximate=True)


def gated_unit(gate, up_val):
    return smooth_gelu(gate) * up_val


def affine_pair(earlier, later):
    return (earlier[0] * later[0], earlier[1] * later[0] + later[1])


def decay_terms(conv_out, decay_pre, input_pre, decay_param, resets):
    log_a = -8.0 * jax.nn.sigmoid(decay_pre) * jax.nn.softplus(-decay_param)
    room = jnp.maximum(-jnp.expm1(2.0 * log_a), mult_floor)
    factor = jnp.where(resets, 1.0, jnp.sqrt(room))
    decay = jnp.where(resets, 0.0, jnp.exp(log_a))
    return (decay, jax.nn.sigmoid(input_pre) * conv_out * factor)


def conv_apply(extended, taps_w, bias, masks):
    taps = taps_w.shape[0]
    rows = masks.shape[1]
    total = jnp.zeros((rows, taps_w.shape[1]), jnp.float32) + bias
    for shift_k in range(taps):
        begin_row = taps - 1 - shift_k
        total = total + taps_w[shift_k] * extended[begin_row : begin_row + rows] * masks[shift_k]
    return total


def block_product(left, weight):
    width = weight.shape[1]
    blocks = weight.shape[0] // width
    result = jnp.einsum(
        "nhk,hkj->nhj",
        left.reshape(left.shape[0], blocks, width),
        weight.reshape(blocks, width, width),
        preferred_element_type=jnp.float32,
    )
    return result.reshape(left.shape[0], -1)


def block_back(grad, weight):
    width = weight.shape[1]
    blocks = weight.shape[0] // width
    result = jnp.einsum(
        "nhj,hkj->nhk",
        grad.reshape(grad.shape[0], blocks, width),
        weight.reshape(blocks, width, width),
        preferred_element_type=jnp.float32,
    )
    return result.reshape(grad.shape[0], -1)


def block_weight_grad(left, grad, width):
    blocks = left.shape[1] // width
    result = jnp.einsum(
        "nhk,nhj->hkj",
        left.reshape(left.shape[0], blocks, width),
        grad.reshape(grad.shape[0], blocks, width),
        preferred_element_type=jnp.float32,
    )
    return result.reshape(blocks * width, width)


def wide_shards(
    tokens,
    cotangent,
    doc_starts,
    mix_gain,
    input_proj,
    gelu_proj,
    conv_taps,
    conv_bias,
    decay_gate,
    decay_bias,
    input_gate,
    input_bias,
    decay_param,
    output_proj,
    mlp_gain,
    mlp_gate,
    mlp_up,
    mlp_down,
):
    rows = tokens.shape[1]
    taps = conv_taps.shape[0]
    width = decay_gate.shape[1]
    input_w, gelu_w, output_w, decay_w, inputg_w, gate_w, up_w, down_w = (
        lax.all_gather(input_proj, "fsdp", axis=0, tiled=True),
        lax.all_gather(gelu_proj, "fsdp", axis=0, tiled=True),
        lax.all_gather(output_proj, "fsdp", axis=0, tiled=True),
        lax.all_gather(decay_gate, "fsdp", axis=0, tiled=True),
        lax.all_gather(input_gate, "fsdp", axis=0, tiled=True),
        lax.all_gather(mlp_gate, "fsdp", axis=0, tiled=True),
        lax.all_gather(mlp_up, "fsdp", axis=0, tiled=True),
        lax.all_gather(mlp_down, "fsdp", axis=0, tiled=True),
    )
    channels = input_w.shape[1]
    first = lax.axis_index("seq") * rows
    positions = first + jnp.arange(rows, dtype=jnp.int32)
    starts = doc_starts[0]
    begin = jnp.max(jnp.where(starts[None, :] <= positions[:, None], starts[None, :], 0), axis=1)
    resets = (begin == positions)[:, None]
    masks = jnp.stack([(positions - k >= begin)[:, None] for k in range(taps)]).astype(jnp.float32)
    values = tokens[0].astype(jnp.float32)
    normed = rms_scale(values, mix_gain).astype(jnp.bfloat16)
    branch = jnp.dot(normed, input_w, preferred_element_type=jnp.float32).astype(jnp.bfloat16)
    gelu_pre = jnp.dot(normed, gelu_w, preferred_element_type=jnp.float32)
    gelu_out = smooth_gelu(gelu_pre)
    previous = from_behind(branch[rows - (taps - 1) :], "seq", 1)
    extended = jnp.concatenate([previous, branch], axis=0).astype(jnp.float32)
    conv_f = conv_apply(extended, conv_taps, conv_bias, masks).astype(jnp.bfloat16)
    conv_val = conv_f.astype(jnp.float32)
    decay_pre = block_product(conv_f, decay_w) + decay_bias
    input_pre = block_product(conv_f, inputg_w) + input_bias
    decay, driven = decay_terms(conv_val, decay_pre, input_pre, decay_param, resets)
    decay_cols, driven_cols = (
        lax.all_to_all(decay, "seq", split_axis=1, concat_axis=0, tiled=True),
        lax.all_to_all(driven, "seq", split_axis=1, concat_axis=0, tiled=True),
    )
    states_cols = lax.associative_scan(affine_pair, (decay_cols, driven_cols), axis=0)[1]
    states_low = lax.all_to_all(
        states_cols.astype(jnp.bfloat16), "seq", split_axis=0, concat_axis=1, tiled=True
    )
    states_val = states_low.astype(jnp.float32)
    merged = (states_val * gelu_out).astype(jnp.bfloat16)
    middle = values + jnp.dot(merged, output_w, preferred_element_type=jnp.float32)
    normed2 = rms_scale(middle, mlp_gain).astype(jnp.bfloat16)
    gate = jnp.dot(normed2, gate_w, preferred_element_type=jnp.float32)
    up_val = jnp.dot(normed2, up_w, preferred_element_type=jnp.float32)
    hidden = gated_unit(gate, up_val).astype(jnp.bfloat16)
    mixed = (middle + jnp.dot(hidden, down_w, preferred_element_type=jnp.float32)).astype(
        jnp.bfloat16
    )
    out_grad = cotangent[0]
    down_grad = jnp.einsum("tf,td->fd", hidden, out_grad, preferred_element_type=jnp.float32)
    hidden_grad = jnp.einsum("td,fd->tf", out_grad, down_w, preferred_element_type=jnp.float32)
    unit_pull = jax.vjp(gated_unit, gate, up_val)[1]
    gate_grad, up_grad = unit_pull(hidden_grad)
    gate_low = gate_grad.astype(jnp.bfloat16)
    up_low = up_grad.astype(jnp.bfloat16)
    gate_w_grad = jnp.einsum("td,tf->df", normed2, gate_low, preferred_element_type=jnp.float32)
    up_w_grad = jnp.einsum("td,tf->df", normed2, up_low, preferred_element_type=jnp.float32)
    mlp_terms = (
        lax.psum_scatter(gate_w_grad, "seq", scatter_dimension=1, tiled=True),
        lax.psum_scatter(up_w_grad, "seq", scatter_dimension=1, tiled=True),
        lax.psum_scatter(down_grad, "seq", scatter_dimension=1, tiled=True),
    )
    mlp_gate_grad, mlp_up_grad, mlp_down_grad = (
        lax.psum_scatter(mlp_terms[0], "fsdp", scatter_dimension=0, tiled=True),
        lax.psum_scatter(mlp_terms[1], "fsdp", scatter_dimension=0, tiled=True),
        lax.psum_scatter(mlp_terms[2], "fsdp", scatter_dimension=0, tiled=True),
    )
    normed2_grad = jnp.einsum(
        "tf,df->td", gate_low, gate_w, preferred_element_type=jnp.float32
    ) + jnp.einsum("tf,df->td", up_low, up_w, preferred_element_type=jnp.float32)
    norm2_pull = jax.vjp(rms_scale, middle, mlp_gain)[1]
    middle_part, mlp_gain_term = norm2_pull(normed2_grad)
    middle_grad = out_grad.astype(jnp.float32) + middle_part
    mixer_grad = middle_grad.astype(jnp.bfloat16)
    output_w_grad = jnp.einsum("tr,td->rd", merged, mixer_grad, preferred_element_type=jnp.float32)
    merged_grad = jnp.einsum("td,rd->tr", mixer_grad, output_w, preferred_element_type=jnp.float32)
    state_low = (merged_grad * gelu_out).astype(jnp.bfloat16)
    gelu_pull = jax.vjp(smooth_gelu, gelu_pre)[1]
    gelu_pre_low = gelu_pull(merged_grad * states_val)[0].astype(jnp.bfloat16)
    grad_cols = lax.all_to_all(state_low, "seq", split_axis=1, concat_axis=0, tiled=True).astype(
        jnp.float32
    )
    width_cols = grad_cols.shape[1]
    next_decay = jnp.concatenate([decay_cols[1:], jnp.zeros((1, width_cols), jnp.float32)], axis=0)
    carried = lax.associative_scan(affine_pair, (next_decay, grad_cols), reverse=True, axis=0)[1]
    prior = jnp.concatenate([jnp.zeros((1, width_cols), jnp.float32), states_cols[:-1]], axis=0)
    decay_grad, driven_grad = (
        lax.all_to_all(carried * prior, "seq", split_axis=0, concat_axis=1, tiled=True),
        lax.all_to_all(carried, "seq", split_axis=0, concat_axis=1, tiled=True),
    )
    terms_pull = jax.vjp(
        lambda conv_in, dpre, ipre, dparam: decay_terms(conv_in, dpre, ipre, dparam, resets),
        conv_val,
        decay_pre,
        input_pre,
        decay_param,
    )[1]
    gate_conv_grad, dpre_grad, ipre_grad, decay_param_term = terms_pull((decay_grad, driven_grad))
    dpre_low = dpre_grad.astype(jnp.bfloat16)
    ipre_low = ipre_grad.astype(jnp.bfloat16)
    decay_w_grad = block_weight_grad(conv_f, dpre_low, width)
    inputg_w_grad = block_weight_grad(conv_f, ipre_low, width)
    conv_grad = gate_conv_grad + block_back(dpre_low, decay_w) + block_back(ipre_low, inputg_w)
    conv_pull = jax.vjp(
        lambda ext, taps_w, bias: conv_apply(ext, taps_w, bias, masks),
        extended,
        conv_taps,
        conv_bias,
    )[1]
    extended_grad, taps_term, conv_bias_term = conv_pull(conv_grad)
    returned = from_behind(extended_grad[: taps - 1], "seq", -1)
    branch_grad = extended_grad[taps - 1 :] + jnp.concatenate(
        [jnp.zeros((rows - (taps - 1), channels), jnp.float32), returned], axis=0
    )
    branch_low = branch_grad.astype(jnp.bfloat16)
    input_w_grad = jnp.einsum("td,tr->dr", normed, branch_low, preferred_element_type=jnp.float32)
    gelu_w_grad = jnp.einsum("td,tr->dr", normed, gelu_pre_low, preferred_element_type=jnp.float32)
    mix_terms = (
        lax.psum_scatter(input_w_grad, "seq", scatter_dimension=1, tiled=True),
        lax.psum_scatter(gelu_w_grad, "seq", scatter_dimension=1, tiled=True),
        lax.psum_scatter(output_w_grad, "seq", scatter_dimension=1, tiled=True),
        lax.psum_scatter(decay_w_grad, "seq", scatter_dimension=1, tiled=True),
        lax.psum_scatter(inputg_w_grad, "seq", scatter_dimension=1, tiled=True),
    )
    input_proj_grad, gelu_proj_grad, output_proj_grad, decay_gate_grad, input_gate_grad = (
        lax.psum_scatter(mix_terms[0], "fsdp", scatter_dimension=0, tiled=True),
        lax.psum_scatter(mix_terms[1], "fsdp", scatter_dimension=0, tiled=True),
        lax.psum_scatter(mix_terms[2], "fsdp", scatter_dimension=0, tiled=True),
        lax.psum_scatter(mix_terms[3], "fsdp", scatter_dimension=0, tiled=True),
        lax.psum_scatter(mix_terms[4], "fsdp", scatter_dimension=0, tiled=True),
    )
    normed_grad = jnp.einsum(
        "tr,dr->td", branch_low, input_w, preferred_element_type=jnp.float32
    ) + jnp.einsum("tr,dr->td", gelu_pre_low, gelu_w, preferred_element_type=jnp.float32)
    norm1_pull = jax.vjp(rms_scale, values, mix_gain)[1]
    values_part, mix_gain_term = norm1_pull(normed_grad)
    tokens_grad = (middle_grad + values_part).astype(jnp.bfloat16)
    (
        mix_gain_grad,
        conv_taps_grad,
        conv_bias_grad,
        decay_bias_grad,
        input_bias_grad,
        decay_param_grad,
        mlp_gain_grad,
    ) = lax.psum(
        (
            mix_gain_term,
            taps_term,
            conv_bias_term,
            jnp.sum(dpre_low.astype(jnp.float32), axis=0),
            jnp.sum(ipre_low.astype(jnp.float32), axis=0),
            decay_param_term,
            mlp_gain_term,
        ),
        ("seq", "fsdp"),
    )
    return (
        mixed[None],
        tokens_grad[None],
        mix_gain_grad,
        input_proj_grad,
        gelu_proj_grad,
        conv_taps_grad,
        conv_bias_grad,
        decay_gate_grad,
        decay_bias_grad,
        input_gate_grad,
        input_bias_grad,
        decay_param_grad,
        output_proj_grad,
        mlp_gain_grad,
        mlp_gate_grad,
        mlp_up_grad,
        mlp_down_grad,
    )


def chip_swap(x, k):
    devices = lax.axis_size("seq")
    return lax.ppermute(x, "seq", [(i, i ^ (2 * k)) for i in range(devices)])


def core_swap(x):
    devices = lax.axis_size("seq")
    return lax.ppermute(x, "seq", [(i, i ^ 1) for i in range(devices)])


def gather_blocks(x):
    chips = lax.axis_size("seq") // 2
    near = jnp.stack([x] + [chip_swap(x, k) for k in range(1, chips)])
    return near, core_swap(near)


def tie(*arrays):
    return lax.optimization_barrier(arrays)


def pair_blocks(near, far):
    pair = near.astype(jnp.float32) + core_swap(far).astype(jnp.float32)
    return pair.astype(jnp.bfloat16), pair[0]


def spread_pairs(low, own):
    total = own
    for k in range(1, low.shape[0]):
        total = total + chip_swap(low[k], k).astype(jnp.float32)
    return total


def scatter_blocks(near, far):
    return spread_pairs(*pair_blocks(near, far))


def exchange(x, chip, core, turn):
    chips = x.shape[0]
    parts = [
        lax.dynamic_index_in_dim(x, chip ^ k ^ turn, 0, keepdims=False) for k in range(chips)
    ]
    got = jnp.stack([parts[0]] + [chip_swap(parts[k], k) for k in range(1, chips)])
    keep = lax.dynamic_index_in_dim(got, core, 1, keepdims=False)
    give = lax.dynamic_index_in_dim(got, 1 - core, 1, keepdims=False)
    return keep, core_swap(give)


def reorder(parts, index):
    bit = 1
    while bit < len(parts):
        flip = (index & bit) != 0
        parts = [jnp.where(flip, parts[i ^ bit], parts[i]) for i in range(len(parts))]
        bit *= 2
    return parts


def over_planes(x):
    planes = lax.axis_size("fsdp")
    total = x
    for k in range(1, planes):
        total = total + lax.ppermute(x, "fsdp", [(i, i ^ k) for i in range(planes)])
    return total


def total_over(x, axes):
    for axis in axes:
        devices = lax.axis_size(axis)
        bit = 1
        while bit < devices:
            x = x + lax.ppermute(x, axis, [(i, i ^ bit) for i in range(devices)])
            bit *= 2
    return x


def gelu_parts(v):
    root = 0.7978845608028654
    square = v * v
    h = 0.5 + 0.5 * jnp.tanh(v * (root + root * 0.044715 * square))
    value = v * h
    return value, h + value * (1.0 - h) * (2.0 * root + root * 0.26829 * square)


def sigmoid(v):
    return 1.0 / (1.0 + jnp.exp(-v))


def one_less_exp(v):
    series = -v * (1.0 + v * (0.5 + v * (1.0 / 6.0 + v * (1.0 / 24.0 + v * (1.0 / 120.0)))))
    return jnp.where(v > -0.1, series, 1.0 - jnp.exp(v))


def dot_nn(a, b):
    return lax.dot_general(a, b, (((1,), (0,)), ((), ())), preferred_element_type=jnp.float32)


def dot_nt(a, b):
    return lax.dot_general(a, b, (((1,), (1,)), ((), ())), preferred_element_type=jnp.float32)


def dot_tn(a, b):
    return lax.dot_general(a, b, (((0,), (0,)), ((), ())), preferred_element_type=jnp.float32)


def scan_rows(a, b, carry, later):
    rows = a.shape[0]
    group = 8
    row = lax.broadcasted_iota(jnp.int32, a.shape, 0) % group
    step = 1
    while step < group:
        turn = rows - step if later else step
        there = (row < group - step) if later else (row >= step)
        a_next = jnp.where(there, pltpu.roll(a, turn, 0), 1.0)
        b_next = jnp.where(there, pltpu.roll(b, turn, 0), 0.0)
        b = a * b_next + b
        a = a * a_next
        step *= 2
    starts = list(range(0, rows, group))
    done = {}
    for start in reversed(starts) if later else starts:
        states = a[start : start + group] * carry + b[start : start + group]
        done[start] = states
        carry = states[:1] if later else states[group - 1 :]
    return jnp.concatenate([done[start] for start in starts], axis=0)


def in_time(value, core):
    rows = value.shape[0] // 2
    near, far = value[:rows], value[rows:]
    odd = core == 1
    return jnp.concatenate([jnp.where(odd, far, near), jnp.where(odd, near, far)], axis=0)


def by_core(value, ref, core):
    rows = value.shape[0] // 2
    first, second = value[:rows], value[rows:]
    odd = core == 1
    ref[0] = jnp.where(odd, second, first).astype(ref.dtype)
    ref[1] = jnp.where(odd, first, second).astype(ref.dtype)


def mix_forward_kernel(
    seq_ref,
    near_ref,
    far_ref,
    age_ref,
    chan_ref,
    in_ref,
    keep_ref,
    got_ref,
    merged_ref,
    branch_ref,
    gelu_pre_ref,
    conv_ref,
    decay_pre_ref,
    input_pre_ref,
    prior_ref,
    low_ref,
    weights_ref,
    extended,
    carry,
):
    place = seq_ref[0]
    chips = near_ref.shape[0]
    step = pl.program_id(0)
    chip, core = place // 2, place % 2
    rows, width = branch_ref.shape
    planes, near_model, both = in_ref.shape
    model = planes * near_model
    parts = weights_ref.shape[1] // both
    piece = keep_ref.shape[1] // parts

    @pl.when(step == 0)
    def _():
        extended[pl.ds(0, 8), :] = jnp.zeros((8, width), jnp.float32)
        carry[...] = jnp.zeros_like(carry)
        for k in range(chips):
            home = pl.multiple_of(piece * 2 * (chip ^ k) + piece * core, piece)
            away = pl.multiple_of(piece * 2 * (chip ^ k) + piece * (1 - core), piece)
            for j in range(parts):
                where = pl.ds(j * both, both)
                weights_ref[pl.ds(home, piece), where] = keep_ref[k, pl.ds(j * piece, piece), :]
                weights_ref[pl.ds(away, piece), where] = got_ref[k, pl.ds(j * piece, piece), :]

    @pl.when(step > 0)
    def _():
        extended[pl.ds(0, 8), :] = extended[pl.ds(rows, 8), :]

    turn = step ^ chip
    normed = jnp.concatenate([near_ref[turn], far_ref[turn]], axis=0)
    pre = dot_nn(normed[:, :near_model], in_ref[0])
    for z in range(1, planes):
        pre = pre + dot_nn(normed[:, z * near_model : (z + 1) * near_model], in_ref[z])
    pre = in_time(pre, core)
    branch = pre[:, :width].astype(jnp.bfloat16)
    gelu_pre = pre[:, width:]
    branch_ref[...] = branch
    gelu_pre_ref[...] = gelu_pre
    extended[pl.ds(8, rows), :] = branch.astype(jnp.float32)
    age = age_ref[...]
    total = jnp.zeros((rows, width), jnp.float32) + chan_ref[4:5, :]
    for k in range(4):
        shifted = extended[pl.ds(8 - k, rows), :]
        total = total + chan_ref[k : k + 1, :] * shifted * jnp.where(age >= k, 1.0, 0.0)
    conv_low = total.astype(jnp.bfloat16)
    conv = conv_low.astype(jnp.float32)
    conv_ref[...] = conv_low
    decay_pre = dot_nn(conv_low, weights_ref[:, model : model + width]) + chan_ref[5:6, :]
    input_pre = dot_nn(conv_low, weights_ref[:, model + width :]) + chan_ref[6:7, :]
    decay_pre_ref[...] = decay_pre
    input_pre_ref[...] = input_pre
    log_a = -8.0 * sigmoid(decay_pre) * chan_ref[7:8, :]
    reset = age < 0.5
    room = jnp.maximum(one_less_exp(2.0 * log_a), mult_floor)
    factor = jnp.where(reset, 1.0, jnp.sqrt(room))
    decay = jnp.where(reset, 0.0, jnp.exp(log_a))
    driven = sigmoid(input_pre) * conv * factor
    before = carry[0:1, :]
    states = scan_rows(decay, driven, before, False)
    carry[0:1, :] = states[rows - 1 :, :]
    row = lax.broadcasted_iota(jnp.int32, states.shape, 0)
    prior_ref[...] = jnp.where(row == 0, before, pltpu.roll(states, 1, 0))
    low = states.astype(jnp.bfloat16)
    low_ref[...] = low
    merged = low.astype(jnp.float32) * gelu_parts(gelu_pre)[0]
    by_core(merged, merged_ref, core)


def mix_forward(place, near, far, age, chan, pack, keep, got):
    chips, rows, model = near.shape
    planes, _, both = pack.shape
    width = both // 2
    length = 2 * chips * rows
    chunk = 2 * rows
    columns = keep.shape[1] * both // (width // (2 * chips))
    time_block = lambda i, s: (i, 0)
    token_block = lambda i, s: (0, i ^ (s[0] // 2), 0, 0)
    saved = lambda dtype: jax.ShapeDtypeStruct((length, width), dtype)
    spec = pl.BlockSpec((chunk, width), time_block)
    fixed = lambda shape: pl.BlockSpec(shape, lambda i, s: (0,) * len(shape))
    return pl.pallas_call(
        mix_forward_kernel,
        grid_spec=pltpu.PrefetchScalarGridSpec(
            num_scalar_prefetch=1,
            grid=(chips,),
            in_specs=[
                fixed(near.shape),
                fixed(far.shape),
                pl.BlockSpec((chunk, 1), time_block),
                pl.BlockSpec((chan.shape[0], width), lambda i, s: (0, s[0])),
                fixed((planes, model // planes, both)),
                fixed(keep.shape),
                fixed(got.shape),
            ],
            out_specs=[pl.BlockSpec((2, None, rows, width), token_block)]
            + [spec] * 7
            + [fixed((width, columns))],
            scratch_shapes=[
                pltpu.VMEM((chunk + 8, width), jnp.float32),
                pltpu.VMEM((8, width), jnp.float32),
            ],
        ),
        out_shape=[
            jax.ShapeDtypeStruct((2, chips, rows, width), jnp.bfloat16),
            saved(jnp.bfloat16),
            saved(jnp.float32),
            saved(jnp.bfloat16),
            saved(jnp.float32),
            saved(jnp.float32),
            saved(jnp.float32),
            saved(jnp.bfloat16),
            jax.ShapeDtypeStruct((width, columns), jnp.bfloat16),
        ],
        compiler_params=pltpu.CompilerParams(vmem_limit_bytes=56 * 1024 * 1024),
        name="mix_forward",
    )(place, near, far, age, chan, pack, keep, got)


def mix_backward_kernel(
    seq_ref,
    near_ref,
    far_ref,
    age_ref,
    chan_ref,
    weights_ref,
    branch_ref,
    gelu_pre_ref,
    conv_ref,
    decay_pre_ref,
    input_pre_ref,
    prior_ref,
    low_ref,
    both_ref,
    small_ref,
    *rest,
):
    place = seq_ref[0]
    chips = near_ref.shape[0]
    row_refs, (out_grad, gate_grads, ahead, carry) = rest[:chips], rest[chips:]
    step = pl.program_id(0)
    chip, core = place // 2, place % 2
    rows, width = branch_ref.shape
    model = near_ref.shape[-1]

    @pl.when(step == 0)
    def _():
        carry[...] = jnp.zeros_like(carry)
        ahead[:, pl.ds(rows, 8), :] = jnp.zeros((3, 8, width), jnp.float32)
        small_ref[...] = jnp.zeros_like(small_ref)
        gate_grads[...] = jnp.zeros_like(gate_grads)
        out_grad[...] = jnp.zeros_like(out_grad)

    @pl.when(step > 0)
    def _():
        ahead[:, pl.ds(rows, 8), :] = ahead[:, pl.ds(0, 8), :]

    turn = (chips - 1 - step) ^ chip
    mixer_grad = jnp.concatenate([near_ref[turn], far_ref[turn]], axis=0)
    merged_grad = in_time(dot_nt(mixer_grad, weights_ref[:, :model]), core)
    age = age_ref[...]
    gelu_out, slope = gelu_parts(gelu_pre_ref[...])
    state_grad = (merged_grad * gelu_out).astype(jnp.bfloat16).astype(jnp.float32)
    low = low_ref[...].astype(jnp.float32)
    gelu_pre_grad = merged_grad * low * slope
    merged = in_time((low * gelu_out).astype(jnp.bfloat16), core)
    out_grad[...] += dot_tn(mixer_grad, merged)
    reset = age < 0.5
    sig_d = sigmoid(decay_pre_ref[...])
    sig_i = sigmoid(input_pre_ref[...])
    soft = chan_ref[7:8, :]
    log_a = -8.0 * sig_d * soft
    a = jnp.exp(log_a)
    open_room = one_less_exp(2.0 * log_a)
    room = jnp.maximum(open_room, mult_floor)
    root = jnp.sqrt(room)
    factor = jnp.where(reset, 1.0, root)
    decay = jnp.where(reset, 0.0, a)
    conv_low = conv_ref[...]
    conv = conv_low.astype(jnp.float32)
    row = lax.broadcasted_iota(jnp.int32, (rows, width), 0)
    next_decay = jnp.where(row == rows - 1, carry[0:1, :], pltpu.roll(decay, rows - 1, 0))
    carried = scan_rows(next_decay, state_grad, carry[1:2, :], True)
    carry[0:1, :] = decay[0:1, :]
    carry[1:2, :] = carried[0:1, :]
    decay_grad = carried * prior_ref[...]
    input_pre_grad = carried * conv * factor * sig_i * (1.0 - sig_i)
    gate_conv_grad = carried * sig_i * factor
    room_grad = jnp.where(open_room > mult_floor, carried * sig_i * conv * 0.5 / root, 0.0)
    log_a_grad = jnp.where(reset, 0.0, decay_grad * a - 2.0 * a * a * room_grad)
    sig_grad = log_a_grad * sig_d
    decay_pre_grad = -8.0 * soft * sig_grad * (1.0 - sig_d)
    decay_low = decay_pre_grad.astype(jnp.bfloat16)
    input_low = input_pre_grad.astype(jnp.bfloat16)
    conv_grad = (
        gate_conv_grad
        + dot_nt(decay_low, weights_ref[:, model : model + width])
        + dot_nt(input_low, weights_ref[:, model + width :])
    )
    gate_grads[0] += dot_tn(decay_low, conv_low)
    gate_grads[1] += dot_tn(input_low, conv_low)
    branch = branch_ref[...].astype(jnp.float32)
    branch_grad = chan_ref[0:1, :] * conv_grad
    small_ref[0:1, :] += jnp.sum(conv_grad * branch, axis=0, keepdims=True)
    for k in range(1, 4):
        ahead[k - 1, pl.ds(0, rows), :] = conv_grad * jnp.where(age >= k, 1.0, 0.0)
        shifted = ahead[k - 1, pl.ds(k, rows), :]
        branch_grad = branch_grad + chan_ref[k : k + 1, :] * shifted
        small_ref[k : k + 1, :] += jnp.sum(shifted * branch, axis=0, keepdims=True)
    small_ref[4:5, :] += jnp.sum(conv_grad, axis=0, keepdims=True)
    small_ref[5:6, :] += jnp.sum(decay_low.astype(jnp.float32), axis=0, keepdims=True)
    small_ref[6:7, :] += jnp.sum(input_low.astype(jnp.float32), axis=0, keepdims=True)
    small_ref[7:8, :] += 8.0 * chan_ref[8:9, :] * jnp.sum(sig_grad, axis=0, keepdims=True)
    by_core(jnp.concatenate([branch_grad, gelu_pre_grad], axis=1), both_ref, core)

    @pl.when(step == chips - 1)
    def _():
        slim, piece = model // (2 * chips), width // (2 * chips)
        for k in range(chips):
            for e in range(2):
                target = 2 * (chip ^ k) + (core ^ e)
                rows = pl.ds(pl.multiple_of(target * slim, slim), slim)
                row_refs[k][e, pl.ds(0, slim), :] = out_grad[rows, :].astype(jnp.bfloat16)
                rows = pl.ds(pl.multiple_of(target * piece, piece), piece)
                for j in range(2):
                    row_refs[k][e, pl.ds(slim + j * piece, piece), :] = gate_grads[j, rows, :].astype(
                        jnp.bfloat16
                    )


def mix_backward(place, near, far, age, chan, weights, saved):
    chips, rows, model = near.shape
    width, columns = weights.shape
    tall = (model + 2 * width) // (2 * chips)
    chunk = 2 * rows
    last = chips - 1
    time_block = lambda i, s: (last - i, 0)
    token_block = lambda i, s: (0, (last - i) ^ (s[0] // 2), 0, 0)
    spec = pl.BlockSpec((chunk, width), time_block)
    fixed = lambda shape: pl.BlockSpec(shape, lambda i, s: (0,) * len(shape))
    return pl.pallas_call(
        mix_backward_kernel,
        grid_spec=pltpu.PrefetchScalarGridSpec(
            num_scalar_prefetch=1,
            grid=(chips,),
            in_specs=[
                fixed(near.shape),
                fixed(far.shape),
                pl.BlockSpec((chunk, 1), time_block),
                pl.BlockSpec((chan.shape[0], width), lambda i, s: (0, s[0])),
                fixed((width, columns)),
            ]
            + [spec] * 7,
            out_specs=[
                pl.BlockSpec((2, None, rows, 2 * width), token_block),
                fixed((8, width)),
            ]
            + [fixed((2, tall, width))] * chips,
            scratch_shapes=[
                pltpu.VMEM((model, width), jnp.float32),
                pltpu.VMEM((2, width, width), jnp.float32),
                pltpu.VMEM((3, chunk + 8, width), jnp.float32),
                pltpu.VMEM((8, width), jnp.float32),
            ],
        ),
        out_shape=[
            jax.ShapeDtypeStruct((2, chips, rows, 2 * width), jnp.bfloat16),
            jax.ShapeDtypeStruct((8, width), jnp.float32),
        ]
        + [jax.ShapeDtypeStruct((2, tall, width), jnp.bfloat16)] * chips,
        compiler_params=pltpu.CompilerParams(vmem_limit_bytes=56 * 1024 * 1024),
        cost_estimate=pl.CostEstimate(
            flops=10**10, bytes_accessed=40 * 10**6, transcendentals=6 * width * 2 * chips * rows
        ),
        name="mix_backward",
    )(place, near, far, age, chan, weights, *saved)


def unit_kernel(
    near_ref,
    far_ref,
    cot_near_ref,
    cot_far_ref,
    pack_ref,
    back_near_out,
    back_far_out,
    mixed_near_out,
    mixed_far_out,
    grads_out,
    normed,
    cot,
    gate_up,
    down,
    pair,
    hidden,
    pair_t,
    hidden_t,
    grads,
    back,
    mixed,
    in_sems,
    out_sems,
):
    bf16 = jnp.bfloat16
    chips, rows, _ = near_ref.shape
    planes, tall, near_model = pack_ref.shape
    both = pair.shape[1]
    part = both // 2
    span = part // planes
    side = near_model // 2
    half = chips * rows
    incoming, outgoing = [], []

    def fetch(source, target):
        copy = pltpu.make_async_copy(source, target, in_sems.at[len(incoming)])
        copy.start()
        incoming.append(copy)
        return copy

    def send(source, target):
        copy = pltpu.make_async_copy(source, target, out_sems.at[len(outgoing)])
        copy.start()
        outgoing.append(copy)

    def fetch_half(source, target, i):
        return [
            fetch(source.at[k], target.at[pl.ds(i * half + k * rows, rows), :]) for k in range(chips)
        ]

    gate_up_copies = [
        fetch(
            pack_ref.at[z, pl.ds(j * near_model, near_model), :],
            gate_up.at[pl.ds(z * near_model, near_model), pl.ds(j * near_model, near_model)],
        )
        for z in range(planes)
        for j in range(3)
    ]
    normed_copies = [fetch_half(near_ref, normed, 0)]
    for copy in gate_up_copies + normed_copies[0]:
        copy.wait()
    down_copies = [
        fetch(
            pack_ref.at[z, pl.ds(3 * near_model + j * span, span), :],
            down.at[pl.ds(z * span, span), pl.ds(j * near_model, near_model)],
        )
        for z in range(planes)
        for j in range(planes)
    ]
    cot_copies = [fetch_half(cot_near_ref, cot, 0)]
    normed_copies.append(fetch_half(far_ref, normed, 1))
    cot_copies.append(fetch_half(cot_far_ref, cot, 1))
    chunk = 2 * rows
    first_unit, mid_unit, last_unit = (pl.ds(j * near_model, near_model) for j in range(3))
    for i in range(chips):
        here = pl.ds(i * chunk, chunk)
        if i * chunk == half:
            for copy in normed_copies[1] + cot_copies[1]:
                copy.wait()
        pre = dot_nn(normed[here, :], gate_up[...])
        if i == 0:
            for copy in down_copies + cot_copies[0]:
                copy.wait()
            down[pl.ds(part, side), :] = down[pl.ds(part - side, side), :]
        above = dot_nt(cot[here, :], down[...])
        up = pre[:, 2 * near_model :]
        value, slope = gelu_parts(pre[:, :near_model])
        grad = above[:, :near_model]
        hidden[here, first_unit] = (value * up).astype(bf16)
        pair[here, first_unit] = (grad * up * slope).astype(bf16)
        pair[here, last_unit] = (grad * value).astype(bf16)
        mid = pre[:, near_model : 2 * near_model]
        first = lax.broadcasted_iota(jnp.int32, mid.shape, 1) < side
        turned = pltpu.roll(mid, side, 1)
        gate, up = jnp.where(first, mid, turned), jnp.where(first, turned, mid)
        value, slope = gelu_parts(gate)
        grad = above[:, near_model:]
        hidden[here, pl.ds(near_model, side)] = (value * up)[:, :side].astype(bf16)
        pair[here, mid_unit] = jnp.where(first, grad * up * slope, grad * value).astype(bf16)
        pair_t[:, here] = pair[here, :].T
        hidden_t[:, here] = hidden[here, :].T
    low = pl.ds(both, planes * span)
    for z in range(planes):
        here = pl.ds(z * near_model, near_model)
        grad = dot_nn(hidden_t[...], cot[:, here]).astype(bf16)
        for j in range(planes):
            grads[j, pl.ds(both + z * span, span), :] = grad[j * span : (j + 1) * span]
    for z in range(planes):
        send(grads.at[z, low, :], grads_out.at[z, low, :])
    for z in range(planes):
        here = pl.ds(z * near_model, near_model)
        grads[z, pl.ds(0, both), :] = dot_nn(pair_t[...], normed[:, here]).astype(bf16)
        send(grads.at[z, pl.ds(0, both), :], grads_out.at[z, pl.ds(0, both), :])
    for i, out in ((0, mixed_near_out), (1, mixed_far_out)):
        here = pl.ds(i * half, half)
        mixed[here, :] = dot_nn(hidden[here, :], down[pl.ds(0, part), :]).astype(bf16)
        for k in range(chips):
            send(mixed.at[pl.ds(i * half + k * rows, rows), :], out.at[k])
    for i, out in ((1, back_far_out), (0, back_near_out)):
        here = pl.ds(i * half, half)
        back[here, :] = dot_nt(pair[here, :], gate_up[...]).astype(bf16)
        for k in range(chips):
            send(back.at[pl.ds(i * half + k * rows, rows), :], out.at[k])
    for copy in outgoing:
        copy.wait()


def unit_back_and_forth(near, far, cot_near, cot_far, pack, part):
    chips, rows, model = near.shape
    length = 2 * chips * rows
    planes, _, near_model = pack.shape
    bf16 = jnp.bfloat16
    there = pl.BlockSpec(memory_space=pl.ANY)
    return pl.pallas_call(
        unit_kernel,
        in_specs=[there] * 5,
        out_specs=[there] * 5,
        scratch_shapes=[
            pltpu.VMEM((length, model), bf16),
            pltpu.VMEM((length, model), bf16),
            pltpu.VMEM((model, 2 * part), bf16),
            pltpu.VMEM((part + near_model // 2, model), bf16),
            pltpu.VMEM((length, 2 * part), bf16),
            pltpu.VMEM((length, part), bf16),
            pltpu.VMEM((2 * part, length), bf16),
            pltpu.VMEM((part, length), bf16),
            pltpu.VMEM(pack.shape, bf16),
            pltpu.VMEM((length, model), bf16),
            pltpu.VMEM((length, model), bf16),
            pltpu.SemaphoreType.DMA((4 * chips + planes * (3 + planes),)),
            pltpu.SemaphoreType.DMA((4 * chips + 2 * planes,)),
        ],
        out_shape=[jax.ShapeDtypeStruct(near.shape, bf16)] * 4
        + [jax.ShapeDtypeStruct(pack.shape, bf16)],
        compiler_params=pltpu.CompilerParams(vmem_limit_bytes=58 * 1024 * 1024),
        name="unit_back_and_forth",
    )(near, far, cot_near, cot_far, pack)


def mix_pack_kernel(place_ref, input_ref, gelu_ref, out_ref, decay_ref, gate_ref, pack_ref):
    near_model, width = input_ref.shape
    heads, piece, model = out_ref.shape
    pack_ref[pl.ds(0, near_model), pl.ds(0, width)] = input_ref[...]
    pack_ref[pl.ds(0, near_model), pl.ds(width, width)] = gelu_ref[...]
    row = near_model
    for h in range(heads):
        for j in range(model // (2 * width)):
            pack_ref[pl.ds(row, piece), :] = out_ref[h, :, pl.ds(j * 2 * width, 2 * width)]
            row += piece
        pack_ref[pl.ds(row, piece), pl.ds(0, width)] = decay_ref[h]
        pack_ref[pl.ds(row, piece), pl.ds(width, width)] = gate_ref[h]
        row += piece


def own_mix_pack(place, input_proj, gelu_proj, output_proj, decay_gate, input_gate):
    near_model, channels = input_proj.shape
    width = decay_gate.shape[1]
    heads = decay_gate.shape[0] // width
    model = output_proj.shape[1]
    piece = width // (channels // width)
    tall = near_model + heads * (model // (2 * width) + 1) * piece
    mine = pl.BlockSpec((near_model, width), lambda i, s: (0, s[0]))
    rows = lambda columns: pl.BlockSpec((heads, piece, columns), lambda i, s: (0, s[0], 0))
    return pl.pallas_call(
        mix_pack_kernel,
        grid_spec=pltpu.PrefetchScalarGridSpec(
            num_scalar_prefetch=1,
            grid=(1,),
            in_specs=[mine, mine, rows(model), rows(width), rows(width)],
            out_specs=pl.BlockSpec((tall, 2 * width), lambda i, s: (0, 0)),
        ),
        out_shape=jax.ShapeDtypeStruct((tall, 2 * width), input_proj.dtype),
        name="own_mix_pack",
    )(
        place,
        input_proj,
        gelu_proj,
        output_proj.reshape(heads, width, model),
        decay_gate.reshape(heads, width, width),
        input_gate.reshape(heads, width, width),
    )


def unit_pack_kernel(place_ref, gate_ref, up_ref, down_ref, pack_ref, windows, sems):
    place = place_ref[0]
    near_model, deep = gate_ref.shape
    planes = windows.shape[1]
    tile = 128
    span = (pack_ref.shape[0] - 3 * near_model) // planes
    extra = span - tile
    copies = []

    def fetch(source, target):
        copies.append(pltpu.make_async_copy(source, target, sems.at[len(copies)]))
        copies[-1].start()

    for i, ref in enumerate((gate_ref, up_ref)):
        for z in range(planes):
            start = pl.multiple_of(z * (deep // planes) + place * tile, tile)
            fetch(ref.at[:, pl.ds(start, 2 * tile)], windows.at[i, z])
    rows = pl.ds(pl.multiple_of(place * span, 16), span)
    for j in range(planes):
        fetch(
            down_ref.at[rows, pl.ds(j * near_model, near_model)],
            pack_ref.at[pl.ds(3 * near_model + j * span, span), :],
        )
    lane = lax.broadcasted_iota(jnp.int32, (near_model, tile), 1)

    def tiles(i):
        parts = []
        for z in range(planes):
            copies[i * planes + z].wait()
            turn = lax.rem((z - place) * extra + 2 * tile, 2 * tile)
            parts.append(pltpu.roll(windows[i, z].astype(jnp.float32), turn, 1))
        found = [parts[0][:, :tile]]
        for z in range(1, planes):
            found.append(jnp.where(lane < z * extra, parts[z - 1][:, tile:], parts[z][:, :tile]))
        return found + [parts[planes - 1][:, tile:]]

    gate, up = tiles(0), tiles(1)
    half = tile // 2
    turned = [pltpu.roll(up[j], half, 1) for j in (3, 4)]
    mid = [
        gate[3],
        jnp.where(lane < half, gate[4], turned[0]),
        jnp.where(lane < half, turned[0], turned[1]),
    ]
    for block, found in enumerate((gate[:3], mid, up[:3])):
        for j in range(3):
            pack_ref[pl.ds(block * near_model, near_model), pl.ds(j * tile, tile)] = found[
                j
            ].astype(pack_ref.dtype)
    for copy in copies[2 * planes :]:
        copy.wait()


def own_unit_pack(place, mlp_gate, mlp_up, mlp_down, planes, span):
    near_model = mlp_gate.shape[0]
    tall = 3 * near_model + planes * span
    there = pl.BlockSpec(memory_space=pl.ANY)
    return pl.pallas_call(
        unit_pack_kernel,
        grid_spec=pltpu.PrefetchScalarGridSpec(
            num_scalar_prefetch=1,
            grid=(1,),
            in_specs=[there] * 3,
            out_specs=pl.BlockSpec((tall, near_model), lambda i, s: (0, 0)),
            scratch_shapes=[
                pltpu.VMEM((2, planes, near_model, 256), mlp_gate.dtype),
                pltpu.SemaphoreType.DMA((3 * planes,)),
            ],
        ),
        out_shape=jax.ShapeDtypeStruct((tall, near_model), mlp_gate.dtype),
        compiler_params=pltpu.CompilerParams(vmem_limit_bytes=48 * 1024 * 1024),
        name="own_unit_pack",
    )(place, mlp_gate, mlp_up, mlp_down)


def grad_pack_kernel(place_ref, in_ref, *refs):
    *blocks, pack_ref = refs
    place = place_ref[0]
    chips = len(blocks) // 2
    chip, core = place // 2, place % 2
    near_model, both = in_ref.shape[1:]
    tall, width = blocks[0].shape
    pack_ref[:, pl.ds(0, near_model), :] = in_ref[...]
    for k in range(chips):
        home, away = blocks[k][...], blocks[chips + k][...]
        odd = core == 1
        pack_ref[chip ^ k, pl.ds(near_model, tall), pl.ds(0, width)] = jnp.where(odd, away, home)
        pack_ref[chip ^ k, pl.ds(near_model, tall), pl.ds(width, width)] = jnp.where(odd, home, away)


def grad_pack(place, in_grad, home, away):
    planes, near_model, both = in_grad.shape
    tall, width = home[0].shape
    return pl.pallas_call(
        grad_pack_kernel,
        grid_spec=pltpu.PrefetchScalarGridSpec(
            num_scalar_prefetch=1,
            grid=(1,),
            in_specs=[pl.BlockSpec(in_grad.shape, lambda i, s: (0, 0, 0))]
            + [pl.BlockSpec((tall, width), lambda i, s: (0, 0))] * (2 * len(home)),
            out_specs=pl.BlockSpec((planes, near_model + tall, both), lambda i, s: (0, 0, 0)),
        ),
        out_shape=jax.ShapeDtypeStruct((planes, near_model + tall, both), jnp.bfloat16),
        compiler_params=pltpu.CompilerParams(vmem_limit_bytes=32 * 1024 * 1024),
        name="grad_pack",
    )(place, in_grad, *home, *away)


def norm_back(values, scale, gain, grad):
    inner = jnp.mean(gain * grad * values, axis=-1, keepdims=True)
    return scale * gain * grad - values * (scale * scale * scale) * inner


def narrow_shards(
    tokens,
    cotangent,
    doc_starts,
    mix_gain,
    input_proj,
    gelu_proj,
    conv_taps,
    conv_bias,
    decay_gate,
    decay_bias,
    input_gate,
    input_bias,
    decay_param,
    output_proj,
    mlp_gain,
    mlp_gate,
    mlp_up,
    mlp_down,
):
    f32, bf16 = jnp.float32, jnp.bfloat16
    devices, planes = lax.axis_size("seq"), lax.axis_size("fsdp")
    chips = devices // 2
    place = lax.axis_index("seq")
    chip, core = place // 2, place % 2
    rows, model = tokens.shape[1:]
    length = rows * devices
    channels = conv_taps.shape[1]
    width = decay_gate.shape[1]
    deep = mlp_gate.shape[1]
    heads = output_proj.shape[0] // width
    piece = width // devices
    span = deep // (planes * devices)
    part = deep // devices
    near_model = model // planes

    def along_fsdp(x):
        return lax.all_gather(x, "fsdp", axis=0, tiled=True)

    def columns(x, start, size):
        return lax.dynamic_slice_in_dim(x, start, size, axis=1)

    place_arg = place.astype(jnp.int32)[None]
    mix_pack, tokens = tie(
        own_mix_pack(place_arg, input_proj, gelu_proj, output_proj, decay_gate, input_gate), tokens
    )
    mix_pack = lax.all_gather(mix_pack, "fsdp", axis=0)

    values = tokens[0].astype(f32)
    scale1 = lax.rsqrt(jnp.mean(values * values, axis=-1, keepdims=True) + norm_eps)
    normed_own, mlp_gate, mlp_up, mlp_down = tie(
        (values * scale1 * mix_gain).astype(bf16), mlp_gate, mlp_up, mlp_down
    )
    normed_near, normed_far = gather_blocks(normed_own)
    unit_pack = own_unit_pack(place_arg, mlp_gate, mlp_up, mlp_down, planes, span)
    unit_pack, normed_near, normed_far, out_grad = tie(
        unit_pack, normed_near, normed_far, cotangent[0]
    )
    unit_pack = lax.all_gather(unit_pack, "fsdp", axis=0)
    cot_near, cot_far = gather_blocks(out_grad)

    positions = jnp.arange(length, dtype=jnp.int32)
    starts = doc_starts[0]
    begin = jnp.max(jnp.where(starts[None, :] <= positions[:, None], starts[None, :], 0), axis=1)
    age = (positions - begin).astype(f32)[:, None]
    chan = jnp.concatenate(
        [
            conv_taps,
            conv_bias[None],
            decay_bias[None],
            input_bias[None],
            jax.nn.softplus(-decay_param)[None],
            jax.nn.sigmoid(-decay_param)[None],
            jnp.zeros((7, channels), f32),
        ],
        axis=0,
    )

    mix_pack, cot_near, cot_far, normed_near, normed_far = tie(
        mix_pack, cot_near, cot_far, normed_near, normed_far
    )
    keep, got = exchange(mix_pack[:, near_model:].reshape(chips, 2, -1, 2 * width), chip, core, 0)
    merged, *saved, weights = mix_forward(
        place_arg, normed_near, normed_far, age, chan, mix_pack, keep, got
    )
    out_weights = weights[:, :model]
    in_weights = mix_pack[:, :near_model].reshape(model, 2 * width)
    far = dot_nn(merged[1].reshape(-1, width), out_weights).astype(bf16)
    near = dot_nn(merged[0].reshape(-1, width), out_weights)
    middle = values + scatter_blocks(
        near.reshape(chips, rows, model), far.reshape(chips, rows, model)
    )

    scale2 = lax.rsqrt(jnp.mean(middle * middle, axis=-1, keepdims=True) + norm_eps)
    near, far = gather_blocks((middle * scale2 * mlp_gain).astype(bf16))
    back_near, back_far, mixed_near, mixed_far, unit_grads = unit_back_and_forth(
        near, far, cot_near, cot_far, unit_pack, part
    )
    unit_sum = lax.psum_scatter(unit_grads, "fsdp", scatter_dimension=0, tiled=False)
    normed2_grad = scatter_blocks(back_near, back_far)

    mlp_gain_term = jnp.sum(normed2_grad * middle * scale2, axis=0)
    middle_grad = out_grad.astype(f32) + norm_back(middle, scale2, mlp_gain, normed2_grad)
    middle_low, mixed_near, mixed_far = tie(middle_grad.astype(bf16), mixed_near, mixed_far)
    near, far = gather_blocks(middle_low)
    mixed_low, mixed_own = pair_blocks(mixed_near, mixed_far)
    near, far, mixed_low, mixed_own = tie(near, far, mixed_low, mixed_own)

    both, small, *by_chip = mix_backward(place_arg, near, far, age, chan, weights, saved)
    mixed = (middle + spread_pairs(mixed_low, mixed_own)).astype(bf16)
    mixed, *by_chip = tie(mixed, *by_chip)
    arrived = [by_chip[0]] + [chip_swap(by_chip[k], k) for k in range(1, chips)]
    in_grad = dot_tn(normed_near.reshape(-1, model), both[0].reshape(-1, 2 * width)) + dot_tn(
        normed_far.reshape(-1, model), both[1].reshape(-1, 2 * width)
    )
    *arrived, both = tie(*arrived, both)
    away = core_swap(jnp.stack([block[1] for block in arrived]))
    pack, unit_sum, small, both = tie(
        grad_pack(
            place_arg,
            in_grad.astype(bf16).reshape(planes, near_model, 2 * width),
            [block[0] for block in arrived],
            [away[k] for k in range(chips)],
        ),
        unit_sum,
        small,
        both,
    )
    mix_sum = lax.psum_scatter(pack, "fsdp", scatter_dimension=0, tiled=False).astype(f32)
    input_proj_grad = mix_sum[:near_model, :width]
    gelu_proj_grad = mix_sum[:near_model, width:]
    turned_sum = mix_sum[near_model:].T
    slim = model // devices
    output_proj_grad = turned_sum[:, :slim]
    decay_gate_grad = turned_sum[:, slim : slim + piece]
    input_gate_grad = turned_sum[:, slim + piece :]

    normed_grad = scatter_blocks(
        dot_nt(both[0].reshape(-1, 2 * width), in_weights).reshape(chips, rows, model),
        dot_nt(both[1].reshape(-1, 2 * width), in_weights).astype(bf16).reshape(chips, rows, model),
    )

    up_first = unit_sum[part + near_model // 2 : 2 * part]
    up_sum = jnp.concatenate([up_first, unit_sum[part : part + near_model // 2]], axis=0)
    gate_up_sum = jnp.stack([unit_sum[:part], up_sum]).reshape(2, planes, span, near_model)
    mlp_gate_grad, mlp_up_grad, mlp_down_grad = final_exchange(
        gate_up_sum.swapaxes(0, 1),
        unit_sum[2 * part :].reshape(planes, span, near_model),
        chip,
        core,
        chips,
    )

    mix_gain_term = jnp.sum(in_grad * in_weights.astype(f32), axis=1) / mix_gain
    gains = jnp.stack([mix_gain_term, mlp_gain_term]).reshape(-1, width)
    small = over_planes(jnp.concatenate([small, gains], axis=0))
    values_part = norm_back(values, scale1, mix_gain, normed_grad)
    tokens_grad = (middle_grad + values_part).astype(bf16)
    where_mine = (jnp.arange(devices) == place)[None, :, None]
    spread = jnp.where(where_mine, small[:8, None, :], 0.0).reshape(8, channels)
    gains = jnp.pad(small[8:].reshape(2, model), ((0, 0), (0, channels - model)))
    sums = total_over(jnp.concatenate([spread, gains], axis=0), ("seq",))
    return (
        mixed[None],
        tokens_grad[None],
        sums[8, :model],
        input_proj_grad,
        gelu_proj_grad,
        sums[:4],
        sums[4],
        decay_gate_grad,
        sums[5],
        input_gate_grad,
        sums[6],
        sums[7],
        output_proj_grad,
        sums[9, :model],
        mlp_gate_grad,
        mlp_up_grad,
        mlp_down_grad,
    )


def final_exchange(gate_up_sum, down_sum, chip, core, chips):
    f32 = jnp.float32
    span, cols = down_sum.shape[1:]
    half = cols // 2
    sent = jnp.concatenate([gate_up_sum, down_sum[:, None]], axis=1)
    parts = [lax.dynamic_index_in_dim(sent, chip ^ k, 0, keepdims=False) for k in range(chips)]
    got = [parts[0]] + [chip_swap(parts[k], k) for k in range(1, chips)]
    turn = core ^ (chip // 2)
    low, high = jnp.stack(got[:2]), jnp.stack(got[2:])
    keep_gu = jnp.where(turn == 0, low[:, :2], high[:, :2])
    give_gu = jnp.where(turn == 0, high[:, :2], low[:, :2])
    downs = jnp.stack([g[2] for g in got])
    keep_d = jnp.where(core == 0, downs[:, :, :half], downs[:, :, half:])
    give_d = jnp.where(core == 0, downs[:, :, half:], downs[:, :, :half])
    got_gu, got_d = core_swap(give_gu), core_swap(give_d)
    home = reorder([keep_gu[0], keep_gu[1]], chip & 1)
    away = reorder([got_gu[0], got_gu[1]], chip & 1)
    blocks = []
    for x in range(2):
        blocks.append(jnp.where(core == 0, home[x], away[x]))
        blocks.append(jnp.where(core == 0, away[x], home[x]))
    gate_up = jnp.concatenate(blocks, axis=1).astype(f32)
    home = reorder([keep_d[k] for k in range(chips)], chip)
    away = reorder([got_d[k] for k in range(chips)], chip)
    blocks = []
    for k in range(chips):
        blocks.append(jnp.where(core == 0, home[k], away[k]))
        blocks.append(jnp.where(core == 0, away[k], home[k]))
    return gate_up[0].T, gate_up[1].T, jnp.concatenate(blocks, axis=0).astype(f32)


def choose_plan(mesh):
    devices, planes = mesh.shape["seq"], mesh.shape["fsdp"]

    def plan(*args):
        channels, width = args[6].shape[1], args[8].shape[1]
        if channels == width * devices and devices == 2 * planes and planes == 4:
            return narrow_shards(*args)
        return wide_shards(*args)

    return plan


def solution(mesh):
    return jax.shard_map(
        choose_plan(mesh),
        mesh=mesh,
        in_specs=(
            P("fsdp", "seq", None),
            P("fsdp", "seq", None),
            P("fsdp", None),
            P(),
            P("fsdp", None),
            P("fsdp", None),
            P(),
            P(),
            P("fsdp", None),
            P(),
            P("fsdp", None),
            P(),
            P(),
            P("fsdp", None),
            P(),
            P("fsdp", None),
            P("fsdp", None),
            P("fsdp", None),
        ),
        out_specs=(
            P("fsdp", "seq", None),
            P("fsdp", "seq", None),
            P(),
            P("fsdp", "seq"),
            P("fsdp", "seq"),
            P(),
            P(),
            P("fsdp", "seq"),
            P(),
            P("fsdp", "seq"),
            P(),
            P(),
            P("fsdp", "seq"),
            P(),
            P("fsdp", "seq"),
            P("fsdp", "seq"),
            P("fsdp", "seq"),
        ),
        check_vma=False,
    )
```

```python
import functools

import jax
import jax.numpy as jnp
from jax import lax
from jax.experimental import pallas as pl
from jax.experimental.pallas import tpu as pltpu
from jax.sharding import PartitionSpec as P

norm_eps = 1e-06
mult_floor = 0.0001


def from_behind(x, axis, by):
    devices = lax.axis_size(axis)
    pairs = [(i, i + by) for i in range(devices) if 0 <= i + by < devices]
    return lax.ppermute(x, axis, pairs)


def rms_scale(values, gain):
    scale = lax.rsqrt(jnp.mean(values * values, axis=-1, keepdims=True) + norm_eps)
    return values * scale * gain


def smooth_gelu(values):
    return jax.nn.gelu(values, approximate=True)


def gated_unit(gate, up_val):
    return smooth_gelu(gate) * up_val


def affine_pair(earlier, later):
    return (earlier[0] * later[0], earlier[1] * later[0] + later[1])


def decay_terms(conv_out, decay_pre, input_pre, decay_param, resets):
    log_a = -8.0 * jax.nn.sigmoid(decay_pre) * jax.nn.softplus(-decay_param)
    room = jnp.maximum(-jnp.expm1(2.0 * log_a), mult_floor)
    factor = jnp.where(resets, 1.0, jnp.sqrt(room))
    decay = jnp.where(resets, 0.0, jnp.exp(log_a))
    return (decay, jax.nn.sigmoid(input_pre) * conv_out * factor)


def conv_apply(extended, taps_w, bias, masks):
    taps = taps_w.shape[0]
    rows = masks.shape[1]
    total = jnp.zeros((rows, taps_w.shape[1]), jnp.float32) + bias
    for shift_k in range(taps):
        begin_row = taps - 1 - shift_k
        total = total + taps_w[shift_k] * extended[begin_row : begin_row + rows] * masks[shift_k]
    return total


def block_product(left, weight):
    width = weight.shape[1]
    blocks = weight.shape[0] // width
    result = jnp.einsum(
        "nhk,hkj->nhj",
        left.reshape(left.shape[0], blocks, width),
        weight.reshape(blocks, width, width),
        preferred_element_type=jnp.float32,
    )
    return result.reshape(left.shape[0], -1)


def block_back(grad, weight):
    width = weight.shape[1]
    blocks = weight.shape[0] // width
    result = jnp.einsum(
        "nhj,hkj->nhk",
        grad.reshape(grad.shape[0], blocks, width),
        weight.reshape(blocks, width, width),
        preferred_element_type=jnp.float32,
    )
    return result.reshape(grad.shape[0], -1)


def block_weight_grad(left, grad, width):
    blocks = left.shape[1] // width
    result = jnp.einsum(
        "nhk,nhj->hkj",
        left.reshape(left.shape[0], blocks, width),
        grad.reshape(grad.shape[0], blocks, width),
        preferred_element_type=jnp.float32,
    )
    return result.reshape(blocks * width, width)


def wide_shards(
    tokens,
    cotangent,
    doc_starts,
    mix_gain,
    input_proj,
    gelu_proj,
    conv_taps,
    conv_bias,
    decay_gate,
    decay_bias,
    input_gate,
    input_bias,
    decay_param,
    output_proj,
    mlp_gain,
    mlp_gate,
    mlp_up,
    mlp_down,
):
    rows = tokens.shape[1]
    taps = conv_taps.shape[0]
    width = decay_gate.shape[1]
    input_w, gelu_w, output_w, decay_w, inputg_w, gate_w, up_w, down_w = (
        lax.all_gather(input_proj, "fsdp", axis=0, tiled=True),
        lax.all_gather(gelu_proj, "fsdp", axis=0, tiled=True),
        lax.all_gather(output_proj, "fsdp", axis=0, tiled=True),
        lax.all_gather(decay_gate, "fsdp", axis=0, tiled=True),
        lax.all_gather(input_gate, "fsdp", axis=0, tiled=True),
        lax.all_gather(mlp_gate, "fsdp", axis=0, tiled=True),
        lax.all_gather(mlp_up, "fsdp", axis=0, tiled=True),
        lax.all_gather(mlp_down, "fsdp", axis=0, tiled=True),
    )
    channels = input_w.shape[1]
    first = lax.axis_index("seq") * rows
    positions = first + jnp.arange(rows, dtype=jnp.int32)
    starts = doc_starts[0]
    begin = jnp.max(jnp.where(starts[None, :] <= positions[:, None], starts[None, :], 0), axis=1)
    resets = (begin == positions)[:, None]
    masks = jnp.stack([(positions - k >= begin)[:, None] for k in range(taps)]).astype(jnp.float32)
    values = tokens[0].astype(jnp.float32)
    normed = rms_scale(values, mix_gain).astype(jnp.bfloat16)
    branch = jnp.dot(normed, input_w, preferred_element_type=jnp.float32).astype(jnp.bfloat16)
    gelu_pre = jnp.dot(normed, gelu_w, preferred_element_type=jnp.float32)
    gelu_out = smooth_gelu(gelu_pre)
    previous = from_behind(branch[rows - (taps - 1) :], "seq", 1)
    extended = jnp.concatenate([previous, branch], axis=0).astype(jnp.float32)
    conv_f = conv_apply(extended, conv_taps, conv_bias, masks).astype(jnp.bfloat16)
    conv_val = conv_f.astype(jnp.float32)
    decay_pre = block_product(conv_f, decay_w) + decay_bias
    input_pre = block_product(conv_f, inputg_w) + input_bias
    decay, driven = decay_terms(conv_val, decay_pre, input_pre, decay_param, resets)
    decay_cols, driven_cols = (
        lax.all_to_all(decay, "seq", split_axis=1, concat_axis=0, tiled=True),
        lax.all_to_all(driven, "seq", split_axis=1, concat_axis=0, tiled=True),
    )
    states_cols = lax.associative_scan(affine_pair, (decay_cols, driven_cols), axis=0)[1]
    states_low = lax.all_to_all(
        states_cols.astype(jnp.bfloat16), "seq", split_axis=0, concat_axis=1, tiled=True
    )
    states_val = states_low.astype(jnp.float32)
    merged = (states_val * gelu_out).astype(jnp.bfloat16)
    middle = values + jnp.dot(merged, output_w, preferred_element_type=jnp.float32)
    normed2 = rms_scale(middle, mlp_gain).astype(jnp.bfloat16)
    gate = jnp.dot(normed2, gate_w, preferred_element_type=jnp.float32)
    up_val = jnp.dot(normed2, up_w, preferred_element_type=jnp.float32)
    hidden = gated_unit(gate, up_val).astype(jnp.bfloat16)
    mixed = (middle + jnp.dot(hidden, down_w, preferred_element_type=jnp.float32)).astype(
        jnp.bfloat16
    )
    out_grad = cotangent[0]
    down_grad = jnp.einsum("tf,td->fd", hidden, out_grad, preferred_element_type=jnp.float32)
    hidden_grad = jnp.einsum("td,fd->tf", out_grad, down_w, preferred_element_type=jnp.float32)
    unit_pull = jax.vjp(gated_unit, gate, up_val)[1]
    gate_grad, up_grad = unit_pull(hidden_grad)
    gate_low = gate_grad.astype(jnp.bfloat16)
    up_low = up_grad.astype(jnp.bfloat16)
    gate_w_grad = jnp.einsum("td,tf->df", normed2, gate_low, preferred_element_type=jnp.float32)
    up_w_grad = jnp.einsum("td,tf->df", normed2, up_low, preferred_element_type=jnp.float32)
    mlp_terms = (
        lax.psum_scatter(gate_w_grad, "seq", scatter_dimension=1, tiled=True),
        lax.psum_scatter(up_w_grad, "seq", scatter_dimension=1, tiled=True),
        lax.psum_scatter(down_grad, "seq", scatter_dimension=1, tiled=True),
    )
    mlp_gate_grad, mlp_up_grad, mlp_down_grad = (
        lax.psum_scatter(mlp_terms[0], "fsdp", scatter_dimension=0, tiled=True),
        lax.psum_scatter(mlp_terms[1], "fsdp", scatter_dimension=0, tiled=True),
        lax.psum_scatter(mlp_terms[2], "fsdp", scatter_dimension=0, tiled=True),
    )
    normed2_grad = jnp.einsum(
        "tf,df->td", gate_low, gate_w, preferred_element_type=jnp.float32
    ) + jnp.einsum("tf,df->td", up_low, up_w, preferred_element_type=jnp.float32)
    norm2_pull = jax.vjp(rms_scale, middle, mlp_gain)[1]
    middle_part, mlp_gain_term = norm2_pull(normed2_grad)
    middle_grad = out_grad.astype(jnp.float32) + middle_part
    mixer_grad = middle_grad.astype(jnp.bfloat16)
    output_w_grad = jnp.einsum("tr,td->rd", merged, mixer_grad, preferred_element_type=jnp.float32)
    merged_grad = jnp.einsum("td,rd->tr", mixer_grad, output_w, preferred_element_type=jnp.float32)
    state_low = (merged_grad * gelu_out).astype(jnp.bfloat16)
    gelu_pull = jax.vjp(smooth_gelu, gelu_pre)[1]
    gelu_pre_low = gelu_pull(merged_grad * states_val)[0].astype(jnp.bfloat16)
    grad_cols = lax.all_to_all(state_low, "seq", split_axis=1, concat_axis=0, tiled=True).astype(
        jnp.float32
    )
    width_cols = grad_cols.shape[1]
    next_decay = jnp.concatenate([decay_cols[1:], jnp.zeros((1, width_cols), jnp.float32)], axis=0)
    carried = lax.associative_scan(affine_pair, (next_decay, grad_cols), reverse=True, axis=0)[1]
    prior = jnp.concatenate([jnp.zeros((1, width_cols), jnp.float32), states_cols[:-1]], axis=0)
    decay_grad, driven_grad = (
        lax.all_to_all(carried * prior, "seq", split_axis=0, concat_axis=1, tiled=True),
        lax.all_to_all(carried, "seq", split_axis=0, concat_axis=1, tiled=True),
    )
    terms_pull = jax.vjp(
        lambda conv_in, dpre, ipre, dparam: decay_terms(conv_in, dpre, ipre, dparam, resets),
        conv_val,
        decay_pre,
        input_pre,
        decay_param,
    )[1]
    gate_conv_grad, dpre_grad, ipre_grad, decay_param_term = terms_pull((decay_grad, driven_grad))
    dpre_low = dpre_grad.astype(jnp.bfloat16)
    ipre_low = ipre_grad.astype(jnp.bfloat16)
    decay_w_grad = block_weight_grad(conv_f, dpre_low, width)
    inputg_w_grad = block_weight_grad(conv_f, ipre_low, width)
    conv_grad = gate_conv_grad + block_back(dpre_low, decay_w) + block_back(ipre_low, inputg_w)
    conv_pull = jax.vjp(
        lambda ext, taps_w, bias: conv_apply(ext, taps_w, bias, masks),
        extended,
        conv_taps,
        conv_bias,
    )[1]
    extended_grad, taps_term, conv_bias_term = conv_pull(conv_grad)
    returned = from_behind(extended_grad[: taps - 1], "seq", -1)
    branch_grad = extended_grad[taps - 1 :] + jnp.concatenate(
        [jnp.zeros((rows - (taps - 1), channels), jnp.float32), returned], axis=0
    )
    branch_low = branch_grad.astype(jnp.bfloat16)
    input_w_grad = jnp.einsum("td,tr->dr", normed, branch_low, preferred_element_type=jnp.float32)
    gelu_w_grad = jnp.einsum("td,tr->dr", normed, gelu_pre_low, preferred_element_type=jnp.float32)
    mix_terms = (
        lax.psum_scatter(input_w_grad, "seq", scatter_dimension=1, tiled=True),
        lax.psum_scatter(gelu_w_grad, "seq", scatter_dimension=1, tiled=True),
        lax.psum_scatter(output_w_grad, "seq", scatter_dimension=1, tiled=True),
        lax.psum_scatter(decay_w_grad, "seq", scatter_dimension=1, tiled=True),
        lax.psum_scatter(inputg_w_grad, "seq", scatter_dimension=1, tiled=True),
    )
    input_proj_grad, gelu_proj_grad, output_proj_grad, decay_gate_grad, input_gate_grad = (
        lax.psum_scatter(mix_terms[0], "fsdp", scatter_dimension=0, tiled=True),
        lax.psum_scatter(mix_terms[1], "fsdp", scatter_dimension=0, tiled=True),
        lax.psum_scatter(mix_terms[2], "fsdp", scatter_dimension=0, tiled=True),
        lax.psum_scatter(mix_terms[3], "fsdp", scatter_dimension=0, tiled=True),
        lax.psum_scatter(mix_terms[4], "fsdp", scatter_dimension=0, tiled=True),
    )
    normed_grad = jnp.einsum(
        "tr,dr->td", branch_low, input_w, preferred_element_type=jnp.float32
    ) + jnp.einsum("tr,dr->td", gelu_pre_low, gelu_w, preferred_element_type=jnp.float32)
    norm1_pull = jax.vjp(rms_scale, values, mix_gain)[1]
    values_part, mix_gain_term = norm1_pull(normed_grad)
    tokens_grad = (middle_grad + values_part).astype(jnp.bfloat16)
    (
        mix_gain_grad,
        conv_taps_grad,
        conv_bias_grad,
        decay_bias_grad,
        input_bias_grad,
        decay_param_grad,
        mlp_gain_grad,
    ) = lax.psum(
        (
            mix_gain_term,
            taps_term,
            conv_bias_term,
            jnp.sum(dpre_low.astype(jnp.float32), axis=0),
            jnp.sum(ipre_low.astype(jnp.float32), axis=0),
            decay_param_term,
            mlp_gain_term,
        ),
        ("seq", "fsdp"),
    )
    return (
        mixed[None],
        tokens_grad[None],
        mix_gain_grad,
        input_proj_grad,
        gelu_proj_grad,
        conv_taps_grad,
        conv_bias_grad,
        decay_gate_grad,
        decay_bias_grad,
        input_gate_grad,
        input_bias_grad,
        decay_param_grad,
        output_proj_grad,
        mlp_gain_grad,
        mlp_gate_grad,
        mlp_up_grad,
        mlp_down_grad,
    )


def chip_swap(x, k):
    devices = lax.axis_size("seq")
    return lax.ppermute(x, "seq", [(i, i ^ (2 * k)) for i in range(devices)])


def core_swap(x):
    devices = lax.axis_size("seq")
    return lax.ppermute(x, "seq", [(i, i ^ 1) for i in range(devices)])


def gather_blocks(x):
    chips = lax.axis_size("seq") // 2
    near = jnp.stack([x] + [chip_swap(x, k) for k in range(1, chips)])
    return near, core_swap(near)


def tie(*arrays):
    return lax.optimization_barrier(arrays)


def pair_blocks(near, far, extra=None):
    if extra is None:
        extra = jnp.zeros((0, near.shape[2]), jnp.bfloat16)
    return payloads(near, core_swap(far), extra)


def spread_pairs(own, *low):
    return own, *[chip_swap(block, k + 1) for k, block in enumerate(low)]


def exchange(x, chip, core, turn):
    chips = x.shape[0]
    parts = [
        lax.dynamic_index_in_dim(x, chip ^ k ^ turn, 0, keepdims=False) for k in range(chips)
    ]
    got = jnp.stack([parts[0]] + [chip_swap(parts[k], k) for k in range(1, chips)])
    keep = lax.dynamic_index_in_dim(got, core, 1, keepdims=False)
    give = lax.dynamic_index_in_dim(got, 1 - core, 1, keepdims=False)
    return keep, core_swap(give)


def over_planes(x):
    planes = lax.axis_size("fsdp")
    total = x
    for k in range(1, planes):
        got = lax.ppermute(x.astype(jnp.bfloat16), "fsdp", [(i, i ^ k) for i in range(planes)])
        total = total + got.astype(jnp.float32)
    return total


little = pl.CostEstimate(flops=0, bytes_accessed=0, transcendentals=0)


def gelu_parts(v):
    root = 0.7978845608028654
    square = v * v
    h = 0.5 + 0.5 * jnp.tanh(v * (root + root * 0.044715 * square))
    value = v * h
    return value, h + value * (1.0 - h) * (2.0 * root + root * 0.26829 * square)


def sigmoid(v):
    return 1.0 / (1.0 + jnp.exp(-v))


def one_less_exp(v):
    series = -v * (1.0 + v * (0.5 + v * (1.0 / 6.0 + v * (1.0 / 24.0 + v * (1.0 / 120.0)))))
    return jnp.where(v > -0.1, series, 1.0 - jnp.exp(v))


def dot_nn(a, b):
    return lax.dot_general(a, b, (((1,), (0,)), ((), ())), preferred_element_type=jnp.float32)


def dot_nt(a, b):
    return lax.dot_general(a, b, (((1,), (1,)), ((), ())), preferred_element_type=jnp.float32)


def dot_tn(a, b):
    return lax.dot_general(a, b, (((0,), (0,)), ((), ())), preferred_element_type=jnp.float32)


def scan_rows(a, b, carry, later):
    rows = a.shape[0]
    group = 8
    row = lax.broadcasted_iota(jnp.int32, a.shape, 0) % group
    step = 1
    while step < group:
        turn = rows - step if later else step
        there = (row < group - step) if later else (row >= step)
        a_next = jnp.where(there, pltpu.roll(a, turn, 0), 1.0)
        b_next = jnp.where(there, pltpu.roll(b, turn, 0), 0.0)
        b = a * b_next + b
        a = a * a_next
        step *= 2
    starts = list(range(0, rows, group))
    done = {}
    for start in reversed(starts) if later else starts:
        states = a[start : start + group] * carry + b[start : start + group]
        done[start] = states
        carry = states[:1] if later else states[group - 1 :]
    return jnp.concatenate([done[start] for start in starts], axis=0)


def in_time(value, core):
    rows = value.shape[0] // 2
    near, far = value[:rows], value[rows:]
    odd = core == 1
    return jnp.concatenate([jnp.where(odd, far, near), jnp.where(odd, near, far)], axis=0)


def by_core(value, ref, core):
    rows = value.shape[0] // 2
    first, second = value[:rows], value[rows:]
    odd = core == 1
    ref[0] = jnp.where(odd, second, first).astype(ref.dtype)
    ref[1] = jnp.where(odd, first, second).astype(ref.dtype)


def mix_forward_kernel(
    seq_ref,
    near_ref,
    far_ref,
    age_ref,
    chan_ref,
    in_ref,
    keep_ref,
    got_ref,
    merged_ref,
    middle_near_ref,
    middle_far_ref,
    branch_ref,
    conv_ref,
    gelu_ref,
    gelu_grad_ref,
    decay_ref,
    input_ref,
    direct_ref,
    sig_ref,
    decay_grad_ref,
    weights_ref,
    extended,
    carry,
):
    place = seq_ref[0]
    chips = near_ref.shape[0]
    step = pl.program_id(0)
    chip, core = place // 2, place % 2
    rows, width = branch_ref.shape
    planes, near_model, both = in_ref.shape
    model = planes * near_model
    parts = weights_ref.shape[1] // both
    piece = keep_ref.shape[1] // parts

    @pl.when(step == 0)
    def _():
        extended[pl.ds(0, 8), :] = jnp.zeros((8, width), jnp.float32)
        carry[...] = jnp.zeros_like(carry)
        for k in range(chips):
            home = pl.multiple_of(piece * 2 * (chip ^ k) + piece * core, piece)
            away = pl.multiple_of(piece * 2 * (chip ^ k) + piece * (1 - core), piece)
            for j in range(parts):
                where = pl.ds(j * both, both)
                weights_ref[pl.ds(home, piece), where] = keep_ref[k, pl.ds(j * piece, piece), :]
                weights_ref[pl.ds(away, piece), where] = got_ref[k, pl.ds(j * piece, piece), :]

    @pl.when(step > 0)
    def _():
        extended[pl.ds(0, 8), :] = extended[pl.ds(rows, 8), :]

    turn = step ^ chip
    normed = jnp.concatenate([near_ref[turn], far_ref[turn]], axis=0)
    pre = in_time(dot_nn(normed, in_ref[...].reshape(model, both)), core)
    branch = pre[:, :width].astype(jnp.bfloat16)
    gelu_pre = pre[:, width:]
    branch_ref[...] = branch
    extended[pl.ds(8, rows), :] = branch.astype(jnp.float32)
    age = age_ref[...]
    total = jnp.zeros((rows, width), jnp.float32) + chan_ref[4:5, :]
    for k in range(4):
        shifted = extended[pl.ds(8 - k, rows), :]
        total = total + chan_ref[k : k + 1, :] * shifted * jnp.where(age >= k, 1.0, 0.0)
    conv_low = total.astype(jnp.bfloat16)
    conv = conv_low.astype(jnp.float32)
    conv_ref[...] = conv_low
    decay_pre = dot_nn(conv_low, weights_ref[:, model : model + width]) + chan_ref[5:6, :]
    input_pre = dot_nn(conv_low, weights_ref[:, model + width :]) + chan_ref[6:7, :]
    sig_d, sig_i = sigmoid(decay_pre), sigmoid(input_pre)
    soft = chan_ref[7:8, :]
    log_a = -8.0 * sig_d * soft
    reset = age < 0.5
    open_room = one_less_exp(2.0 * log_a)
    root = jnp.sqrt(jnp.maximum(open_room, mult_floor))
    factor = jnp.where(reset, 1.0, root)
    a = jnp.exp(log_a)
    decay = jnp.where(reset, 0.0, a)
    passed = sig_i * conv
    before = carry[0:1, :]
    states = scan_rows(decay, passed * factor, before, False)
    carry[0:1, :] = states[rows - 1 :, :]
    row = lax.broadcasted_iota(jnp.int32, states.shape, 0)
    prior = jnp.where(row == 0, before, pltpu.roll(states, 1, 0))
    low = states.astype(jnp.bfloat16).astype(jnp.float32)
    value, slope = gelu_parts(gelu_pre)
    by_core(low * value, merged_ref, core)
    product = dot_nn(merged_ref[...].reshape(rows, width), weights_ref[:, :model])
    middle_near_ref[...] = product[: rows // 2].astype(jnp.bfloat16)
    middle_far_ref[...] = product[rows // 2 :].astype(jnp.bfloat16)
    gelu_ref[...] = value
    gelu_grad_ref[...] = low * slope
    decay_ref[...] = decay
    input_ref[...] = passed * (1.0 - sig_i) * factor
    direct_ref[...] = sig_i * factor
    through_room = jnp.where(open_room > mult_floor, a * a * passed / root, 0.0)
    sig_grad = jnp.where(reset, 0.0, (prior * a - through_room) * sig_d)
    sig_ref[...] = sig_grad
    decay_grad_ref[...] = -8.0 * soft * (1.0 - sig_d) * sig_grad


def mix_forward(place, near, far, age, chan, pack, keep, got):
    chips, rows, model = near.shape
    planes, _, both = pack.shape
    width = both // 2
    length = 2 * chips * rows
    chunk = 2 * rows
    columns = keep.shape[1] * both // (width // (2 * chips))
    time_block = lambda i, s: (i, 0)
    token_block = lambda i, s: (0, i ^ (s[0] // 2), 0, 0)
    saved = lambda dtype: jax.ShapeDtypeStruct((length, width), dtype)
    spec = pl.BlockSpec((chunk, width), time_block)
    fixed = lambda shape: pl.BlockSpec(shape, lambda i, s: (0,) * len(shape))
    return pl.pallas_call(
        mix_forward_kernel,
        grid_spec=pltpu.PrefetchScalarGridSpec(
            num_scalar_prefetch=1,
            grid=(chips,),
            in_specs=[
                fixed(near.shape),
                fixed(far.shape),
                pl.BlockSpec((chunk, 1), time_block),
                pl.BlockSpec((chan.shape[0], width), lambda i, s: (0, s[0])),
                fixed((planes, model // planes, both)),
                fixed(keep.shape),
                fixed(got.shape),
            ],
            out_specs=[pl.BlockSpec((2, None, rows, width), token_block)]
            + [pl.BlockSpec((None, rows, model), lambda i, s: (i ^ (s[0] // 2), 0, 0))] * 2
            + [spec] * 9
            + [fixed((width, columns))],
            scratch_shapes=[
                pltpu.VMEM((chunk + 8, width), jnp.float32),
                pltpu.VMEM((8, width), jnp.float32),
            ],
        ),
        out_shape=[
            jax.ShapeDtypeStruct((2, chips, rows, width), jnp.bfloat16),
            jax.ShapeDtypeStruct(near.shape, jnp.bfloat16),
            jax.ShapeDtypeStruct(near.shape, jnp.bfloat16),
            saved(jnp.bfloat16),
            saved(jnp.bfloat16),
        ]
        + [saved(jnp.float32)] * 7
        + [jax.ShapeDtypeStruct((width, columns), jnp.bfloat16)],
        compiler_params=pltpu.CompilerParams(vmem_limit_bytes=56 * 1024 * 1024),
        name="mix_forward",
    )(place, near, far, age, chan, pack, keep, got)


def mix_backward_kernel(
    seq_ref,
    near_ref,
    far_ref,
    age_ref,
    chan_ref,
    weights_ref,
    in_ref,
    merged_ref,
    branch_ref,
    conv_ref,
    gelu_ref,
    gelu_grad_ref,
    decay_ref,
    input_ref,
    direct_ref,
    sig_ref,
    decay_grad_ref,
    both_ref,
    small_ref,
    back_near_ref,
    back_far_ref,
    *rest,
):
    place = seq_ref[0]
    chips = near_ref.shape[0]
    row_refs, (out_grad, gate_grads, ahead, carry) = rest[:chips], rest[chips:]
    step = pl.program_id(0)
    chip, core = place // 2, place % 2
    rows, width = branch_ref.shape
    model = near_ref.shape[-1]

    @pl.when(step == 0)
    def _():
        carry[...] = jnp.zeros_like(carry)
        ahead[:, pl.ds(rows, 8), :] = jnp.zeros((3, 8, width), jnp.float32)
        small_ref[...] = jnp.zeros_like(small_ref)
        gate_grads[...] = jnp.zeros_like(gate_grads)
        out_grad[...] = jnp.zeros_like(out_grad)

    @pl.when(step > 0)
    def _():
        ahead[:, pl.ds(rows, 8), :] = ahead[:, pl.ds(0, 8), :]

    turn = (chips - 1 - step) ^ chip
    mixer_grad = jnp.concatenate([near_ref[turn], far_ref[turn]], axis=0)
    merged_grad = in_time(dot_nt(mixer_grad, weights_ref[:, :model]), core)
    age = age_ref[...]
    out_grad[...] += dot_tn(mixer_grad, merged_ref[...].reshape(rows, width))
    state_grad = (merged_grad * gelu_ref[...]).astype(jnp.bfloat16).astype(jnp.float32)
    gelu_pre_grad = merged_grad * gelu_grad_ref[...]
    decay = decay_ref[...]
    conv_low = conv_ref[...]
    row = lax.broadcasted_iota(jnp.int32, (rows, width), 0)
    next_decay = jnp.where(row == rows - 1, carry[0:1, :], pltpu.roll(decay, rows - 1, 0))
    carried = scan_rows(next_decay, state_grad, carry[1:2, :], True)
    carry[0:1, :] = decay[0:1, :]
    carry[1:2, :] = carried[0:1, :]
    gate_conv_grad = carried * direct_ref[...]
    input_low = (carried * input_ref[...]).astype(jnp.bfloat16)
    decay_low = (carried * decay_grad_ref[...]).astype(jnp.bfloat16)
    sig_grad = carried * sig_ref[...]
    conv_grad = (
        gate_conv_grad
        + dot_nt(decay_low, weights_ref[:, model : model + width])
        + dot_nt(input_low, weights_ref[:, model + width :])
    )
    gate_grads[0] += dot_tn(decay_low, conv_low)
    gate_grads[1] += dot_tn(input_low, conv_low)
    branch = branch_ref[...].astype(jnp.float32)
    branch_grad = chan_ref[0:1, :] * conv_grad
    small_ref[0:1, :] += jnp.sum(conv_grad * branch, axis=0, keepdims=True)
    for k in range(1, 4):
        ahead[k - 1, pl.ds(0, rows), :] = conv_grad * jnp.where(age >= k, 1.0, 0.0)
        shifted = ahead[k - 1, pl.ds(k, rows), :]
        branch_grad = branch_grad + chan_ref[k : k + 1, :] * shifted
        small_ref[k : k + 1, :] += jnp.sum(shifted * branch, axis=0, keepdims=True)
    small_ref[4:5, :] += jnp.sum(conv_grad, axis=0, keepdims=True)
    small_ref[5:6, :] += jnp.sum(decay_low.astype(jnp.float32), axis=0, keepdims=True)
    small_ref[6:7, :] += jnp.sum(input_low.astype(jnp.float32), axis=0, keepdims=True)
    small_ref[7:8, :] += 8.0 * chan_ref[8:9, :] * jnp.sum(sig_grad, axis=0, keepdims=True)
    by_core(jnp.concatenate([branch_grad, gelu_pre_grad], axis=1), both_ref, core)
    both = both_ref[...].reshape(rows, 2 * width)
    back = dot_nt(both, in_ref[...].reshape(model, 2 * width)).astype(jnp.bfloat16)
    back_near_ref[...] = back[: rows // 2]
    back_far_ref[...] = back[rows // 2 :]

    @pl.when(step == chips - 1)
    def _():
        slim, piece = model // (2 * chips), width // (2 * chips)
        for k in range(chips):
            for e in range(2):
                target = 2 * (chip ^ k) + (core ^ e)
                rows = pl.ds(pl.multiple_of(target * slim, slim), slim)
                row_refs[k][e, pl.ds(0, slim), :] = out_grad[rows, :].astype(jnp.bfloat16)
                rows = pl.ds(pl.multiple_of(target * piece, piece), piece)
                for j in range(2):
                    row_refs[k][e, pl.ds(slim + j * piece, piece), :] = gate_grads[j, rows, :].astype(
                        jnp.bfloat16
                    )


def mix_backward(place, near, far, age, chan, weights, pack, merged, saved):
    planes, _, both = pack.shape
    chips, rows, model = near.shape
    width, columns = weights.shape
    tall = (model + 2 * width) // (2 * chips)
    chunk = 2 * rows
    last = chips - 1
    time_block = lambda i, s: (last - i, 0)
    token_block = lambda i, s: (0, (last - i) ^ (s[0] // 2), 0, 0)
    spec = pl.BlockSpec((chunk, width), time_block)
    back = pl.BlockSpec((None, rows, model), lambda i, s: ((last - i) ^ (s[0] // 2), 0, 0))
    fixed = lambda shape: pl.BlockSpec(shape, lambda i, s: (0,) * len(shape))
    return pl.pallas_call(
        mix_backward_kernel,
        grid_spec=pltpu.PrefetchScalarGridSpec(
            num_scalar_prefetch=1,
            grid=(chips,),
            in_specs=[
                fixed(near.shape),
                fixed(far.shape),
                pl.BlockSpec((chunk, 1), time_block),
                pl.BlockSpec((chan.shape[0], width), lambda i, s: (0, s[0])),
                fixed((width, columns)),
                fixed((planes, model // planes, both)),
                pl.BlockSpec((2, None, rows, width), token_block),
            ]
            + [spec] * 9,
            out_specs=[
                pl.BlockSpec((2, None, rows, 2 * width), token_block),
                fixed((8, width)),
                back,
                back,
            ]
            + [fixed((2, tall, width))] * chips,
            scratch_shapes=[
                pltpu.VMEM((model, width), jnp.float32),
                pltpu.VMEM((2, width, width), jnp.float32),
                pltpu.VMEM((3, chunk + 8, width), jnp.float32),
                pltpu.VMEM((8, width), jnp.float32),
            ],
        ),
        out_shape=[
            jax.ShapeDtypeStruct((2, chips, rows, 2 * width), jnp.bfloat16),
            jax.ShapeDtypeStruct((8, width), jnp.float32),
            jax.ShapeDtypeStruct(near.shape, jnp.bfloat16),
            jax.ShapeDtypeStruct(near.shape, jnp.bfloat16),
        ]
        + [jax.ShapeDtypeStruct((2, tall, width), jnp.bfloat16)] * chips,
        compiler_params=pltpu.CompilerParams(vmem_limit_bytes=50 * 1024 * 1024),
        cost_estimate=pl.CostEstimate(
            flops=10**9, bytes_accessed=24 * 10**6, transcendentals=0
        ),
        name="mix_backward",
    )(place, near, far, age, chan, weights, pack, merged, *saved)


def unit_kernel(
    near_ref,
    far_ref,
    cot_near_ref,
    cot_far_ref,
    pack_ref,
    back_near_out,
    back_far_out,
    mixed_near_out,
    mixed_far_out,
    grads_out,
    normed,
    cot,
    gate_up,
    down,
    pair,
    hidden,
    pair_t,
    hidden_t,
    grads,
    back,
    mixed,
    in_sems,
    out_sems,
):
    bf16 = jnp.bfloat16
    chips, rows, _ = near_ref.shape
    planes, tall, near_model = pack_ref.shape
    both = pair.shape[1]
    part = both // 2
    span = part // planes
    side = near_model // 2
    half = chips * rows
    incoming, outgoing = [], []

    def fetch(source, target):
        copy = pltpu.make_async_copy(source, target, in_sems.at[len(incoming)])
        copy.start()
        incoming.append(copy)
        return copy

    def send(source, target):
        copy = pltpu.make_async_copy(source, target, out_sems.at[len(outgoing)])
        copy.start()
        outgoing.append(copy)

    def fetch_half(source, target, i):
        return [
            fetch(source.at[k], target.at[pl.ds(i * half + k * rows, rows), :]) for k in range(chips)
        ]

    gate_up_copies = [
        fetch(
            pack_ref.at[z, pl.ds(j * near_model, near_model), :],
            gate_up.at[pl.ds(z * near_model, near_model), pl.ds(j * near_model, near_model)],
        )
        for z in range(planes)
        for j in range(3)
    ]
    normed_copies = [fetch_half(near_ref, normed, 0)]
    for copy in gate_up_copies + normed_copies[0]:
        copy.wait()
    down_copies = [
        fetch(
            pack_ref.at[z, pl.ds(3 * near_model + j * span, span), :],
            down.at[pl.ds(z * span, span), pl.ds(j * near_model, near_model)],
        )
        for z in range(planes)
        for j in range(planes)
    ]
    cot_copies = [fetch_half(cot_near_ref, cot, 0)]
    normed_copies.append(fetch_half(far_ref, normed, 1))
    cot_copies.append(fetch_half(cot_far_ref, cot, 1))
    chunk = 2 * rows
    first_unit, mid_unit, last_unit = (pl.ds(j * near_model, near_model) for j in range(3))
    for i in range(chips):
        here = pl.ds(i * chunk, chunk)
        if i * chunk == half:
            for copy in normed_copies[1] + cot_copies[1]:
                copy.wait()
        pre = dot_nn(normed[here, :], gate_up[...])
        if i == 0:
            for copy in down_copies + cot_copies[0]:
                copy.wait()
            down[pl.ds(part, side), :] = down[pl.ds(part - side, side), :]
        above = dot_nt(cot[here, :], down[...])
        up = pre[:, 2 * near_model :]
        value, slope = gelu_parts(pre[:, :near_model])
        grad = above[:, :near_model]
        hidden[here, first_unit] = (value * up).astype(bf16)
        pair[here, first_unit] = (grad * up * slope).astype(bf16)
        pair[here, last_unit] = (grad * value).astype(bf16)
        mid = pre[:, near_model : 2 * near_model]
        first = lax.broadcasted_iota(jnp.int32, mid.shape, 1) < side
        turned = pltpu.roll(mid, side, 1)
        gate, up = jnp.where(first, mid, turned), jnp.where(first, turned, mid)
        value, slope = gelu_parts(gate)
        grad = above[:, near_model:]
        hidden[here, pl.ds(near_model, side)] = (value * up)[:, :side].astype(bf16)
        pair[here, mid_unit] = jnp.where(first, grad * up * slope, grad * value).astype(bf16)
        pair_t[:, here] = pair[here, :].T
        hidden_t[:, here] = hidden[here, :].T
    def unit_rows(start):
        pieces, stop = [], start + span
        if start < near_model:
            pieces.append((2 * near_model + start, min(stop, near_model) - start))
        if stop > near_model:
            first = max(start, near_model)
            pieces.append((part + first - near_model, stop - first))
        return pieces

    for first_z in range(0, planes, 2):
        here = pl.ds(first_z * near_model, 2 * near_model)
        grad = dot_nn(hidden_t[...], cot[:, here]).astype(bf16)
        for z in (first_z, first_z + 1):
            columns = slice((z - first_z) * near_model, (z - first_z + 1) * near_model)
            for j in range(planes):
                grads[j, pl.ds((3 * z + 2) * span, span), :] = grad[
                    j * span : (j + 1) * span, columns
                ]
    for first_z in range(0, planes, 2):
        here = pl.ds(first_z * near_model, 2 * near_model)
        grad = dot_nn(pair_t[...], normed[:, here]).astype(bf16)
        for z in (first_z, first_z + 1):
            columns = slice((z - first_z) * near_model, (z - first_z + 1) * near_model)
            for j in range(planes):
                row = 3 * j * span
                grads[z, pl.ds(row, span), :] = grad[j * span : (j + 1) * span, columns]
                row += span
                for first, count in unit_rows(j * span):
                    grads[z, pl.ds(row, count), :] = grad[first : first + count, columns]
                    row += count
            send(grads.at[z], grads_out.at[z])
    for i, out in ((0, mixed_near_out), (1, mixed_far_out)):
        here = pl.ds(i * half, half)
        mixed[here, :] = dot_nn(hidden[here, :], down[pl.ds(0, part), :]).astype(bf16)
        for k in range(chips):
            send(mixed.at[pl.ds(i * half + k * rows, rows), :], out.at[k])
    for i, out in ((1, back_far_out), (0, back_near_out)):
        here = pl.ds(i * half, half)
        back[here, :] = dot_nt(pair[here, :], gate_up[...]).astype(bf16)
        for k in range(chips):
            send(back.at[pl.ds(i * half + k * rows, rows), :], out.at[k])
    for copy in outgoing:
        copy.wait()


def unit_back_and_forth(near, far, cot_near, cot_far, pack, part):
    chips, rows, model = near.shape
    length = 2 * chips * rows
    planes, _, near_model = pack.shape
    bf16 = jnp.bfloat16
    there = pl.BlockSpec(memory_space=pl.ANY)
    return pl.pallas_call(
        unit_kernel,
        in_specs=[there] * 5,
        out_specs=[there] * 5,
        scratch_shapes=[
            pltpu.VMEM((length, model), bf16),
            pltpu.VMEM((length, model), bf16),
            pltpu.VMEM((model, 2 * part), bf16),
            pltpu.VMEM((part + near_model // 2, model), bf16),
            pltpu.VMEM((length, 2 * part), bf16),
            pltpu.VMEM((length, part), bf16),
            pltpu.VMEM((2 * part, length), bf16),
            pltpu.VMEM((part, length), bf16),
            pltpu.VMEM(pack.shape, bf16),
            pltpu.VMEM((length, model), bf16),
            pltpu.VMEM((length, model), bf16),
            pltpu.SemaphoreType.DMA((4 * chips + planes * (3 + planes),)),
            pltpu.SemaphoreType.DMA((4 * chips + planes,)),
        ],
        out_shape=[jax.ShapeDtypeStruct(near.shape, bf16)] * 4
        + [jax.ShapeDtypeStruct(pack.shape, bf16)],
        compiler_params=pltpu.CompilerParams(vmem_limit_bytes=58 * 1024 * 1024),
        name="unit_back_and_forth",
    )(near, far, cot_near, cot_far, pack)


def mix_pack_kernel(place_ref, input_ref, gelu_ref, out_ref, decay_ref, gate_ref, pack_ref):
    near_model, width = input_ref.shape
    heads, piece, model = out_ref.shape
    pack_ref[pl.ds(0, near_model), pl.ds(0, width)] = input_ref[...]
    pack_ref[pl.ds(0, near_model), pl.ds(width, width)] = gelu_ref[...]
    row = near_model
    for h in range(heads):
        for j in range(model // (2 * width)):
            pack_ref[pl.ds(row, piece), :] = out_ref[h, :, pl.ds(j * 2 * width, 2 * width)]
            row += piece
        pack_ref[pl.ds(row, piece), pl.ds(0, width)] = decay_ref[h]
        pack_ref[pl.ds(row, piece), pl.ds(width, width)] = gate_ref[h]
        row += piece


def own_mix_pack(place, input_proj, gelu_proj, output_proj, decay_gate, input_gate):
    near_model, channels = input_proj.shape
    width = decay_gate.shape[1]
    heads = decay_gate.shape[0] // width
    model = output_proj.shape[1]
    piece = width // (channels // width)
    tall = near_model + heads * (model // (2 * width) + 1) * piece
    mine = pl.BlockSpec((near_model, width), lambda i, s: (0, s[0]))
    rows = lambda columns: pl.BlockSpec((heads, piece, columns), lambda i, s: (0, s[0], 0))
    return pl.pallas_call(
        mix_pack_kernel,
        grid_spec=pltpu.PrefetchScalarGridSpec(
            num_scalar_prefetch=1,
            grid=(1,),
            in_specs=[mine, mine, rows(model), rows(width), rows(width)],
            out_specs=pl.BlockSpec((tall, 2 * width), lambda i, s: (0, 0)),
        ),
        out_shape=jax.ShapeDtypeStruct((tall, 2 * width), input_proj.dtype),
        name="own_mix_pack",
    )(
        place,
        input_proj,
        gelu_proj,
        output_proj.reshape(heads, width, model),
        decay_gate.reshape(heads, width, width),
        input_gate.reshape(heads, width, width),
    )


def unit_pack_kernel(place_ref, gate_ref, up_ref, down_ref, pack_ref, windows, sems):
    place = place_ref[0]
    near_model, deep = gate_ref.shape
    planes = windows.shape[1]
    tile = 128
    span = (pack_ref.shape[0] - 3 * near_model) // planes
    extra = span - tile
    copies = []

    def fetch(source, target):
        copies.append(pltpu.make_async_copy(source, target, sems.at[len(copies)]))
        copies[-1].start()

    for i, ref in enumerate((gate_ref, up_ref)):
        for z in range(planes):
            start = pl.multiple_of(z * (deep // planes) + place * tile, tile)
            fetch(ref.at[:, pl.ds(start, 2 * tile)], windows.at[i, z])
    rows = pl.ds(pl.multiple_of(place * span, 16), span)
    for j in range(planes):
        fetch(
            down_ref.at[rows, pl.ds(j * near_model, near_model)],
            pack_ref.at[pl.ds(3 * near_model + j * span, span), :],
        )
    lane = lax.broadcasted_iota(jnp.int32, (near_model, tile), 1)

    def tiles(i):
        parts = []
        for z in range(planes):
            copies[i * planes + z].wait()
            turn = lax.rem((z - place) * extra + 2 * tile, 2 * tile)
            parts.append(pltpu.roll(windows[i, z].astype(jnp.float32), turn, 1))
        found = [parts[0][:, :tile]]
        for z in range(1, planes):
            found.append(jnp.where(lane < z * extra, parts[z - 1][:, tile:], parts[z][:, :tile]))
        return found + [parts[planes - 1][:, tile:]]

    gate, up = tiles(0), tiles(1)
    half = tile // 2
    turned = [pltpu.roll(up[j], half, 1) for j in (3, 4)]
    mid = [
        gate[3],
        jnp.where(lane < half, gate[4], turned[0]),
        jnp.where(lane < half, turned[0], turned[1]),
    ]
    for block, found in enumerate((gate[:3], mid, up[:3])):
        for j in range(3):
            pack_ref[pl.ds(block * near_model, near_model), pl.ds(j * tile, tile)] = found[
                j
            ].astype(pack_ref.dtype)
    for copy in copies[2 * planes :]:
        copy.wait()


def own_unit_pack(place, mlp_gate, mlp_up, mlp_down, planes, span):
    near_model = mlp_gate.shape[0]
    tall = 3 * near_model + planes * span
    there = pl.BlockSpec(memory_space=pl.ANY)
    return pl.pallas_call(
        unit_pack_kernel,
        grid_spec=pltpu.PrefetchScalarGridSpec(
            num_scalar_prefetch=1,
            grid=(1,),
            in_specs=[there] * 3,
            out_specs=pl.BlockSpec((tall, near_model), lambda i, s: (0, 0)),
            scratch_shapes=[
                pltpu.VMEM((2, planes, near_model, 256), mlp_gate.dtype),
                pltpu.SemaphoreType.DMA((3 * planes,)),
            ],
        ),
        out_shape=jax.ShapeDtypeStruct((tall, near_model), mlp_gate.dtype),
        compiler_params=pltpu.CompilerParams(vmem_limit_bytes=48 * 1024 * 1024),
        cost_estimate=pl.CostEstimate(flops=0, bytes_accessed=5 << 20, transcendentals=0),
        name="own_unit_pack",
    )(place, mlp_gate, mlp_up, mlp_down)


def in_grads_kernel(
    place_ref,
    near_ref,
    far_ref,
    both_ref,
    back_near_ref,
    back_far_ref,
    gain_ref,
    later_gain_ref,
    small_ref,
    grads_ref,
    sums_ref,
):
    place = place_ref[0]
    chips, rows, model = near_ref.shape
    planes, near_model, _ = grads_ref.shape
    taken, width = small_ref.shape
    near = near_ref[...].reshape(chips * rows, model)
    far = far_ref[...].reshape(chips * rows, model)
    for z in range(planes):
        here = slice(z * near_model, (z + 1) * near_model)
        total = dot_tn(near[:, here], both_ref[0].reshape(chips * rows, -1))
        total = total + dot_tn(far[:, here], both_ref[1].reshape(chips * rows, -1))
        grads_ref[z] = total.astype(grads_ref.dtype)
    gain_sum = jnp.zeros((1, model), jnp.float32)
    for ref, back_ref in ((near_ref, back_near_ref), (far_ref, back_far_ref)):
        for k in range(chips):
            product = ref[k].astype(jnp.float32) * back_ref[k].astype(jnp.float32)
            gain_sum = gain_sum + jnp.sum(product, axis=0, keepdims=True)
    sums_ref[...] = jnp.zeros_like(sums_ref)
    across = model // width
    row = pl.multiple_of(taken * (place // across), taken)
    column = pl.multiple_of(width * lax.rem(place, across), width)
    sums_ref[pl.ds(row, taken), pl.ds(column, width)] = small_ref[...]
    band = model // 3
    for j in range(3):
        here = slice(j * band, (j + 1) * band)
        sums_ref[pl.ds(taken + j, 1), pl.ds(band, band)] = gain_sum[:, here] / gain_ref[:, here]
        sums_ref[pl.ds(taken + 3 + j, 1), pl.ds(band, band)] = later_gain_ref[:, here]


def in_grads(place, near, far, both, back_near, back_far, gain, later_gain, small, planes):
    chips, rows, model = near.shape
    columns = both.shape[-1]
    whole = lambda shape: pl.BlockSpec(shape, lambda i, s: (0,) * len(shape))
    inputs = (near, far, both, back_near, back_far, gain[None], later_gain, small)
    shapes = [
        jax.ShapeDtypeStruct((planes, model // planes, columns), jnp.bfloat16),
        jax.ShapeDtypeStruct((16, model), jnp.float32),
    ]
    return pl.pallas_call(
        in_grads_kernel,
        grid_spec=pltpu.PrefetchScalarGridSpec(
            num_scalar_prefetch=1,
            grid=(1,),
            in_specs=[whole(x.shape) for x in inputs],
            out_specs=[whole(x.shape) for x in shapes],
        ),
        out_shape=shapes,
        compiler_params=pltpu.CompilerParams(vmem_limit_bytes=24 * 1024 * 1024),
        name="in_grads",
    )(place, *inputs)


def payload_kernel(*refs):
    near_ref, got_ref, *extra_refs = refs[: -near_count(refs)]
    own_ref, *out_refs = refs[-near_count(refs) :]
    chips, rows, _ = near_ref.shape
    for k in range(chips):
        total = near_ref[k].astype(jnp.float32) + got_ref[k].astype(jnp.float32)
        if k == 0:
            own_ref[...] = total
        else:
            out_refs[k - 1][pl.ds(0, rows), :] = total.astype(jnp.bfloat16)
            for ref in extra_refs:
                out_refs[k - 1][pl.ds(rows, ref.shape[0]), :] = ref[...]


def near_count(refs):
    return refs[0].shape[0]


def payloads(near, got, extra):
    chips, rows, model = near.shape
    tall = rows + extra.shape[0]
    whole = pl.BlockSpec(memory_space=pltpu.VMEM)
    inputs = (near, got) + ((extra,) if extra.shape[0] else ())
    return pl.pallas_call(
        payload_kernel,
        in_specs=[whole] * len(inputs),
        out_specs=[whole] * chips,
        out_shape=[jax.ShapeDtypeStruct((rows, model), jnp.float32)]
        + [jax.ShapeDtypeStruct((tall, model), jnp.bfloat16)] * (chips - 1),
        compiler_params=pltpu.CompilerParams(vmem_limit_bytes=20 * 1024 * 1024),
        cost_estimate=little,
        name="payloads",
    )(*inputs)


def middle_kernel(tokens_ref, gain_ref, *refs):
    *parts, middle_ref, normed_ref = refs
    total = tokens_ref[...].astype(jnp.float32)
    for ref in parts:
        total = total + ref[...].astype(jnp.float32)
    middle_ref[...] = total
    scale = lax.rsqrt(jnp.mean(total * total, axis=-1, keepdims=True) + norm_eps)
    normed_ref[...] = (total * scale * gain_ref[...]).astype(jnp.bfloat16)


def middle_and_normed(tokens, gain, parts):
    rows, model = tokens.shape
    whole = pl.BlockSpec(memory_space=pltpu.VMEM)
    return pl.pallas_call(
        middle_kernel,
        in_specs=[whole] * (2 + len(parts)),
        out_specs=[whole] * 2,
        out_shape=[
            jax.ShapeDtypeStruct((rows, model), jnp.float32),
            jax.ShapeDtypeStruct((rows, model), jnp.bfloat16),
        ],
        cost_estimate=little,
        name="middle_and_normed",
    )(tokens, gain[None], *parts)


def middle_back_kernel(cot_ref, middle_ref, gain_ref, *refs):
    *parts, grad_ref, low_ref, gain_grad_ref = refs
    middle, gain = middle_ref[...], gain_ref[...]
    upper = parts[0][...]
    for ref in parts[1:]:
        upper = upper + ref[...].astype(jnp.float32)
    scale = lax.rsqrt(jnp.mean(middle * middle, axis=-1, keepdims=True) + norm_eps)
    gain_grad_ref[...] = jnp.sum(upper * middle * scale, axis=0, keepdims=True)
    scaled = gain * upper
    inner = jnp.mean(scaled * middle, axis=-1, keepdims=True)
    grad = cot_ref[...].astype(jnp.float32) + scale * scaled - middle * (scale * scale * scale) * inner
    grad_ref[...] = grad
    low_ref[...] = grad.astype(jnp.bfloat16)


def middle_back(cotangent, middle, gain, parts):
    rows, model = middle.shape
    whole = pl.BlockSpec(memory_space=pltpu.VMEM)
    return pl.pallas_call(
        middle_back_kernel,
        in_specs=[whole] * (3 + len(parts)),
        out_specs=[whole] * 3,
        out_shape=[
            jax.ShapeDtypeStruct((rows, model), jnp.float32),
            jax.ShapeDtypeStruct((rows, model), jnp.bfloat16),
            jax.ShapeDtypeStruct((1, model), jnp.float32),
        ],
        cost_estimate=little,
        name="middle_back",
    )(cotangent, middle, gain[None], *parts)


def halves(value, wanted):
    side = value.shape[1] // 2
    return jnp.where(wanted == 1, pltpu.roll(value, side, 1), value)


def unit_give_kernel(place_ref, *refs):
    *piece_refs, give_ref = refs
    place = place_ref[0]
    chip, core = place // 2, place % 2
    turn = core ^ (chip // 2)
    span = piece_refs[0].shape[0] // 3
    for e in range(2):
        first, second = (piece_refs[i][pl.ds(0, 2 * span), :] for i in (e, 2 + e))
        give_ref[pl.ds(2 * e * span, 2 * span), :] = jnp.where(turn == 0, second, first)
    for e in range(2):
        first, second = (
            halves(piece_refs[2 * e + i][pl.ds(2 * span, span), :].astype(jnp.float32), 1 - core)
            for i in range(2)
        )
        side = first.shape[1] // 2
        lane = lax.broadcasted_iota(jnp.int32, first.shape, 1)
        give_ref[pl.ds((4 + e) * span, span), :] = jnp.where(
            lane < side, first, pltpu.roll(second, side, 1)
        ).astype(give_ref.dtype)


def unit_finish_kernel(place_ref, *refs):
    *piece_refs, got_ref, gate_ref, up_ref, down_ref, down = refs
    place = place_ref[0]
    chip, core = place // 2, place % 2
    turn = core ^ (chip // 2)
    span = piece_refs[0].shape[0] // 3
    side = piece_refs[0].shape[1] // 2
    for e in range(2):
        first, second = (piece_refs[i][pl.ds(0, 2 * span), :] for i in (e, 2 + e))
        mine = jnp.where(turn == 0, first, second).astype(jnp.float32)
        away = got_ref[pl.ds(2 * e * span, 2 * span), :].astype(jnp.float32)
        column = 2 * ((chip % 2) ^ e)
        for value, at in ((mine, column + core), (away, column + 1 - core)):
            rows = pl.ds(pl.multiple_of(at * span, span), span)
            gate_ref[rows, :] = value[:span]
            up_ref[rows, :] = value[span:]
    for k in range(4):
        mine = halves(piece_refs[k][pl.ds(2 * span, span), :].astype(jnp.float32), core)
        away = halves(got_ref[pl.ds((4 + k // 2) * span, span), :].astype(jnp.float32), k % 2)
        for value, at in ((mine, core), (away, 1 - core)):
            row = pl.multiple_of((2 * (chip ^ k) + at) * span, span)
            down[pl.ds(row, span), :] = value[:, :side]
    down_ref[...] = down[...].T


def unit_pieces(total, chip):
    chips = total.shape[0]
    pieces = [
        lax.dynamic_index_in_dim(total, chip ^ k, 0, keepdims=False) for k in range(chips)
    ]
    return [pieces[0]] + [chip_swap(pieces[k], k) for k in range(1, chips)]


def unit_exchange(place, pieces):
    chips = len(pieces)
    tall, cols = pieces[0].shape
    span = tall // 3
    fixed = lambda shape: pl.BlockSpec(shape, lambda i, s: (0,) * len(shape))
    give = pl.pallas_call(
        unit_give_kernel,
        grid_spec=pltpu.PrefetchScalarGridSpec(
            num_scalar_prefetch=1,
            grid=(1,),
            in_specs=[fixed((tall, cols))] * chips,
            out_specs=fixed((6 * span, cols)),
        ),
        out_shape=jax.ShapeDtypeStruct((6 * span, cols), pieces[0].dtype),
        name="unit_give",
    )(place, *pieces)
    shapes = [(4 * span, cols), (4 * span, cols), (cols // 2, 2 * chips * span)]
    grads = pl.pallas_call(
        unit_finish_kernel,
        grid_spec=pltpu.PrefetchScalarGridSpec(
            num_scalar_prefetch=1,
            grid=(1,),
            in_specs=[fixed((tall, cols))] * chips + [fixed((6 * span, cols))],
            out_specs=[fixed(shape) for shape in shapes],
            scratch_shapes=[pltpu.VMEM((2 * chips * span, cols // 2), jnp.float32)],
        ),
        out_shape=[jax.ShapeDtypeStruct(shape, jnp.float32) for shape in shapes],
        compiler_params=pltpu.CompilerParams(vmem_limit_bytes=32 * 1024 * 1024),
        name="unit_finish",
    )(place, *pieces, core_swap(give))
    return [grad.T for grad in grads]


def grad_pack_kernel(place_ref, in_ref, *refs):
    *blocks, pack_ref = refs
    place = place_ref[0]
    chips = len(blocks) // 2
    chip, core = place // 2, place % 2
    near_model, both = in_ref.shape[1:]
    tall, width = blocks[0].shape
    pack_ref[:, pl.ds(0, near_model), :] = in_ref[...]
    for k in range(chips):
        home, away = blocks[k][...], blocks[chips + k][...]
        odd = core == 1
        pack_ref[chip ^ k, pl.ds(near_model, tall), pl.ds(0, width)] = jnp.where(odd, away, home)
        pack_ref[chip ^ k, pl.ds(near_model, tall), pl.ds(width, width)] = jnp.where(odd, home, away)


def grad_pack(place, in_grad, home, away):
    planes, near_model, both = in_grad.shape
    tall, width = home[0].shape
    return pl.pallas_call(
        grad_pack_kernel,
        grid_spec=pltpu.PrefetchScalarGridSpec(
            num_scalar_prefetch=1,
            grid=(1,),
            in_specs=[pl.BlockSpec(in_grad.shape, lambda i, s: (0, 0, 0))]
            + [pl.BlockSpec((tall, width), lambda i, s: (0, 0))] * (2 * len(home)),
            out_specs=pl.BlockSpec((planes, near_model + tall, both), lambda i, s: (0, 0, 0)),
        ),
        out_shape=jax.ShapeDtypeStruct((planes, near_model + tall, both), jnp.bfloat16),
        compiler_params=pltpu.CompilerParams(vmem_limit_bytes=32 * 1024 * 1024),
        name="grad_pack",
    )(place, in_grad, *home, *away)


def mix_results_kernel(sum_ref, *refs):
    row = 0
    width = sum_ref.shape[1] // 2
    for j, ref in enumerate(refs):
        rows = ref.shape[0]
        if j < 2:
            ref[...] = sum_ref[pl.ds(0, rows), pl.ds(j * width, width)].astype(jnp.float32)
            row = rows
        else:
            ref[...] = sum_ref[pl.ds(row, rows), :].astype(jnp.float32)
            row += rows


def mix_results(total, near_model, slim):
    tall, both = total.shape
    piece = (tall - near_model - slim) // 2
    shapes = [(near_model, both // 2)] * 2 + [(slim, both), (piece, both), (piece, both)]
    whole = pl.BlockSpec(memory_space=pltpu.VMEM)
    found = pl.pallas_call(
        mix_results_kernel,
        in_specs=[whole],
        out_specs=[whole] * len(shapes),
        out_shape=[jax.ShapeDtypeStruct(shape, jnp.float32) for shape in shapes],
        name="mix_results",
    )(total)
    return [*found[:2], *[grad.T for grad in found[2:]]]


def norm_back(values, scale, gain, grad):
    inner = jnp.mean(gain * grad * values, axis=-1, keepdims=True)
    return scale * gain * grad - values * (scale * scale * scale) * inner


def narrow_shards(
    tokens,
    cotangent,
    doc_starts,
    mix_gain,
    input_proj,
    gelu_proj,
    conv_taps,
    conv_bias,
    decay_gate,
    decay_bias,
    input_gate,
    input_bias,
    decay_param,
    output_proj,
    mlp_gain,
    mlp_gate,
    mlp_up,
    mlp_down,
):
    f32, bf16 = jnp.float32, jnp.bfloat16
    devices, planes = lax.axis_size("seq"), lax.axis_size("fsdp")
    chips = devices // 2
    place = lax.axis_index("seq")
    chip, core = place // 2, place % 2
    rows, model = tokens.shape[1:]
    length = rows * devices
    channels = conv_taps.shape[1]
    width = decay_gate.shape[1]
    deep = mlp_gate.shape[1]
    heads = output_proj.shape[0] // width
    piece = width // devices
    span = deep // (planes * devices)
    part = deep // devices
    near_model = model // planes

    def along_fsdp(x):
        return lax.all_gather(x, "fsdp", axis=0, tiled=True)

    def columns(x, start, size):
        return lax.dynamic_slice_in_dim(x, start, size, axis=1)

    place_arg = place.astype(jnp.int32)[None]
    mix_pack, tokens = tie(
        own_mix_pack(place_arg, input_proj, gelu_proj, output_proj, decay_gate, input_gate), tokens
    )
    mix_pack = lax.all_gather(mix_pack, "fsdp", axis=0)

    values = tokens[0].astype(f32)
    scale1 = lax.rsqrt(jnp.mean(values * values, axis=-1, keepdims=True) + norm_eps)
    normed_own, mlp_gate, mlp_up, mlp_down = tie(
        (values * scale1 * mix_gain).astype(bf16), mlp_gate, mlp_up, mlp_down
    )
    normed_near, normed_far = gather_blocks(normed_own)
    unit_pack = own_unit_pack(place_arg, mlp_gate, mlp_up, mlp_down, planes, span)
    unit_pack, normed_near, normed_far = tie(unit_pack, normed_near, normed_far)
    unit_pack = lax.all_gather(unit_pack, "fsdp", axis=0)
    mix_pack, normed_near, normed_far = tie(mix_pack, normed_near, normed_far)

    positions = jnp.arange(length, dtype=jnp.int32)
    starts = doc_starts[0]
    begin = jnp.max(jnp.where(starts[None, :] <= positions[:, None], starts[None, :], 0), axis=1)
    age = (positions - begin).astype(f32)[:, None]
    chan = jnp.concatenate(
        [
            conv_taps,
            conv_bias[None],
            decay_bias[None],
            input_bias[None],
            jax.nn.softplus(-decay_param)[None],
            jax.nn.sigmoid(-decay_param)[None],
            jnp.zeros((7, channels), f32),
        ],
        axis=0,
    )

    keep, got = exchange(mix_pack[:, near_model:].reshape(chips, 2, -1, 2 * width), chip, core, 0)
    keep, got, out_grad = tie(keep, got, cotangent[0])
    cot_got = [chip_swap(out_grad, k) for k in range(1, chips)]
    merged, middle_near, middle_far, *saved, weights = mix_forward(
        place_arg, normed_near, normed_far, age, chan, mix_pack, keep, got
    )
    middle_near, middle_far, *cot_got = tie(middle_near, middle_far, *cot_got)
    cot_near = jnp.stack([out_grad, *cot_got])
    cot_far = core_swap(cot_near)
    middle, normed2 = middle_and_normed(
        tokens[0], mlp_gain, spread_pairs(*pair_blocks(middle_near, middle_far))
    )

    near, far = gather_blocks(normed2)
    back_near, back_far, mixed_near, mixed_far, unit_grads = unit_back_and_forth(
        near, far, cot_near, cot_far, unit_pack, part
    )
    unit_sum = lax.psum_scatter(unit_grads, "fsdp", scatter_dimension=0, tiled=False)

    middle_grad, middle_low, mlp_gain_term = middle_back(
        out_grad, middle, mlp_gain, spread_pairs(*pair_blocks(back_near, back_far))
    )
    middle_low, mixed_near, mixed_far = tie(middle_low, mixed_near, mixed_far)
    mixed_own, *mixed_low = pair_blocks(mixed_near, mixed_far)
    first, *others = [chip_swap(middle_low, k) for k in range(1, chips)]
    first, mixed_own, *mixed_low = tie(first, mixed_own, *mixed_low)
    near = jnp.stack([middle_low, first, *others])
    far = core_swap(near)

    both, small, back_near, back_far, *by_chip = mix_backward(
        place_arg, near, far, age, chan, weights, mix_pack, merged, saved
    )
    mixed_got = [chip_swap(block, k + 1) for k, block in enumerate(mixed_low)]
    held = tie(*mixed_got, *by_chip)
    mixed_got, by_chip = held[: chips - 1], held[chips - 1 :]
    arrived = [by_chip[0]] + [chip_swap(by_chip[k], k) for k in range(1, chips)]
    arrived[1], both, back_near, back_far, small = tie(
        arrived[1], both, back_near, back_far, small
    )
    in_pack, sums = in_grads(
        place_arg,
        normed_near,
        normed_far,
        both,
        back_near,
        back_far,
        mix_gain,
        mlp_gain_term,
        small,
        planes,
    )
    sums = sums + core_swap(sums)
    *arrived, back_near, back_far = tie(*arrived, back_near, back_far)
    normed_own, *normed_low = pair_blocks(back_near, back_far)
    away = core_swap(jnp.stack([block[1] for block in arrived]))
    held = tie(
        grad_pack(
            place_arg,
            in_pack,
            [block[0] for block in arrived],
            [away[k] for k in range(chips)],
        ),
        unit_sum,
        sums,
        normed_own,
        *normed_low,
        *mixed_got,
    )
    pack, unit_sum, sums, normed_own = held[:4]
    normed_low, mixed_got = held[4 : 3 + chips], held[3 + chips :]
    mixed = mixed_own
    for got in mixed_got:
        mixed = mixed + got.astype(f32)
    mixed = (middle + mixed).astype(bf16)
    mix_sum = lax.psum_scatter(pack, "fsdp", scatter_dimension=0, tiled=False)
    (
        input_proj_grad,
        gelu_proj_grad,
        output_proj_grad,
        decay_gate_grad,
        input_gate_grad,
    ) = mix_results(mix_sum, near_model, model // devices)

    pieces = unit_pieces(unit_sum.reshape(planes, 3 * span, near_model), chip)
    pieces[1], *normed_low = tie(pieces[1], *normed_low)
    normed_grad = normed_own
    for k in range(1, chips):
        normed_grad = normed_grad + chip_swap(normed_low[k - 1], k).astype(f32)
    values_part = norm_back(values, scale1, mix_gain, normed_grad)
    tokens_grad = (middle_grad + values_part).astype(bf16)

    low = sums.astype(bf16)
    for k in range(1, chips):
        sums = sums + chip_swap(low, k).astype(f32)
    sums, *pieces = tie(over_planes(sums), *pieces)
    channel_sums = jnp.concatenate([sums[:8], sums[8:, : channels - model]], axis=1)
    band = model // 3
    gain_sums = sums[8:14, band : 2 * band].reshape(2, model)
    mlp_gate_grad, mlp_up_grad, mlp_down_grad = unit_exchange(place_arg, pieces)

    return (
        mixed[None],
        tokens_grad[None],
        gain_sums[0],
        input_proj_grad,
        gelu_proj_grad,
        channel_sums[:4],
        channel_sums[4],
        decay_gate_grad,
        channel_sums[5],
        input_gate_grad,
        channel_sums[6],
        channel_sums[7],
        output_proj_grad,
        gain_sums[1],
        mlp_gate_grad,
        mlp_up_grad,
        mlp_down_grad,
    )


def choose_plan(mesh):
    devices, planes = mesh.shape["seq"], mesh.shape["fsdp"]

    def plan(*args):
        channels, width = args[6].shape[1], args[8].shape[1]
        if channels == width * devices and devices == 2 * planes and planes == 4:
            return narrow_shards(*args)
        return wide_shards(*args)

    return plan


def solution(mesh):
    return jax.shard_map(
        choose_plan(mesh),
        mesh=mesh,
        in_specs=(
            P("fsdp", "seq", None),
            P("fsdp", "seq", None),
            P("fsdp", None),
            P(),
            P("fsdp", None),
            P("fsdp", None),
            P(),
            P(),
            P("fsdp", None),
            P(),
            P("fsdp", None),
            P(),
            P(),
            P("fsdp", None),
            P(),
            P("fsdp", None),
            P("fsdp", None),
            P("fsdp", None),
        ),
        out_specs=(
            P("fsdp", "seq", None),
            P("fsdp", "seq", None),
            P(),
            P("fsdp", "seq"),
            P("fsdp", "seq"),
            P(),
            P(),
            P("fsdp", "seq"),
            P(),
            P("fsdp", "seq"),
            P(),
            P(),
            P("fsdp", "seq"),
            P(),
            P("fsdp", "seq"),
            P("fsdp", "seq"),
            P("fsdp", "seq"),
        ),
        check_vma=False,
    )
```

```python
import functools

import jax
import jax.numpy as jnp
from jax import lax
from jax.experimental import pallas as pl
from jax.experimental.pallas import tpu as pltpu
from jax.sharding import PartitionSpec as P

norm_eps = 1e-06
mult_floor = 0.0001


def from_behind(x, axis, by):
    devices = lax.axis_size(axis)
    pairs = [(i, i + by) for i in range(devices) if 0 <= i + by < devices]
    return lax.ppermute(x, axis, pairs)


def rms_scale(values, gain):
    scale = lax.rsqrt(jnp.mean(values * values, axis=-1, keepdims=True) + norm_eps)
    return values * scale * gain


def smooth_gelu(values):
    return jax.nn.gelu(values, approximate=True)


def gated_unit(gate, up_val):
    return smooth_gelu(gate) * up_val


def affine_pair(earlier, later):
    return (earlier[0] * later[0], earlier[1] * later[0] + later[1])


def decay_terms(conv_out, decay_pre, input_pre, decay_param, resets):
    log_a = -8.0 * jax.nn.sigmoid(decay_pre) * jax.nn.softplus(-decay_param)
    room = jnp.maximum(-jnp.expm1(2.0 * log_a), mult_floor)
    factor = jnp.where(resets, 1.0, jnp.sqrt(room))
    decay = jnp.where(resets, 0.0, jnp.exp(log_a))
    return (decay, jax.nn.sigmoid(input_pre) * conv_out * factor)


def conv_apply(extended, taps_w, bias, masks):
    taps = taps_w.shape[0]
    rows = masks.shape[1]
    total = jnp.zeros((rows, taps_w.shape[1]), jnp.float32) + bias
    for shift_k in range(taps):
        begin_row = taps - 1 - shift_k
        total = total + taps_w[shift_k] * extended[begin_row : begin_row + rows] * masks[shift_k]
    return total


def block_product(left, weight):
    width = weight.shape[1]
    blocks = weight.shape[0] // width
    result = jnp.einsum(
        "nhk,hkj->nhj",
        left.reshape(left.shape[0], blocks, width),
        weight.reshape(blocks, width, width),
        preferred_element_type=jnp.float32,
    )
    return result.reshape(left.shape[0], -1)


def block_back(grad, weight):
    width = weight.shape[1]
    blocks = weight.shape[0] // width
    result = jnp.einsum(
        "nhj,hkj->nhk",
        grad.reshape(grad.shape[0], blocks, width),
        weight.reshape(blocks, width, width),
        preferred_element_type=jnp.float32,
    )
    return result.reshape(grad.shape[0], -1)


def block_weight_grad(left, grad, width):
    blocks = left.shape[1] // width
    result = jnp.einsum(
        "nhk,nhj->hkj",
        left.reshape(left.shape[0], blocks, width),
        grad.reshape(grad.shape[0], blocks, width),
        preferred_element_type=jnp.float32,
    )
    return result.reshape(blocks * width, width)


def wide_shards(
    tokens,
    cotangent,
    doc_starts,
    mix_gain,
    input_proj,
    gelu_proj,
    conv_taps,
    conv_bias,
    decay_gate,
    decay_bias,
    input_gate,
    input_bias,
    decay_param,
    output_proj,
    mlp_gain,
    mlp_gate,
    mlp_up,
    mlp_down,
):
    rows = tokens.shape[1]
    taps = conv_taps.shape[0]
    width = decay_gate.shape[1]
    input_w, gelu_w, output_w, decay_w, inputg_w, gate_w, up_w, down_w = (
        lax.all_gather(input_proj, "fsdp", axis=0, tiled=True),
        lax.all_gather(gelu_proj, "fsdp", axis=0, tiled=True),
        lax.all_gather(output_proj, "fsdp", axis=0, tiled=True),
        lax.all_gather(decay_gate, "fsdp", axis=0, tiled=True),
        lax.all_gather(input_gate, "fsdp", axis=0, tiled=True),
        lax.all_gather(mlp_gate, "fsdp", axis=0, tiled=True),
        lax.all_gather(mlp_up, "fsdp", axis=0, tiled=True),
        lax.all_gather(mlp_down, "fsdp", axis=0, tiled=True),
    )
    channels = input_w.shape[1]
    first = lax.axis_index("seq") * rows
    positions = first + jnp.arange(rows, dtype=jnp.int32)
    starts = doc_starts[0]
    begin = jnp.max(jnp.where(starts[None, :] <= positions[:, None], starts[None, :], 0), axis=1)
    resets = (begin == positions)[:, None]
    masks = jnp.stack([(positions - k >= begin)[:, None] for k in range(taps)]).astype(jnp.float32)
    values = tokens[0].astype(jnp.float32)
    normed = rms_scale(values, mix_gain).astype(jnp.bfloat16)
    branch = jnp.dot(normed, input_w, preferred_element_type=jnp.float32).astype(jnp.bfloat16)
    gelu_pre = jnp.dot(normed, gelu_w, preferred_element_type=jnp.float32)
    gelu_out = smooth_gelu(gelu_pre)
    previous = from_behind(branch[rows - (taps - 1) :], "seq", 1)
    extended = jnp.concatenate([previous, branch], axis=0).astype(jnp.float32)
    conv_f = conv_apply(extended, conv_taps, conv_bias, masks).astype(jnp.bfloat16)
    conv_val = conv_f.astype(jnp.float32)
    decay_pre = block_product(conv_f, decay_w) + decay_bias
    input_pre = block_product(conv_f, inputg_w) + input_bias
    decay, driven = decay_terms(conv_val, decay_pre, input_pre, decay_param, resets)
    decay_cols, driven_cols = (
        lax.all_to_all(decay, "seq", split_axis=1, concat_axis=0, tiled=True),
        lax.all_to_all(driven, "seq", split_axis=1, concat_axis=0, tiled=True),
    )
    states_cols = lax.associative_scan(affine_pair, (decay_cols, driven_cols), axis=0)[1]
    states_low = lax.all_to_all(
        states_cols.astype(jnp.bfloat16), "seq", split_axis=0, concat_axis=1, tiled=True
    )
    states_val = states_low.astype(jnp.float32)
    merged = (states_val * gelu_out).astype(jnp.bfloat16)
    middle = values + jnp.dot(merged, output_w, preferred_element_type=jnp.float32)
    normed2 = rms_scale(middle, mlp_gain).astype(jnp.bfloat16)
    gate = jnp.dot(normed2, gate_w, preferred_element_type=jnp.float32)
    up_val = jnp.dot(normed2, up_w, preferred_element_type=jnp.float32)
    hidden = gated_unit(gate, up_val).astype(jnp.bfloat16)
    mixed = (middle + jnp.dot(hidden, down_w, preferred_element_type=jnp.float32)).astype(
        jnp.bfloat16
    )
    out_grad = cotangent[0]
    down_grad = jnp.einsum("tf,td->fd", hidden, out_grad, preferred_element_type=jnp.float32)
    hidden_grad = jnp.einsum("td,fd->tf", out_grad, down_w, preferred_element_type=jnp.float32)
    unit_pull = jax.vjp(gated_unit, gate, up_val)[1]
    gate_grad, up_grad = unit_pull(hidden_grad)
    gate_low = gate_grad.astype(jnp.bfloat16)
    up_low = up_grad.astype(jnp.bfloat16)
    gate_w_grad = jnp.einsum("td,tf->df", normed2, gate_low, preferred_element_type=jnp.float32)
    up_w_grad = jnp.einsum("td,tf->df", normed2, up_low, preferred_element_type=jnp.float32)
    mlp_terms = (
        lax.psum_scatter(gate_w_grad, "seq", scatter_dimension=1, tiled=True),
        lax.psum_scatter(up_w_grad, "seq", scatter_dimension=1, tiled=True),
        lax.psum_scatter(down_grad, "seq", scatter_dimension=1, tiled=True),
    )
    mlp_gate_grad, mlp_up_grad, mlp_down_grad = (
        lax.psum_scatter(mlp_terms[0], "fsdp", scatter_dimension=0, tiled=True),
        lax.psum_scatter(mlp_terms[1], "fsdp", scatter_dimension=0, tiled=True),
        lax.psum_scatter(mlp_terms[2], "fsdp", scatter_dimension=0, tiled=True),
    )
    normed2_grad = jnp.einsum(
        "tf,df->td", gate_low, gate_w, preferred_element_type=jnp.float32
    ) + jnp.einsum("tf,df->td", up_low, up_w, preferred_element_type=jnp.float32)
    norm2_pull = jax.vjp(rms_scale, middle, mlp_gain)[1]
    middle_part, mlp_gain_term = norm2_pull(normed2_grad)
    middle_grad = out_grad.astype(jnp.float32) + middle_part
    mixer_grad = middle_grad.astype(jnp.bfloat16)
    output_w_grad = jnp.einsum("tr,td->rd", merged, mixer_grad, preferred_element_type=jnp.float32)
    merged_grad = jnp.einsum("td,rd->tr", mixer_grad, output_w, preferred_element_type=jnp.float32)
    state_low = (merged_grad * gelu_out).astype(jnp.bfloat16)
    gelu_pull = jax.vjp(smooth_gelu, gelu_pre)[1]
    gelu_pre_low = gelu_pull(merged_grad * states_val)[0].astype(jnp.bfloat16)
    grad_cols = lax.all_to_all(state_low, "seq", split_axis=1, concat_axis=0, tiled=True).astype(
        jnp.float32
    )
    width_cols = grad_cols.shape[1]
    next_decay = jnp.concatenate([decay_cols[1:], jnp.zeros((1, width_cols), jnp.float32)], axis=0)
    carried = lax.associative_scan(affine_pair, (next_decay, grad_cols), reverse=True, axis=0)[1]
    prior = jnp.concatenate([jnp.zeros((1, width_cols), jnp.float32), states_cols[:-1]], axis=0)
    decay_grad, driven_grad = (
        lax.all_to_all(carried * prior, "seq", split_axis=0, concat_axis=1, tiled=True),
        lax.all_to_all(carried, "seq", split_axis=0, concat_axis=1, tiled=True),
    )
    terms_pull = jax.vjp(
        lambda conv_in, dpre, ipre, dparam: decay_terms(conv_in, dpre, ipre, dparam, resets),
        conv_val,
        decay_pre,
        input_pre,
        decay_param,
    )[1]
    gate_conv_grad, dpre_grad, ipre_grad, decay_param_term = terms_pull((decay_grad, driven_grad))
    dpre_low = dpre_grad.astype(jnp.bfloat16)
    ipre_low = ipre_grad.astype(jnp.bfloat16)
    decay_w_grad = block_weight_grad(conv_f, dpre_low, width)
    inputg_w_grad = block_weight_grad(conv_f, ipre_low, width)
    conv_grad = gate_conv_grad + block_back(dpre_low, decay_w) + block_back(ipre_low, inputg_w)
    conv_pull = jax.vjp(
        lambda ext, taps_w, bias: conv_apply(ext, taps_w, bias, masks),
        extended,
        conv_taps,
        conv_bias,
    )[1]
    extended_grad, taps_term, conv_bias_term = conv_pull(conv_grad)
    returned = from_behind(extended_grad[: taps - 1], "seq", -1)
    branch_grad = extended_grad[taps - 1 :] + jnp.concatenate(
        [jnp.zeros((rows - (taps - 1), channels), jnp.float32), returned], axis=0
    )
    branch_low = branch_grad.astype(jnp.bfloat16)
    input_w_grad = jnp.einsum("td,tr->dr", normed, branch_low, preferred_element_type=jnp.float32)
    gelu_w_grad = jnp.einsum("td,tr->dr", normed, gelu_pre_low, preferred_element_type=jnp.float32)
    mix_terms = (
        lax.psum_scatter(input_w_grad, "seq", scatter_dimension=1, tiled=True),
        lax.psum_scatter(gelu_w_grad, "seq", scatter_dimension=1, tiled=True),
        lax.psum_scatter(output_w_grad, "seq", scatter_dimension=1, tiled=True),
        lax.psum_scatter(decay_w_grad, "seq", scatter_dimension=1, tiled=True),
        lax.psum_scatter(inputg_w_grad, "seq", scatter_dimension=1, tiled=True),
    )
    input_proj_grad, gelu_proj_grad, output_proj_grad, decay_gate_grad, input_gate_grad = (
        lax.psum_scatter(mix_terms[0], "fsdp", scatter_dimension=0, tiled=True),
        lax.psum_scatter(mix_terms[1], "fsdp", scatter_dimension=0, tiled=True),
        lax.psum_scatter(mix_terms[2], "fsdp", scatter_dimension=0, tiled=True),
        lax.psum_scatter(mix_terms[3], "fsdp", scatter_dimension=0, tiled=True),
        lax.psum_scatter(mix_terms[4], "fsdp", scatter_dimension=0, tiled=True),
    )
    normed_grad = jnp.einsum(
        "tr,dr->td", branch_low, input_w, preferred_element_type=jnp.float32
    ) + jnp.einsum("tr,dr->td", gelu_pre_low, gelu_w, preferred_element_type=jnp.float32)
    norm1_pull = jax.vjp(rms_scale, values, mix_gain)[1]
    values_part, mix_gain_term = norm1_pull(normed_grad)
    tokens_grad = (middle_grad + values_part).astype(jnp.bfloat16)
    (
        mix_gain_grad,
        conv_taps_grad,
        conv_bias_grad,
        decay_bias_grad,
        input_bias_grad,
        decay_param_grad,
        mlp_gain_grad,
    ) = lax.psum(
        (
            mix_gain_term,
            taps_term,
            conv_bias_term,
            jnp.sum(dpre_low.astype(jnp.float32), axis=0),
            jnp.sum(ipre_low.astype(jnp.float32), axis=0),
            decay_param_term,
            mlp_gain_term,
        ),
        ("seq", "fsdp"),
    )
    return (
        mixed[None],
        tokens_grad[None],
        mix_gain_grad,
        input_proj_grad,
        gelu_proj_grad,
        conv_taps_grad,
        conv_bias_grad,
        decay_gate_grad,
        decay_bias_grad,
        input_gate_grad,
        input_bias_grad,
        decay_param_grad,
        output_proj_grad,
        mlp_gain_grad,
        mlp_gate_grad,
        mlp_up_grad,
        mlp_down_grad,
    )


def chip_swap(x, k):
    devices = lax.axis_size("seq")
    return lax.ppermute(x, "seq", [(i, i ^ (2 * k)) for i in range(devices)])


def core_swap(x):
    devices = lax.axis_size("seq")
    return lax.ppermute(x, "seq", [(i, i ^ 1) for i in range(devices)])


def gather_blocks(x):
    chips = lax.axis_size("seq") // 2
    near = jnp.stack([x] + [chip_swap(x, k) for k in range(1, chips)])
    return near, core_swap(near)


def tie(*arrays):
    return lax.optimization_barrier(arrays)


def pair_blocks(near, far, extra=None):
    if extra is None:
        extra = jnp.zeros((0, near.shape[2]), jnp.bfloat16)
    return payloads(near, core_swap(far), extra)


def spread_pairs(own, *low):
    return own, *[chip_swap(block, k + 1) for k, block in enumerate(low)]


def plane_swap(x, k):
    if k == 0:
        return x
    return lax.ppermute(x, "fsdp", [(i, i ^ k) for i in range(lax.axis_size("fsdp"))])


def exchange(x, chip, core, turn, beside):
    chips = x.shape[0]
    parts = [
        lax.dynamic_index_in_dim(x, chip ^ k ^ turn, 0, keepdims=False) for k in range(chips)
    ]
    got = [chip_swap(parts[k], k) for k in range(1, chips)]
    got[0], *beside = tie(got[0], *beside)
    got = jnp.stack([parts[0], *got])
    keep = lax.dynamic_index_in_dim(got, core, 1, keepdims=False)
    give = lax.dynamic_index_in_dim(got, 1 - core, 1, keepdims=False)
    return keep, core_swap(give), *beside


def over_planes(x):
    planes = lax.axis_size("fsdp")
    total = x
    for k in range(1, planes):
        got = lax.ppermute(x.astype(jnp.bfloat16), "fsdp", [(i, i ^ k) for i in range(planes)])
        total = total + got.astype(jnp.float32)
    return total


little = pl.CostEstimate(flops=0, bytes_accessed=0, transcendentals=0)


def gelu_parts(v):
    root = 0.7978845608028654
    square = v * v
    h = 0.5 + 0.5 * jnp.tanh(v * (root + root * 0.044715 * square))
    value = v * h
    return value, h + value * (1.0 - h) * (2.0 * root + root * 0.26829 * square)


def sigmoid(v):
    return 1.0 / (1.0 + jnp.exp(-v))


def one_less_exp(v):
    series = -v * (1.0 + v * (0.5 + v * (1.0 / 6.0 + v * (1.0 / 24.0 + v * (1.0 / 120.0)))))
    return jnp.where(v > -0.1, series, 1.0 - jnp.exp(v))


def dot_nn(a, b):
    return lax.dot_general(a, b, (((1,), (0,)), ((), ())), preferred_element_type=jnp.float32)


def dot_nt(a, b):
    return lax.dot_general(a, b, (((1,), (1,)), ((), ())), preferred_element_type=jnp.float32)


def dot_tn(a, b):
    return lax.dot_general(a, b, (((0,), (0,)), ((), ())), preferred_element_type=jnp.float32)


def scan_rows(a, b, carry, later):
    rows = a.shape[0]
    group = 8
    row = lax.broadcasted_iota(jnp.int32, a.shape, 0) % group
    step = 1
    while step < group:
        turn = rows - step if later else step
        there = (row < group - step) if later else (row >= step)
        a_next = jnp.where(there, pltpu.roll(a, turn, 0), 1.0)
        b_next = jnp.where(there, pltpu.roll(b, turn, 0), 0.0)
        b = a * b_next + b
        a = a * a_next
        step *= 2
    starts = list(range(0, rows, group))
    done = {}
    for start in reversed(starts) if later else starts:
        states = a[start : start + group] * carry + b[start : start + group]
        done[start] = states
        carry = states[:1] if later else states[group - 1 :]
    return jnp.concatenate([done[start] for start in starts], axis=0)


def in_time(value, core):
    rows = value.shape[0] // 2
    near, far = value[:rows], value[rows:]
    odd = core == 1
    return jnp.concatenate([jnp.where(odd, far, near), jnp.where(odd, near, far)], axis=0)


def by_core(value, ref, core):
    rows = value.shape[0] // 2
    first, second = value[:rows], value[rows:]
    odd = core == 1
    ref[0] = jnp.where(odd, second, first).astype(ref.dtype)
    ref[1] = jnp.where(odd, first, second).astype(ref.dtype)


def mix_forward_kernel(
    seq_ref,
    near_ref,
    far_ref,
    age_ref,
    chan_ref,
    keep_ref,
    got_ref,
    merged_ref,
    middle_near_ref,
    middle_far_ref,
    branch_ref,
    conv_ref,
    gelu_ref,
    gelu_grad_ref,
    decay_ref,
    input_ref,
    direct_ref,
    sig_ref,
    decay_grad_ref,
    weights_ref,
    extended,
    carry,
):
    place = seq_ref[0]
    chips = keep_ref.shape[0]
    step = pl.program_id(0)
    chip, core = place // 2, place % 2
    rows, width = branch_ref.shape
    model = middle_near_ref.shape[1]
    piece = keep_ref.shape[1]

    @pl.when(step == 0)
    def _():
        extended[pl.ds(0, 8), :] = jnp.zeros((8, width), jnp.float32)
        carry[...] = jnp.zeros_like(carry)
        for k in range(chips):
            home = pl.multiple_of(piece * 2 * (chip ^ k) + piece * core, piece)
            away = pl.multiple_of(piece * 2 * (chip ^ k) + piece * (1 - core), piece)
            weights_ref[pl.ds(home, piece), :] = keep_ref[k]
            weights_ref[pl.ds(away, piece), :] = got_ref[k]

    @pl.when(step > 0)
    def _():
        extended[pl.ds(0, 8), :] = extended[pl.ds(rows, 8), :]

    pre = in_time(jnp.concatenate([near_ref[...], far_ref[...]], axis=0), core)
    branch = pre[:, :width].astype(jnp.bfloat16)
    gelu_pre = pre[:, width:]
    branch_ref[...] = branch
    extended[pl.ds(8, rows), :] = branch.astype(jnp.float32)
    age = age_ref[...]
    total = jnp.zeros((rows, width), jnp.float32) + chan_ref[4:5, :]
    for k in range(4):
        shifted = extended[pl.ds(8 - k, rows), :]
        total = total + chan_ref[k : k + 1, :] * shifted * jnp.where(age >= k, 1.0, 0.0)
    conv_low = total.astype(jnp.bfloat16)
    conv = conv_low.astype(jnp.float32)
    conv_ref[...] = conv_low
    decay_pre = dot_nn(conv_low, weights_ref[:, model : model + width]) + chan_ref[5:6, :]
    input_pre = dot_nn(conv_low, weights_ref[:, model + width :]) + chan_ref[6:7, :]
    sig_d, sig_i = sigmoid(decay_pre), sigmoid(input_pre)
    soft = chan_ref[7:8, :]
    log_a = -8.0 * sig_d * soft
    reset = age < 0.5
    open_room = one_less_exp(2.0 * log_a)
    root = jnp.sqrt(jnp.maximum(open_room, mult_floor))
    factor = jnp.where(reset, 1.0, root)
    a = jnp.exp(log_a)
    decay = jnp.where(reset, 0.0, a)
    passed = sig_i * conv
    before = carry[0:1, :]
    states = scan_rows(decay, passed * factor, before, False)
    carry[0:1, :] = states[rows - 1 :, :]
    row = lax.broadcasted_iota(jnp.int32, states.shape, 0)
    prior = jnp.where(row == 0, before, pltpu.roll(states, 1, 0))
    low = states.astype(jnp.bfloat16).astype(jnp.float32)
    value, slope = gelu_parts(gelu_pre)
    by_core(low * value, merged_ref, core)
    product = dot_nn(merged_ref[...].reshape(rows, width), weights_ref[:, :model])
    middle_near_ref[...] = product[: rows // 2].astype(jnp.bfloat16)
    middle_far_ref[...] = product[rows // 2 :].astype(jnp.bfloat16)
    gelu_ref[...] = value
    gelu_grad_ref[...] = low * slope
    decay_ref[...] = decay
    input_ref[...] = passed * (1.0 - sig_i) * factor
    direct_ref[...] = sig_i * factor
    through_room = jnp.where(open_room > mult_floor, a * a * passed / root, 0.0)
    sig_grad = jnp.where(reset, 0.0, (prior * a - through_room) * sig_d)
    sig_ref[...] = sig_grad
    decay_grad_ref[...] = -8.0 * soft * (1.0 - sig_d) * sig_grad


def mix_forward(place, near, far, age, chan, keep, got):
    chips, rows, both = near.shape
    width = both // 2
    model = keep.shape[2] - both
    length = 2 * chips * rows
    chunk = 2 * rows
    columns = keep.shape[2]
    one_block = lambda i, s: (i ^ (s[0] // 2), 0, 0)
    time_block = lambda i, s: (i, 0)
    token_block = lambda i, s: (0, i ^ (s[0] // 2), 0, 0)
    saved = lambda dtype: jax.ShapeDtypeStruct((length, width), dtype)
    spec = pl.BlockSpec((chunk, width), time_block)
    fixed = lambda shape: pl.BlockSpec(shape, lambda i, s: (0,) * len(shape))
    return pl.pallas_call(
        mix_forward_kernel,
        grid_spec=pltpu.PrefetchScalarGridSpec(
            num_scalar_prefetch=1,
            grid=(chips,),
            in_specs=[
                pl.BlockSpec((None, rows, both), one_block),
                pl.BlockSpec((None, rows, both), one_block),
                pl.BlockSpec((chunk, 1), time_block),
                pl.BlockSpec((chan.shape[0], width), lambda i, s: (0, s[0])),
                fixed(keep.shape),
                fixed(got.shape),
            ],
            out_specs=[pl.BlockSpec((2, None, rows, width), token_block)]
            + [pl.BlockSpec((None, rows, model), one_block)] * 2
            + [spec] * 9
            + [fixed((width, columns))],
            scratch_shapes=[
                pltpu.VMEM((chunk + 8, width), jnp.float32),
                pltpu.VMEM((8, width), jnp.float32),
            ],
        ),
        out_shape=[
            jax.ShapeDtypeStruct((2, chips, rows, width), jnp.bfloat16),
            jax.ShapeDtypeStruct((chips, rows, model), jnp.bfloat16),
            jax.ShapeDtypeStruct((chips, rows, model), jnp.bfloat16),
            saved(jnp.bfloat16),
            saved(jnp.bfloat16),
        ]
        + [saved(jnp.float32)] * 7
        + [jax.ShapeDtypeStruct((width, columns), jnp.bfloat16)],
        compiler_params=pltpu.CompilerParams(vmem_limit_bytes=56 * 1024 * 1024),
        name="mix_forward",
    )(place, near, far, age, chan, keep, got)


def mix_backward_kernel(
    seq_ref,
    near_ref,
    far_ref,
    age_ref,
    chan_ref,
    weights_ref,
    in_ref,
    merged_ref,
    branch_ref,
    conv_ref,
    gelu_ref,
    gelu_grad_ref,
    decay_ref,
    input_ref,
    direct_ref,
    sig_ref,
    decay_grad_ref,
    both_ref,
    small_ref,
    back_near_ref,
    back_far_ref,
    *rest,
):
    place = seq_ref[0]
    chips = near_ref.shape[0]
    row_refs, (out_grad, gate_grads, ahead, carry) = rest[:chips], rest[chips:]
    step = pl.program_id(0)
    chip, core = place // 2, place % 2
    rows, width = branch_ref.shape
    model = near_ref.shape[-1]

    @pl.when(step == 0)
    def _():
        carry[...] = jnp.zeros_like(carry)
        ahead[:, pl.ds(rows, 8), :] = jnp.zeros((3, 8, width), jnp.float32)
        small_ref[...] = jnp.zeros_like(small_ref)
        gate_grads[...] = jnp.zeros_like(gate_grads)
        out_grad[...] = jnp.zeros_like(out_grad)

    @pl.when(step > 0)
    def _():
        ahead[:, pl.ds(rows, 8), :] = ahead[:, pl.ds(0, 8), :]

    turn = (chips - 1 - step) ^ chip
    mixer_grad = jnp.concatenate([near_ref[turn], far_ref[turn]], axis=0)
    merged_grad = in_time(dot_nt(mixer_grad, weights_ref[:, :model]), core)
    age = age_ref[...]
    out_grad[...] += dot_tn(mixer_grad, merged_ref[...].reshape(rows, width))
    state_grad = (merged_grad * gelu_ref[...]).astype(jnp.bfloat16).astype(jnp.float32)
    gelu_pre_grad = merged_grad * gelu_grad_ref[...]
    decay = decay_ref[...]
    conv_low = conv_ref[...]
    row = lax.broadcasted_iota(jnp.int32, (rows, width), 0)
    next_decay = jnp.where(row == rows - 1, carry[0:1, :], pltpu.roll(decay, rows - 1, 0))
    carried = scan_rows(next_decay, state_grad, carry[1:2, :], True)
    carry[0:1, :] = decay[0:1, :]
    carry[1:2, :] = carried[0:1, :]
    gate_conv_grad = carried * direct_ref[...]
    input_low = (carried * input_ref[...]).astype(jnp.bfloat16)
    decay_low = (carried * decay_grad_ref[...]).astype(jnp.bfloat16)
    sig_grad = carried * sig_ref[...]
    conv_grad = (
        gate_conv_grad
        + dot_nt(decay_low, weights_ref[:, model : model + width])
        + dot_nt(input_low, weights_ref[:, model + width :])
    )
    gate_grads[0] += dot_tn(decay_low, conv_low)
    gate_grads[1] += dot_tn(input_low, conv_low)
    branch = branch_ref[...].astype(jnp.float32)
    branch_grad = chan_ref[0:1, :] * conv_grad
    small_ref[0:1, :] += jnp.sum(conv_grad * branch, axis=0, keepdims=True)
    for k in range(1, 4):
        ahead[k - 1, pl.ds(0, rows), :] = conv_grad * jnp.where(age >= k, 1.0, 0.0)
        shifted = ahead[k - 1, pl.ds(k, rows), :]
        branch_grad = branch_grad + chan_ref[k : k + 1, :] * shifted
        small_ref[k : k + 1, :] += jnp.sum(shifted * branch, axis=0, keepdims=True)
    small_ref[4:5, :] += jnp.sum(conv_grad, axis=0, keepdims=True)
    small_ref[5:6, :] += jnp.sum(decay_low.astype(jnp.float32), axis=0, keepdims=True)
    small_ref[6:7, :] += jnp.sum(input_low.astype(jnp.float32), axis=0, keepdims=True)
    small_ref[7:8, :] += 8.0 * chan_ref[8:9, :] * jnp.sum(sig_grad, axis=0, keepdims=True)
    by_core(jnp.concatenate([branch_grad, gelu_pre_grad], axis=1), both_ref, core)
    both = both_ref[...].reshape(rows, 2 * width)
    back = dot_nt(both, in_ref[...].reshape(model, 2 * width)).astype(jnp.bfloat16)
    back_near_ref[...] = back[: rows // 2]
    back_far_ref[...] = back[rows // 2 :]

    @pl.when(step == chips - 1)
    def _():
        slim, piece = model // (2 * chips), width // (2 * chips)
        for k in range(chips):
            for e in range(2):
                target = 2 * (chip ^ k) + (core ^ e)
                rows = pl.ds(pl.multiple_of(target * slim, slim), slim)
                row_refs[k][e, pl.ds(0, slim), :] = out_grad[rows, :].astype(jnp.bfloat16)
                rows = pl.ds(pl.multiple_of(target * piece, piece), piece)
                for j in range(2):
                    row_refs[k][e, pl.ds(slim + j * piece, piece), :] = gate_grads[j, rows, :].astype(
                        jnp.bfloat16
                    )


def mix_backward(place, near, far, age, chan, weights, pack, merged, saved):
    planes, _, both = pack.shape
    chips, rows, model = near.shape
    width, columns = weights.shape
    tall = (model + 2 * width) // (2 * chips)
    chunk = 2 * rows
    last = chips - 1
    time_block = lambda i, s: (last - i, 0)
    token_block = lambda i, s: (0, (last - i) ^ (s[0] // 2), 0, 0)
    spec = pl.BlockSpec((chunk, width), time_block)
    back = pl.BlockSpec((None, rows, model), lambda i, s: ((last - i) ^ (s[0] // 2), 0, 0))
    fixed = lambda shape: pl.BlockSpec(shape, lambda i, s: (0,) * len(shape))
    return pl.pallas_call(
        mix_backward_kernel,
        grid_spec=pltpu.PrefetchScalarGridSpec(
            num_scalar_prefetch=1,
            grid=(chips,),
            in_specs=[
                fixed(near.shape),
                fixed(far.shape),
                pl.BlockSpec((chunk, 1), time_block),
                pl.BlockSpec((chan.shape[0], width), lambda i, s: (0, s[0])),
                fixed((width, columns)),
                fixed((planes, model // planes, both)),
                pl.BlockSpec((2, None, rows, width), token_block),
            ]
            + [spec] * 9,
            out_specs=[
                pl.BlockSpec((2, None, rows, 2 * width), token_block),
                fixed((8, width)),
                back,
                back,
            ]
            + [fixed((2, tall, width))] * chips,
            scratch_shapes=[
                pltpu.VMEM((model, width), jnp.float32),
                pltpu.VMEM((2, width, width), jnp.float32),
                pltpu.VMEM((3, chunk + 8, width), jnp.float32),
                pltpu.VMEM((8, width), jnp.float32),
            ],
        ),
        out_shape=[
            jax.ShapeDtypeStruct((2, chips, rows, 2 * width), jnp.bfloat16),
            jax.ShapeDtypeStruct((8, width), jnp.float32),
            jax.ShapeDtypeStruct(near.shape, jnp.bfloat16),
            jax.ShapeDtypeStruct(near.shape, jnp.bfloat16),
        ]
        + [jax.ShapeDtypeStruct((2, tall, width), jnp.bfloat16)] * chips,
        compiler_params=pltpu.CompilerParams(vmem_limit_bytes=50 * 1024 * 1024),
        cost_estimate=pl.CostEstimate(
            flops=10**9, bytes_accessed=24 * 10**6, transcendentals=0
        ),
        name="mix_backward",
    )(place, near, far, age, chan, weights, pack, merged, *saved)


def unit_kernel(
    near_ref,
    far_ref,
    cot_near_ref,
    cot_far_ref,
    pack_ref,
    back_near_out,
    back_far_out,
    mixed_near_out,
    mixed_far_out,
    grads_out,
    normed,
    cot,
    gate_up,
    down,
    pair,
    hidden,
    pair_t,
    hidden_t,
    grads,
    back,
    mixed,
    in_sems,
    out_sems,
):
    bf16 = jnp.bfloat16
    chips, rows, _ = near_ref.shape
    planes, tall, near_model = pack_ref.shape
    both = pair.shape[1]
    part = both // 2
    span = part // planes
    side = near_model // 2
    spare = down.shape[0] - part
    half = chips * rows
    incoming, outgoing = [], []

    def fetch(source, target):
        copy = pltpu.make_async_copy(source, target, in_sems.at[len(incoming)])
        copy.start()
        incoming.append(copy)
        return copy

    def send(source, target):
        copy = pltpu.make_async_copy(source, target, out_sems.at[len(outgoing)])
        copy.start()
        outgoing.append(copy)

    def fetch_half(source, target, i):
        return [
            fetch(source.at[k], target.at[pl.ds(i * half + k * rows, rows), :]) for k in range(chips)
        ]

    gate_up_copies = [
        fetch(
            pack_ref.at[z, pl.ds(j * near_model, near_model), :],
            gate_up.at[pl.ds(z * near_model, near_model), pl.ds(j * near_model, near_model)],
        )
        for z in range(planes)
        for j in range(3)
    ]
    normed_copies = [fetch_half(near_ref, normed, 0)]
    for copy in gate_up_copies + normed_copies[0]:
        copy.wait()
    down_copies = [
        fetch(
            pack_ref.at[z, pl.ds(3 * near_model + j * span, span), :],
            down.at[pl.ds(z * span, span), pl.ds(j * near_model, near_model)],
        )
        for z in range(planes)
        for j in range(planes)
    ]
    cot_copies = [fetch_half(cot_near_ref, cot, 0)]
    normed_copies.append(fetch_half(far_ref, normed, 1))
    cot_copies.append(fetch_half(cot_far_ref, cot, 1))
    chunk = 2 * rows
    first_unit, mid_unit, last_unit = (pl.ds(j * near_model, near_model) for j in range(3))
    for i in range(chips):
        here = pl.ds(i * chunk, chunk)
        if i * chunk == half:
            for copy in normed_copies[1] + cot_copies[1]:
                copy.wait()
        pre = dot_nn(normed[here, :], gate_up[...])
        if i == 0:
            for copy in down_copies + cot_copies[0]:
                copy.wait()
            down[pl.ds(part, spare), :] = jnp.zeros((spare, down.shape[1]), bf16)
        above = dot_nt(cot[here, :], down[...])
        up = pre[:, 2 * near_model :]
        value, slope = gelu_parts(pre[:, :near_model])
        grad = above[:, :near_model]
        hidden[here, first_unit] = (value * up).astype(bf16)
        pair[here, first_unit] = (grad * up * slope).astype(bf16)
        pair[here, last_unit] = (grad * value).astype(bf16)
        mid = pre[:, near_model : 2 * near_model]
        broad = side + spare
        up = pltpu.roll(mid, side, 1)[:, :broad]
        value, slope = gelu_parts(mid[:, :broad])
        grad = above[:, near_model:]
        hidden[here, pl.ds(near_model, side)] = (value * up)[:, :side].astype(bf16)
        left, right = grad * up * slope, grad * value
        left = jnp.concatenate([left, left[:, : near_model - broad]], axis=1)
        right = jnp.concatenate([right, right[:, : near_model - broad]], axis=1)
        lane = lax.broadcasted_iota(jnp.int32, left.shape, 1)
        pair[here, mid_unit] = jnp.where(lane < side, left, pltpu.roll(right, side, 1)).astype(bf16)
        pair_t[:, here] = pair[here, :].T
        hidden_t[:, here] = hidden[here, :].T
    def unit_rows(start):
        pieces, stop = [], start + span
        if start < near_model:
            pieces.append((2 * near_model + start, min(stop, near_model) - start))
        if stop > near_model:
            first = max(start, near_model)
            pieces.append((part + first - near_model, stop - first))
        return pieces

    for first_z in range(0, planes, 2):
        here = pl.ds(first_z * near_model, 2 * near_model)
        grad = dot_nn(hidden_t[...], cot[:, here]).astype(bf16)
        for z in (first_z, first_z + 1):
            columns = slice((z - first_z) * near_model, (z - first_z + 1) * near_model)
            for j in range(planes):
                grads[j, pl.ds((3 * z + 2) * span, span), :] = grad[
                    j * span : (j + 1) * span, columns
                ]
    for first_z in range(0, planes, 2):
        here = pl.ds(first_z * near_model, 2 * near_model)
        grad = dot_nn(pair_t[...], normed[:, here]).astype(bf16)
        for z in (first_z, first_z + 1):
            columns = slice((z - first_z) * near_model, (z - first_z + 1) * near_model)
            for j in range(planes):
                row = 3 * j * span
                grads[z, pl.ds(row, span), :] = grad[j * span : (j + 1) * span, columns]
                row += span
                for first, count in unit_rows(j * span):
                    grads[z, pl.ds(row, count), :] = grad[first : first + count, columns]
                    row += count
            send(grads.at[z], grads_out.at[z])
    for i, out in ((0, mixed_near_out), (1, mixed_far_out)):
        here = pl.ds(i * half, half)
        mixed[here, :] = dot_nn(hidden[here, :], down[pl.ds(0, part), :]).astype(bf16)
        for k in range(chips):
            send(mixed.at[pl.ds(i * half + k * rows, rows), :], out.at[k])
    for i, out in ((1, back_far_out), (0, back_near_out)):
        for k in range(0, chips, 2):
            first_row = i * half + k * rows
            here = pl.ds(first_row, chunk)
            back[here, :] = dot_nt(pair[here, :], gate_up[...]).astype(bf16)
            for e in range(2):
                send(back.at[pl.ds(first_row + e * rows, rows), :], out.at[k + e])
    for copy in outgoing:
        copy.wait()


def unit_back_and_forth(near, far, cot_near, cot_far, pack, part):
    chips, rows, model = near.shape
    length = 2 * chips * rows
    planes, _, near_model = pack.shape
    bf16 = jnp.bfloat16
    there = pl.BlockSpec(memory_space=pl.ANY)
    return pl.pallas_call(
        unit_kernel,
        in_specs=[there] * 5,
        out_specs=[there] * 5,
        scratch_shapes=[
            pltpu.VMEM((length, model), bf16),
            pltpu.VMEM((length, model), bf16),
            pltpu.VMEM((model, 2 * part), bf16),
            pltpu.VMEM((pl.cdiv(part, 128) * 128, model), bf16),
            pltpu.VMEM((length, 2 * part), bf16),
            pltpu.VMEM((length, part), bf16),
            pltpu.VMEM((2 * part, length), bf16),
            pltpu.VMEM((part, length), bf16),
            pltpu.VMEM(pack.shape, bf16),
            pltpu.VMEM((length, model), bf16),
            pltpu.VMEM((length, model), bf16),
            pltpu.SemaphoreType.DMA((4 * chips + planes * (3 + planes),)),
            pltpu.SemaphoreType.DMA((4 * chips + planes,)),
        ],
        out_shape=[jax.ShapeDtypeStruct(near.shape, bf16)] * 4
        + [jax.ShapeDtypeStruct(pack.shape, bf16)],
        compiler_params=pltpu.CompilerParams(vmem_limit_bytes=58 * 1024 * 1024),
        name="unit_back_and_forth",
    )(near, far, cot_near, cot_far, pack)


def mix_pack_kernel(
    place_ref, input_ref, gelu_ref, out_ref, decay_ref, gate_ref, in_own_ref, rows_ref
):
    width, model = input_ref.shape[1], out_ref.shape[2]
    in_own_ref[:, pl.ds(0, width)] = input_ref[...]
    in_own_ref[:, pl.ds(width, width)] = gelu_ref[...]
    rows_ref[:, :, pl.ds(0, model)] = out_ref[...]
    rows_ref[:, :, pl.ds(model, width)] = decay_ref[...]
    rows_ref[:, :, pl.ds(model + width, width)] = gate_ref[...]


def own_mix_pack(place, input_proj, gelu_proj, output_proj, decay_gate, input_gate):
    near_model, channels = input_proj.shape
    width = decay_gate.shape[1]
    heads = decay_gate.shape[0] // width
    model = output_proj.shape[1]
    piece = width // (channels // width)
    mine = pl.BlockSpec((near_model, width), lambda i, s: (0, s[0]))
    rows = lambda columns: pl.BlockSpec((heads, piece, columns), lambda i, s: (0, s[0], 0))
    shapes = [(near_model, 2 * width), (heads, piece, model + 2 * width)]
    return pl.pallas_call(
        mix_pack_kernel,
        grid_spec=pltpu.PrefetchScalarGridSpec(
            num_scalar_prefetch=1,
            grid=(1,),
            in_specs=[mine, mine, rows(model), rows(width), rows(width)],
            out_specs=[
                pl.BlockSpec(shape, lambda i, s, zeros=(0,) * len(shape): zeros) for shape in shapes
            ],
        ),
        out_shape=[jax.ShapeDtypeStruct(shape, input_proj.dtype) for shape in shapes],
        name="own_mix_pack",
    )(
        place,
        input_proj,
        gelu_proj,
        output_proj.reshape(heads, width, model),
        decay_gate.reshape(heads, width, width),
        input_gate.reshape(heads, width, width),
    )


def unit_pack_kernel(place_ref, gate_ref, up_ref, down_ref, pack_ref, windows, sems):
    place = place_ref[0]
    near_model, deep = gate_ref.shape
    planes = windows.shape[1]
    tile = 128
    span = (pack_ref.shape[0] - 3 * near_model) // planes
    extra = span - tile
    copies = []

    def fetch(source, target):
        copies.append(pltpu.make_async_copy(source, target, sems.at[len(copies)]))
        copies[-1].start()

    for i, ref in enumerate((gate_ref, up_ref)):
        for z in range(planes):
            start = pl.multiple_of(z * (deep // planes) + place * tile, tile)
            fetch(ref.at[:, pl.ds(start, 2 * tile)], windows.at[i, z])
    rows = pl.ds(pl.multiple_of(place * span, 16), span)
    for j in range(planes):
        fetch(
            down_ref.at[rows, pl.ds(j * near_model, near_model)],
            pack_ref.at[pl.ds(3 * near_model + j * span, span), :],
        )
    lane = lax.broadcasted_iota(jnp.int32, (near_model, tile), 1)

    def tiles(i):
        parts = []
        for z in range(planes):
            copies[i * planes + z].wait()
            turn = lax.rem((z - place) * extra + 2 * tile, 2 * tile)
            parts.append(pltpu.roll(windows[i, z].astype(jnp.float32), turn, 1))
        found = [parts[0][:, :tile]]
        for z in range(1, planes):
            found.append(jnp.where(lane < z * extra, parts[z - 1][:, tile:], parts[z][:, :tile]))
        return found + [parts[planes - 1][:, tile:]]

    gate, up = tiles(0), tiles(1)
    half = tile // 2
    turned = [pltpu.roll(up[j], half, 1) for j in (3, 4)]
    mid = [
        gate[3],
        jnp.where(lane < half, gate[4], turned[0]),
        jnp.where(lane < half, turned[0], turned[1]),
    ]
    for block, found in enumerate((gate[:3], mid, up[:3])):
        for j in range(3):
            pack_ref[pl.ds(block * near_model, near_model), pl.ds(j * tile, tile)] = found[
                j
            ].astype(pack_ref.dtype)
    for copy in copies[2 * planes :]:
        copy.wait()


def own_unit_pack(place, mlp_gate, mlp_up, mlp_down, planes, span):
    near_model = mlp_gate.shape[0]
    tall = 3 * near_model + planes * span
    there = pl.BlockSpec(memory_space=pl.ANY)
    return pl.pallas_call(
        unit_pack_kernel,
        grid_spec=pltpu.PrefetchScalarGridSpec(
            num_scalar_prefetch=1,
            grid=(1,),
            in_specs=[there] * 3,
            out_specs=pl.BlockSpec((tall, near_model), lambda i, s: (0, 0)),
            scratch_shapes=[
                pltpu.VMEM((2, planes, near_model, 256), mlp_gate.dtype),
                pltpu.SemaphoreType.DMA((3 * planes,)),
            ],
        ),
        out_shape=jax.ShapeDtypeStruct((tall, near_model), mlp_gate.dtype),
        compiler_params=pltpu.CompilerParams(vmem_limit_bytes=48 * 1024 * 1024),
        cost_estimate=pl.CostEstimate(flops=0, bytes_accessed=5 << 20, transcendentals=0),
        name="own_unit_pack",
    )(place, mlp_gate, mlp_up, mlp_down)


def in_grads_kernel(
    place_ref,
    near_ref,
    far_ref,
    both_ref,
    back_near_ref,
    back_far_ref,
    gain_ref,
    later_gain_ref,
    small_ref,
    grads_ref,
    sums_ref,
):
    place = place_ref[0]
    chips, rows, model = near_ref.shape
    planes, near_model, _ = grads_ref.shape
    taken, width = small_ref.shape
    near = near_ref[...].reshape(chips * rows, model)
    far = far_ref[...].reshape(chips * rows, model)
    for z in range(planes):
        here = slice(z * near_model, (z + 1) * near_model)
        total = dot_tn(near[:, here], both_ref[0].reshape(chips * rows, -1))
        total = total + dot_tn(far[:, here], both_ref[1].reshape(chips * rows, -1))
        grads_ref[z] = total.astype(grads_ref.dtype)
    gain_sum = jnp.zeros((1, model), jnp.float32)
    for ref, back_ref in ((near_ref, back_near_ref), (far_ref, back_far_ref)):
        for k in range(chips):
            product = ref[k].astype(jnp.float32) * back_ref[k].astype(jnp.float32)
            gain_sum = gain_sum + jnp.sum(product, axis=0, keepdims=True)
    sums_ref[...] = jnp.zeros_like(sums_ref)
    across = model // width
    row = pl.multiple_of(taken * (place // across), taken)
    column = pl.multiple_of(width * lax.rem(place, across), width)
    sums_ref[pl.ds(row, taken), pl.ds(column, width)] = small_ref[...]
    band = model // 3
    for j in range(3):
        here = slice(j * band, (j + 1) * band)
        sums_ref[pl.ds(taken + j, 1), pl.ds(band, band)] = gain_sum[:, here] / gain_ref[:, here]
        sums_ref[pl.ds(taken + 3 + j, 1), pl.ds(band, band)] = later_gain_ref[:, here]


def in_grads(place, near, far, both, back_near, back_far, gain, later_gain, small, planes):
    chips, rows, model = near.shape
    columns = both.shape[-1]
    whole = lambda shape: pl.BlockSpec(shape, lambda i, s: (0,) * len(shape))
    inputs = (near, far, both, back_near, back_far, gain[None], later_gain, small)
    shapes = [
        jax.ShapeDtypeStruct((planes, model // planes, columns), jnp.bfloat16),
        jax.ShapeDtypeStruct((16, model), jnp.float32),
    ]
    return pl.pallas_call(
        in_grads_kernel,
        grid_spec=pltpu.PrefetchScalarGridSpec(
            num_scalar_prefetch=1,
            grid=(1,),
            in_specs=[whole(x.shape) for x in inputs],
            out_specs=[whole(x.shape) for x in shapes],
        ),
        out_shape=shapes,
        compiler_params=pltpu.CompilerParams(vmem_limit_bytes=24 * 1024 * 1024),
        name="in_grads",
    )(place, *inputs)


def payload_kernel(*refs):
    near_ref, got_ref, *extra_refs = refs[: -near_count(refs)]
    own_ref, *out_refs = refs[-near_count(refs) :]
    chips, rows, _ = near_ref.shape
    for k in range(chips):
        total = near_ref[k].astype(jnp.float32) + got_ref[k].astype(jnp.float32)
        if k == 0:
            own_ref[...] = total
        else:
            out_refs[k - 1][pl.ds(0, rows), :] = total.astype(jnp.bfloat16)
            for ref in extra_refs:
                out_refs[k - 1][pl.ds(rows, ref.shape[0]), :] = ref[...]


def near_count(refs):
    return refs[0].shape[0]


def payloads(near, got, extra):
    chips, rows, model = near.shape
    tall = rows + extra.shape[0]
    whole = pl.BlockSpec(memory_space=pltpu.VMEM)
    inputs = (near, got) + ((extra,) if extra.shape[0] else ())
    return pl.pallas_call(
        payload_kernel,
        in_specs=[whole] * len(inputs),
        out_specs=[whole] * chips,
        out_shape=[jax.ShapeDtypeStruct((rows, model), jnp.float32)]
        + [jax.ShapeDtypeStruct((tall, model), jnp.bfloat16)] * (chips - 1),
        compiler_params=pltpu.CompilerParams(vmem_limit_bytes=20 * 1024 * 1024),
        cost_estimate=little,
        name="payloads",
    )(*inputs)


def middle_kernel(tokens_ref, gain_ref, *refs):
    *parts, middle_ref, normed_ref = refs
    total = tokens_ref[...].astype(jnp.float32)
    for ref in parts:
        total = total + ref[...].astype(jnp.float32)
    middle_ref[...] = total
    scale = lax.rsqrt(jnp.mean(total * total, axis=-1, keepdims=True) + norm_eps)
    normed_ref[...] = (total * scale * gain_ref[...]).astype(jnp.bfloat16)


def middle_and_normed(tokens, gain, parts):
    rows, model = tokens.shape
    whole = pl.BlockSpec(memory_space=pltpu.VMEM)
    return pl.pallas_call(
        middle_kernel,
        in_specs=[whole] * (2 + len(parts)),
        out_specs=[whole] * 2,
        out_shape=[
            jax.ShapeDtypeStruct((rows, model), jnp.float32),
            jax.ShapeDtypeStruct((rows, model), jnp.bfloat16),
        ],
        cost_estimate=little,
        name="middle_and_normed",
    )(tokens, gain[None], *parts)


def middle_back_kernel(cot_ref, middle_ref, gain_ref, *refs):
    *parts, grad_ref, low_ref, gain_grad_ref = refs
    middle, gain = middle_ref[...], gain_ref[...]
    upper = parts[0][...]
    for ref in parts[1:]:
        upper = upper + ref[...].astype(jnp.float32)
    scale = lax.rsqrt(jnp.mean(middle * middle, axis=-1, keepdims=True) + norm_eps)
    gain_grad_ref[...] = jnp.sum(upper * middle * scale, axis=0, keepdims=True)
    scaled = gain * upper
    inner = jnp.mean(scaled * middle, axis=-1, keepdims=True)
    grad = cot_ref[...].astype(jnp.float32) + scale * scaled - middle * (scale * scale * scale) * inner
    grad_ref[...] = grad
    low_ref[...] = grad.astype(jnp.bfloat16)


def middle_back(cotangent, middle, gain, parts):
    rows, model = middle.shape
    whole = pl.BlockSpec(memory_space=pltpu.VMEM)
    return pl.pallas_call(
        middle_back_kernel,
        in_specs=[whole] * (3 + len(parts)),
        out_specs=[whole] * 3,
        out_shape=[
            jax.ShapeDtypeStruct((rows, model), jnp.float32),
            jax.ShapeDtypeStruct((rows, model), jnp.bfloat16),
            jax.ShapeDtypeStruct((1, model), jnp.float32),
        ],
        cost_estimate=little,
        name="middle_back",
    )(cotangent, middle, gain[None], *parts)


def halves(value, wanted):
    side = value.shape[1] // 2
    return jnp.where(wanted == 1, pltpu.roll(value, side, 1), value)


def unit_give_kernel(place_ref, *refs):
    *piece_refs, give_ref = refs
    place = place_ref[0]
    chip, core = place // 2, place % 2
    turn = core ^ (chip // 2)
    span = piece_refs[0].shape[0] // 3
    for e in range(2):
        first, second = (piece_refs[i][pl.ds(0, 2 * span), :] for i in (e, 2 + e))
        give_ref[pl.ds(2 * e * span, 2 * span), :] = jnp.where(turn == 0, second, first)
    for e in range(2):
        first, second = (
            halves(piece_refs[2 * e + i][pl.ds(2 * span, span), :].astype(jnp.float32), 1 - core)
            for i in range(2)
        )
        side = first.shape[1] // 2
        lane = lax.broadcasted_iota(jnp.int32, first.shape, 1)
        give_ref[pl.ds((4 + e) * span, span), :] = jnp.where(
            lane < side, first, pltpu.roll(second, side, 1)
        ).astype(give_ref.dtype)


def unit_finish_kernel(place_ref, *refs):
    *piece_refs, got_ref, gate_ref, up_ref, down_ref, down = refs
    place = place_ref[0]
    chip, core = place // 2, place % 2
    turn = core ^ (chip // 2)
    span = piece_refs[0].shape[0] // 3
    side = piece_refs[0].shape[1] // 2
    for e in range(2):
        first, second = (piece_refs[i][pl.ds(0, 2 * span), :] for i in (e, 2 + e))
        mine = jnp.where(turn == 0, first, second).astype(jnp.float32)
        away = got_ref[pl.ds(2 * e * span, 2 * span), :].astype(jnp.float32)
        column = 2 * ((chip % 2) ^ e)
        for value, at in ((mine, column + core), (away, column + 1 - core)):
            rows = pl.ds(pl.multiple_of(at * span, span), span)
            gate_ref[rows, :] = value[:span]
            up_ref[rows, :] = value[span:]
    for k in range(4):
        mine = halves(piece_refs[k][pl.ds(2 * span, span), :].astype(jnp.float32), core)
        away = halves(got_ref[pl.ds((4 + k // 2) * span, span), :].astype(jnp.float32), k % 2)
        for value, at in ((mine, core), (away, 1 - core)):
            row = pl.multiple_of((2 * (chip ^ k) + at) * span, span)
            down[pl.ds(row, span), :] = value[:, :side]
    down_ref[...] = down[...].T


def unit_pieces(total, chip):
    chips = total.shape[0]
    pieces = [
        lax.dynamic_index_in_dim(total, chip ^ k, 0, keepdims=False) for k in range(chips)
    ]
    return [pieces[0]] + [chip_swap(pieces[k], k) for k in range(1, chips)]


def unit_exchange(place, pieces):
    chips = len(pieces)
    tall, cols = pieces[0].shape
    span = tall // 3
    fixed = lambda shape: pl.BlockSpec(shape, lambda i, s: (0,) * len(shape))
    give = pl.pallas_call(
        unit_give_kernel,
        grid_spec=pltpu.PrefetchScalarGridSpec(
            num_scalar_prefetch=1,
            grid=(1,),
            in_specs=[fixed((tall, cols))] * chips,
            out_specs=fixed((6 * span, cols)),
        ),
        out_shape=jax.ShapeDtypeStruct((6 * span, cols), pieces[0].dtype),
        name="unit_give",
    )(place, *pieces)
    shapes = [(4 * span, cols), (4 * span, cols), (cols // 2, 2 * chips * span)]
    grads = pl.pallas_call(
        unit_finish_kernel,
        grid_spec=pltpu.PrefetchScalarGridSpec(
            num_scalar_prefetch=1,
            grid=(1,),
            in_specs=[fixed((tall, cols))] * chips + [fixed((6 * span, cols))],
            out_specs=[fixed(shape) for shape in shapes],
            scratch_shapes=[pltpu.VMEM((2 * chips * span, cols // 2), jnp.float32)],
        ),
        out_shape=[jax.ShapeDtypeStruct(shape, jnp.float32) for shape in shapes],
        compiler_params=pltpu.CompilerParams(vmem_limit_bytes=32 * 1024 * 1024),
        name="unit_finish",
    )(place, *pieces, core_swap(give))
    return [grad.T for grad in grads]


def grad_pack_kernel(place_ref, in_ref, *refs):
    *blocks, pack_ref = refs
    place = place_ref[0]
    chips = len(blocks) // 2
    chip, core = place // 2, place % 2
    near_model, both = in_ref.shape[1:]
    tall, width = blocks[0].shape
    pack_ref[:, pl.ds(0, near_model), :] = in_ref[...]
    for k in range(chips):
        home, away = blocks[k][...], blocks[chips + k][...]
        odd = core == 1
        pack_ref[chip ^ k, pl.ds(near_model, tall), pl.ds(0, width)] = jnp.where(odd, away, home)
        pack_ref[chip ^ k, pl.ds(near_model, tall), pl.ds(width, width)] = jnp.where(odd, home, away)


def grad_pack(place, in_grad, home, away):
    planes, near_model, both = in_grad.shape
    tall, width = home[0].shape
    return pl.pallas_call(
        grad_pack_kernel,
        grid_spec=pltpu.PrefetchScalarGridSpec(
            num_scalar_prefetch=1,
            grid=(1,),
            in_specs=[pl.BlockSpec(in_grad.shape, lambda i, s: (0, 0, 0))]
            + [pl.BlockSpec((tall, width), lambda i, s: (0, 0))] * (2 * len(home)),
            out_specs=pl.BlockSpec((planes, near_model + tall, both), lambda i, s: (0, 0, 0)),
        ),
        out_shape=jax.ShapeDtypeStruct((planes, near_model + tall, both), jnp.bfloat16),
        compiler_params=pltpu.CompilerParams(vmem_limit_bytes=16 * 1024 * 1024),
        name="grad_pack",
    )(place, in_grad, *home, *away)


def mix_results_kernel(sum_ref, *refs):
    row = 0
    width = sum_ref.shape[1] // 2
    for j, ref in enumerate(refs):
        rows = ref.shape[0]
        if j < 2:
            ref[...] = sum_ref[pl.ds(0, rows), pl.ds(j * width, width)].astype(jnp.float32)
            row = rows
        else:
            ref[...] = sum_ref[pl.ds(row, rows), :].astype(jnp.float32)
            row += rows


def mix_results(total, near_model, slim):
    tall, both = total.shape
    piece = (tall - near_model - slim) // 2
    shapes = [(near_model, both // 2)] * 2 + [(slim, both), (piece, both), (piece, both)]
    whole = pl.BlockSpec(memory_space=pltpu.VMEM)
    found = pl.pallas_call(
        mix_results_kernel,
        in_specs=[whole],
        out_specs=[whole] * len(shapes),
        out_shape=[jax.ShapeDtypeStruct(shape, jnp.float32) for shape in shapes],
        name="mix_results",
    )(total)
    return [*found[:2], *[grad.T for grad in found[2:]]]


def norm_back(values, scale, gain, grad):
    inner = jnp.mean(gain * grad * values, axis=-1, keepdims=True)
    return scale * gain * grad - values * (scale * scale * scale) * inner


def narrow_shards(
    tokens,
    cotangent,
    doc_starts,
    mix_gain,
    input_proj,
    gelu_proj,
    conv_taps,
    conv_bias,
    decay_gate,
    decay_bias,
    input_gate,
    input_bias,
    decay_param,
    output_proj,
    mlp_gain,
    mlp_gate,
    mlp_up,
    mlp_down,
):
    f32, bf16 = jnp.float32, jnp.bfloat16
    devices, planes = lax.axis_size("seq"), lax.axis_size("fsdp")
    chips = devices // 2
    place, plane = lax.axis_index("seq"), lax.axis_index("fsdp")
    chip, core = place // 2, place % 2
    rows, model = tokens.shape[1:]
    length = rows * devices
    channels = conv_taps.shape[1]
    width = decay_gate.shape[1]
    deep = mlp_gate.shape[1]
    heads = output_proj.shape[0] // width
    piece = width // devices
    span = deep // (planes * devices)
    part = deep // devices
    near_model = model // planes

    def along_fsdp(x):
        return lax.all_gather(x, "fsdp", axis=0, tiled=True)

    def columns(x, start, size):
        return lax.dynamic_slice_in_dim(x, start, size, axis=1)

    place_arg = place.astype(jnp.int32)[None]
    in_own, rowset = own_mix_pack(
        place_arg, input_proj, gelu_proj, output_proj, decay_gate, input_gate
    )
    in_own, rowset, tokens = tie(in_own, rowset, tokens)
    in_weights = lax.all_gather(in_own, "fsdp", axis=0)
    by_plane = [plane_swap(rowset, k) for k in range(planes)]

    values = tokens[0].astype(f32)
    scale1 = lax.rsqrt(jnp.mean(values * values, axis=-1, keepdims=True) + norm_eps)
    normed_own, mlp_gate, mlp_up, mlp_down = tie(
        (values * scale1 * mix_gain).astype(bf16), mlp_gate, mlp_up, mlp_down
    )
    normed_near, normed_far = gather_blocks(normed_own)
    unit_pack = own_unit_pack(place_arg, mlp_gate, mlp_up, mlp_down, planes, span)
    unit_pack, normed_near, normed_far = tie(unit_pack, normed_near, normed_far)
    unit_pack = lax.all_gather(unit_pack, "fsdp", axis=0)
    positions = jnp.arange(length, dtype=jnp.int32)
    starts = doc_starts[0]
    begin = jnp.max(jnp.where(starts[None, :] <= positions[:, None], starts[None, :], 0), axis=1)
    age = (positions - begin).astype(f32)[:, None]
    chan = jnp.concatenate(
        [
            conv_taps,
            conv_bias[None],
            decay_bias[None],
            input_bias[None],
            jax.nn.softplus(-decay_param)[None],
            jax.nn.sigmoid(-decay_param)[None],
            jnp.zeros((7, channels), f32),
        ],
        axis=0,
    )
    normed_near, normed_far, out_grad = tie(normed_near, normed_far, cotangent[0])
    cot_got = [chip_swap(out_grad, k) for k in range(1, chips)]
    held = tie(normed_near, normed_far, chan, age, *by_plane, *cot_got)
    normed_near, normed_far, chan, age = held[:4]
    by_plane, cot_got = held[4 : 4 + planes], held[4 + planes :]

    pre_near, pre_far = (
        dot_nn(x.reshape(-1, model), in_weights.reshape(model, 2 * width)).reshape(
            chips, rows, 2 * width
        )
        for x in (normed_near, normed_far)
    )
    keep, got, pre_near, pre_far = exchange(
        jnp.stack(by_plane), chip, core, plane, [pre_near, pre_far]
    )
    merged, middle_near, middle_far, *saved, weights = mix_forward(
        place_arg, pre_near, pre_far, age, chan, keep, got
    )
    cot_near = jnp.stack([out_grad, *cot_got])
    cot_far = core_swap(cot_near)
    middle, normed2 = middle_and_normed(
        tokens[0], mlp_gain, spread_pairs(*pair_blocks(middle_near, middle_far))
    )

    near, far = gather_blocks(normed2)
    back_near, back_far, mixed_near, mixed_far, unit_grads = unit_back_and_forth(
        near, far, cot_near, cot_far, unit_pack, part
    )
    unit_sum = lax.psum_scatter(unit_grads, "fsdp", scatter_dimension=0, tiled=False)

    middle_grad, middle_low, mlp_gain_term = middle_back(
        out_grad, middle, mlp_gain, spread_pairs(*pair_blocks(back_near, back_far))
    )
    middle_low, mixed_near, mixed_far = tie(middle_low, mixed_near, mixed_far)
    mixed_own, *mixed_low = pair_blocks(mixed_near, mixed_far)
    first, *others = [chip_swap(middle_low, k) for k in range(1, chips)]
    first, mixed_own, *mixed_low = tie(first, mixed_own, *mixed_low)
    near = jnp.stack([middle_low, first, *others])
    far = core_swap(near)

    both, small, back_near, back_far, *by_chip = mix_backward(
        place_arg, near, far, age, chan, weights, in_weights, merged, saved
    )
    mixed_got = [chip_swap(block, k + 1) for k, block in enumerate(mixed_low)]
    held = tie(*mixed_got, *by_chip)
    mixed_got, by_chip = held[: chips - 1], held[chips - 1 :]
    arrived = [by_chip[0]] + [chip_swap(by_chip[k], k) for k in range(1, chips)]
    arrived[1], both, back_near, back_far, small = tie(
        arrived[1], both, back_near, back_far, small
    )
    in_pack, sums = in_grads(
        place_arg,
        normed_near,
        normed_far,
        both,
        back_near,
        back_far,
        mix_gain,
        mlp_gain_term,
        small,
        planes,
    )
    sums = sums + core_swap(sums)
    *arrived, in_pack = tie(*arrived, in_pack)
    away = core_swap(jnp.stack([block[1] for block in arrived]))
    pack, unit_sum, back_near, back_far, *mixed_got = tie(
        grad_pack(
            place_arg,
            in_pack,
            [block[0] for block in arrived],
            [away[k] for k in range(chips)],
        ),
        unit_sum,
        back_near,
        back_far,
        *mixed_got,
    )
    normed_own, *normed_low = pair_blocks(back_near, back_far)
    mixed = mixed_own
    for got in mixed_got:
        mixed = mixed + got.astype(f32)
    mixed = (middle + mixed).astype(bf16)
    mix_sum = lax.psum_scatter(pack, "fsdp", scatter_dimension=0, tiled=False)
    (
        input_proj_grad,
        gelu_proj_grad,
        output_proj_grad,
        decay_gate_grad,
        input_gate_grad,
    ) = mix_results(mix_sum, near_model, model // devices)

    pieces = unit_pieces(unit_sum.reshape(planes, 3 * span, near_model), chip)
    pieces[1], sums, *normed_low = tie(pieces[1], sums, *normed_low)
    normed_grad = normed_own
    for k in range(1, chips):
        normed_grad = normed_grad + chip_swap(normed_low[k - 1], k).astype(f32)
    values_part = norm_back(values, scale1, mix_gain, normed_grad)
    tokens_grad = (middle_grad + values_part).astype(bf16)

    low = sums.astype(bf16)
    for k in range(1, chips):
        sums = sums + chip_swap(low, k).astype(f32)
    sums = over_planes(sums)
    sums, *pieces = tie(sums, *pieces)
    channel_sums = jnp.concatenate([sums[:8], sums[8:, : channels - model]], axis=1)
    band = model // 3
    gain_sums = sums[8:14, band : 2 * band].reshape(2, model)
    mlp_gate_grad, mlp_up_grad, mlp_down_grad = unit_exchange(place_arg, pieces)

    return (
        mixed[None],
        tokens_grad[None],
        gain_sums[0],
        input_proj_grad,
        gelu_proj_grad,
        channel_sums[:4],
        channel_sums[4],
        decay_gate_grad,
        channel_sums[5],
        input_gate_grad,
        channel_sums[6],
        channel_sums[7],
        output_proj_grad,
        gain_sums[1],
        mlp_gate_grad,
        mlp_up_grad,
        mlp_down_grad,
    )


def choose_plan(mesh):
    devices, planes = mesh.shape["seq"], mesh.shape["fsdp"]

    def plan(*args):
        channels, width = args[6].shape[1], args[8].shape[1]
        if channels == width * devices and devices == 2 * planes and planes == 4:
            return narrow_shards(*args)
        return wide_shards(*args)

    return plan


def solution(mesh):
    return jax.shard_map(
        choose_plan(mesh),
        mesh=mesh,
        in_specs=(
            P("fsdp", "seq", None),
            P("fsdp", "seq", None),
            P("fsdp", None),
            P(),
            P("fsdp", None),
            P("fsdp", None),
            P(),
            P(),
            P("fsdp", None),
            P(),
            P("fsdp", None),
            P(),
            P(),
            P("fsdp", None),
            P(),
            P("fsdp", None),
            P("fsdp", None),
            P("fsdp", None),
        ),
        out_specs=(
            P("fsdp", "seq", None),
            P("fsdp", "seq", None),
            P(),
            P("fsdp", "seq"),
            P("fsdp", "seq"),
            P(),
            P(),
            P("fsdp", "seq"),
            P(),
            P("fsdp", "seq"),
            P(),
            P(),
            P("fsdp", "seq"),
            P(),
            P("fsdp", "seq"),
            P("fsdp", "seq"),
            P("fsdp", "seq"),
        ),
        check_vma=False,
    )
```

```python
import functools

import jax
import jax.numpy as jnp
from jax import lax
from jax.experimental import pallas as pl
from jax.experimental.pallas import tpu as pltpu
from jax.sharding import PartitionSpec as P

norm_eps = 1e-06
mult_floor = 0.0001


def from_behind(x, axis, by):
    devices = lax.axis_size(axis)
    pairs = [(i, i + by) for i in range(devices) if 0 <= i + by < devices]
    return lax.ppermute(x, axis, pairs)


def rms_scale(values, gain):
    scale = lax.rsqrt(jnp.mean(values * values, axis=-1, keepdims=True) + norm_eps)
    return values * scale * gain


def smooth_gelu(values):
    return jax.nn.gelu(values, approximate=True)


def gated_unit(gate, up_val):
    return smooth_gelu(gate) * up_val


def affine_pair(earlier, later):
    return (earlier[0] * later[0], earlier[1] * later[0] + later[1])


def decay_terms(conv_out, decay_pre, input_pre, decay_param, resets):
    log_a = -8.0 * jax.nn.sigmoid(decay_pre) * jax.nn.softplus(-decay_param)
    room = jnp.maximum(-jnp.expm1(2.0 * log_a), mult_floor)
    factor = jnp.where(resets, 1.0, jnp.sqrt(room))
    decay = jnp.where(resets, 0.0, jnp.exp(log_a))
    return (decay, jax.nn.sigmoid(input_pre) * conv_out * factor)


def conv_apply(extended, taps_w, bias, masks):
    taps = taps_w.shape[0]
    rows = masks.shape[1]
    total = jnp.zeros((rows, taps_w.shape[1]), jnp.float32) + bias
    for shift_k in range(taps):
        begin_row = taps - 1 - shift_k
        total = total + taps_w[shift_k] * extended[begin_row : begin_row + rows] * masks[shift_k]
    return total


def block_product(left, weight):
    width = weight.shape[1]
    blocks = weight.shape[0] // width
    result = jnp.einsum(
        "nhk,hkj->nhj",
        left.reshape(left.shape[0], blocks, width),
        weight.reshape(blocks, width, width),
        preferred_element_type=jnp.float32,
    )
    return result.reshape(left.shape[0], -1)


def block_back(grad, weight):
    width = weight.shape[1]
    blocks = weight.shape[0] // width
    result = jnp.einsum(
        "nhj,hkj->nhk",
        grad.reshape(grad.shape[0], blocks, width),
        weight.reshape(blocks, width, width),
        preferred_element_type=jnp.float32,
    )
    return result.reshape(grad.shape[0], -1)


def block_weight_grad(left, grad, width):
    blocks = left.shape[1] // width
    result = jnp.einsum(
        "nhk,nhj->hkj",
        left.reshape(left.shape[0], blocks, width),
        grad.reshape(grad.shape[0], blocks, width),
        preferred_element_type=jnp.float32,
    )
    return result.reshape(blocks * width, width)


def wide_shards(
    tokens,
    cotangent,
    doc_starts,
    mix_gain,
    input_proj,
    gelu_proj,
    conv_taps,
    conv_bias,
    decay_gate,
    decay_bias,
    input_gate,
    input_bias,
    decay_param,
    output_proj,
    mlp_gain,
    mlp_gate,
    mlp_up,
    mlp_down,
):
    rows = tokens.shape[1]
    taps = conv_taps.shape[0]
    width = decay_gate.shape[1]
    input_w, gelu_w, output_w, decay_w, inputg_w, gate_w, up_w, down_w = (
        lax.all_gather(input_proj, "fsdp", axis=0, tiled=True),
        lax.all_gather(gelu_proj, "fsdp", axis=0, tiled=True),
        lax.all_gather(output_proj, "fsdp", axis=0, tiled=True),
        lax.all_gather(decay_gate, "fsdp", axis=0, tiled=True),
        lax.all_gather(input_gate, "fsdp", axis=0, tiled=True),
        lax.all_gather(mlp_gate, "fsdp", axis=0, tiled=True),
        lax.all_gather(mlp_up, "fsdp", axis=0, tiled=True),
        lax.all_gather(mlp_down, "fsdp", axis=0, tiled=True),
    )
    channels = input_w.shape[1]
    first = lax.axis_index("seq") * rows
    positions = first + jnp.arange(rows, dtype=jnp.int32)
    starts = doc_starts[0]
    begin = jnp.max(jnp.where(starts[None, :] <= positions[:, None], starts[None, :], 0), axis=1)
    resets = (begin == positions)[:, None]
    masks = jnp.stack([(positions - k >= begin)[:, None] for k in range(taps)]).astype(jnp.float32)
    values = tokens[0].astype(jnp.float32)
    normed = rms_scale(values, mix_gain).astype(jnp.bfloat16)
    branch = jnp.dot(normed, input_w, preferred_element_type=jnp.float32).astype(jnp.bfloat16)
    gelu_pre = jnp.dot(normed, gelu_w, preferred_element_type=jnp.float32)
    gelu_out = smooth_gelu(gelu_pre)
    previous = from_behind(branch[rows - (taps - 1) :], "seq", 1)
    extended = jnp.concatenate([previous, branch], axis=0).astype(jnp.float32)
    conv_f = conv_apply(extended, conv_taps, conv_bias, masks).astype(jnp.bfloat16)
    conv_val = conv_f.astype(jnp.float32)
    decay_pre = block_product(conv_f, decay_w) + decay_bias
    input_pre = block_product(conv_f, inputg_w) + input_bias
    decay, driven = decay_terms(conv_val, decay_pre, input_pre, decay_param, resets)
    decay_cols, driven_cols = (
        lax.all_to_all(decay, "seq", split_axis=1, concat_axis=0, tiled=True),
        lax.all_to_all(driven, "seq", split_axis=1, concat_axis=0, tiled=True),
    )
    states_cols = lax.associative_scan(affine_pair, (decay_cols, driven_cols), axis=0)[1]
    states_low = lax.all_to_all(
        states_cols.astype(jnp.bfloat16), "seq", split_axis=0, concat_axis=1, tiled=True
    )
    states_val = states_low.astype(jnp.float32)
    merged = (states_val * gelu_out).astype(jnp.bfloat16)
    middle = values + jnp.dot(merged, output_w, preferred_element_type=jnp.float32)
    normed2 = rms_scale(middle, mlp_gain).astype(jnp.bfloat16)
    gate = jnp.dot(normed2, gate_w, preferred_element_type=jnp.float32)
    up_val = jnp.dot(normed2, up_w, preferred_element_type=jnp.float32)
    hidden = gated_unit(gate, up_val).astype(jnp.bfloat16)
    mixed = (middle + jnp.dot(hidden, down_w, preferred_element_type=jnp.float32)).astype(
        jnp.bfloat16
    )
    out_grad = cotangent[0]
    down_grad = jnp.einsum("tf,td->fd", hidden, out_grad, preferred_element_type=jnp.float32)
    hidden_grad = jnp.einsum("td,fd->tf", out_grad, down_w, preferred_element_type=jnp.float32)
    unit_pull = jax.vjp(gated_unit, gate, up_val)[1]
    gate_grad, up_grad = unit_pull(hidden_grad)
    gate_low = gate_grad.astype(jnp.bfloat16)
    up_low = up_grad.astype(jnp.bfloat16)
    gate_w_grad = jnp.einsum("td,tf->df", normed2, gate_low, preferred_element_type=jnp.float32)
    up_w_grad = jnp.einsum("td,tf->df", normed2, up_low, preferred_element_type=jnp.float32)
    mlp_terms = (
        lax.psum_scatter(gate_w_grad, "seq", scatter_dimension=1, tiled=True),
        lax.psum_scatter(up_w_grad, "seq", scatter_dimension=1, tiled=True),
        lax.psum_scatter(down_grad, "seq", scatter_dimension=1, tiled=True),
    )
    mlp_gate_grad, mlp_up_grad, mlp_down_grad = (
        lax.psum_scatter(mlp_terms[0], "fsdp", scatter_dimension=0, tiled=True),
        lax.psum_scatter(mlp_terms[1], "fsdp", scatter_dimension=0, tiled=True),
        lax.psum_scatter(mlp_terms[2], "fsdp", scatter_dimension=0, tiled=True),
    )
    normed2_grad = jnp.einsum(
        "tf,df->td", gate_low, gate_w, preferred_element_type=jnp.float32
    ) + jnp.einsum("tf,df->td", up_low, up_w, preferred_element_type=jnp.float32)
    norm2_pull = jax.vjp(rms_scale, middle, mlp_gain)[1]
    middle_part, mlp_gain_term = norm2_pull(normed2_grad)
    middle_grad = out_grad.astype(jnp.float32) + middle_part
    mixer_grad = middle_grad.astype(jnp.bfloat16)
    output_w_grad = jnp.einsum("tr,td->rd", merged, mixer_grad, preferred_element_type=jnp.float32)
    merged_grad = jnp.einsum("td,rd->tr", mixer_grad, output_w, preferred_element_type=jnp.float32)
    state_low = (merged_grad * gelu_out).astype(jnp.bfloat16)
    gelu_pull = jax.vjp(smooth_gelu, gelu_pre)[1]
    gelu_pre_low = gelu_pull(merged_grad * states_val)[0].astype(jnp.bfloat16)
    grad_cols = lax.all_to_all(state_low, "seq", split_axis=1, concat_axis=0, tiled=True).astype(
        jnp.float32
    )
    width_cols = grad_cols.shape[1]
    next_decay = jnp.concatenate([decay_cols[1:], jnp.zeros((1, width_cols), jnp.float32)], axis=0)
    carried = lax.associative_scan(affine_pair, (next_decay, grad_cols), reverse=True, axis=0)[1]
    prior = jnp.concatenate([jnp.zeros((1, width_cols), jnp.float32), states_cols[:-1]], axis=0)
    decay_grad, driven_grad = (
        lax.all_to_all(carried * prior, "seq", split_axis=0, concat_axis=1, tiled=True),
        lax.all_to_all(carried, "seq", split_axis=0, concat_axis=1, tiled=True),
    )
    terms_pull = jax.vjp(
        lambda conv_in, dpre, ipre, dparam: decay_terms(conv_in, dpre, ipre, dparam, resets),
        conv_val,
        decay_pre,
        input_pre,
        decay_param,
    )[1]
    gate_conv_grad, dpre_grad, ipre_grad, decay_param_term = terms_pull((decay_grad, driven_grad))
    dpre_low = dpre_grad.astype(jnp.bfloat16)
    ipre_low = ipre_grad.astype(jnp.bfloat16)
    decay_w_grad = block_weight_grad(conv_f, dpre_low, width)
    inputg_w_grad = block_weight_grad(conv_f, ipre_low, width)
    conv_grad = gate_conv_grad + block_back(dpre_low, decay_w) + block_back(ipre_low, inputg_w)
    conv_pull = jax.vjp(
        lambda ext, taps_w, bias: conv_apply(ext, taps_w, bias, masks),
        extended,
        conv_taps,
        conv_bias,
    )[1]
    extended_grad, taps_term, conv_bias_term = conv_pull(conv_grad)
    returned = from_behind(extended_grad[: taps - 1], "seq", -1)
    branch_grad = extended_grad[taps - 1 :] + jnp.concatenate(
        [jnp.zeros((rows - (taps - 1), channels), jnp.float32), returned], axis=0
    )
    branch_low = branch_grad.astype(jnp.bfloat16)
    input_w_grad = jnp.einsum("td,tr->dr", normed, branch_low, preferred_element_type=jnp.float32)
    gelu_w_grad = jnp.einsum("td,tr->dr", normed, gelu_pre_low, preferred_element_type=jnp.float32)
    mix_terms = (
        lax.psum_scatter(input_w_grad, "seq", scatter_dimension=1, tiled=True),
        lax.psum_scatter(gelu_w_grad, "seq", scatter_dimension=1, tiled=True),
        lax.psum_scatter(output_w_grad, "seq", scatter_dimension=1, tiled=True),
        lax.psum_scatter(decay_w_grad, "seq", scatter_dimension=1, tiled=True),
        lax.psum_scatter(inputg_w_grad, "seq", scatter_dimension=1, tiled=True),
    )
    input_proj_grad, gelu_proj_grad, output_proj_grad, decay_gate_grad, input_gate_grad = (
        lax.psum_scatter(mix_terms[0], "fsdp", scatter_dimension=0, tiled=True),
        lax.psum_scatter(mix_terms[1], "fsdp", scatter_dimension=0, tiled=True),
        lax.psum_scatter(mix_terms[2], "fsdp", scatter_dimension=0, tiled=True),
        lax.psum_scatter(mix_terms[3], "fsdp", scatter_dimension=0, tiled=True),
        lax.psum_scatter(mix_terms[4], "fsdp", scatter_dimension=0, tiled=True),
    )
    normed_grad = jnp.einsum(
        "tr,dr->td", branch_low, input_w, preferred_element_type=jnp.float32
    ) + jnp.einsum("tr,dr->td", gelu_pre_low, gelu_w, preferred_element_type=jnp.float32)
    norm1_pull = jax.vjp(rms_scale, values, mix_gain)[1]
    values_part, mix_gain_term = norm1_pull(normed_grad)
    tokens_grad = (middle_grad + values_part).astype(jnp.bfloat16)
    (
        mix_gain_grad,
        conv_taps_grad,
        conv_bias_grad,
        decay_bias_grad,
        input_bias_grad,
        decay_param_grad,
        mlp_gain_grad,
    ) = lax.psum(
        (
            mix_gain_term,
            taps_term,
            conv_bias_term,
            jnp.sum(dpre_low.astype(jnp.float32), axis=0),
            jnp.sum(ipre_low.astype(jnp.float32), axis=0),
            decay_param_term,
            mlp_gain_term,
        ),
        ("seq", "fsdp"),
    )
    return (
        mixed[None],
        tokens_grad[None],
        mix_gain_grad,
        input_proj_grad,
        gelu_proj_grad,
        conv_taps_grad,
        conv_bias_grad,
        decay_gate_grad,
        decay_bias_grad,
        input_gate_grad,
        input_bias_grad,
        decay_param_grad,
        output_proj_grad,
        mlp_gain_grad,
        mlp_gate_grad,
        mlp_up_grad,
        mlp_down_grad,
    )


def chip_swap(x, k):
    devices = lax.axis_size("seq")
    return lax.ppermute(x, "seq", [(i, i ^ (2 * k)) for i in range(devices)])


def core_swap(x):
    devices = lax.axis_size("seq")
    return lax.ppermute(x, "seq", [(i, i ^ 1) for i in range(devices)])


def gather_blocks(x):
    chips = lax.axis_size("seq") // 2
    near = jnp.stack([x] + [chip_swap(x, k) for k in range(1, chips)])
    return near, core_swap(near)


def tie(*arrays):
    return lax.optimization_barrier(arrays)


def pair_blocks(near, far, extra=None):
    if extra is None:
        extra = jnp.zeros((0, near.shape[2]), jnp.bfloat16)
    return payloads(near, core_swap(far), extra)


def spread_pairs(own, *low):
    return own, *[chip_swap(block, k + 1) for k, block in enumerate(low)]


def plane_swap(x, k):
    if k == 0:
        return x
    return lax.ppermute(x, "fsdp", [(i, i ^ k) for i in range(lax.axis_size("fsdp"))])


def exchange(x, chip, core, turn, beside):
    chips = x.shape[0]
    parts = [
        lax.dynamic_index_in_dim(x, chip ^ k ^ turn, 0, keepdims=False) for k in range(chips)
    ]
    got = [chip_swap(parts[k], k) for k in range(1, chips)]
    got[0], *beside = tie(got[0], *beside)
    got = jnp.stack([parts[0], *got])
    keep = lax.dynamic_index_in_dim(got, core, 1, keepdims=False)
    give = lax.dynamic_index_in_dim(got, 1 - core, 1, keepdims=False)
    return keep, core_swap(give), *beside


def over_planes(x):
    planes = lax.axis_size("fsdp")
    total = x
    for k in range(1, planes):
        got = lax.ppermute(x.astype(jnp.bfloat16), "fsdp", [(i, i ^ k) for i in range(planes)])
        total = total + got.astype(jnp.float32)
    return total


little = pl.CostEstimate(flops=0, bytes_accessed=0, transcendentals=0)


def gelu_parts(v):
    root = 0.7978845608028654
    square = v * v
    h = 0.5 + 0.5 * jnp.tanh(v * (root + root * 0.044715 * square))
    value = v * h
    return value, h + value * (1.0 - h) * (2.0 * root + root * 0.26829 * square)


def sigmoid(v):
    return 1.0 / (1.0 + jnp.exp(-v))


def one_less_exp(v):
    series = -v * (1.0 + v * (0.5 + v * (1.0 / 6.0 + v * (1.0 / 24.0 + v * (1.0 / 120.0)))))
    return jnp.where(v > -0.1, series, 1.0 - jnp.exp(v))


def dot_nn(a, b):
    return lax.dot_general(a, b, (((1,), (0,)), ((), ())), preferred_element_type=jnp.float32)


def dot_nt(a, b):
    return lax.dot_general(a, b, (((1,), (1,)), ((), ())), preferred_element_type=jnp.float32)


def dot_tn(a, b):
    return lax.dot_general(a, b, (((0,), (0,)), ((), ())), preferred_element_type=jnp.float32)


def scan_rows(a, b, carry, later):
    rows = a.shape[0]
    group = 8
    row = lax.broadcasted_iota(jnp.int32, a.shape, 0) % group
    step = 1
    while step < group:
        turn = rows - step if later else step
        there = (row < group - step) if later else (row >= step)
        a_next = jnp.where(there, pltpu.roll(a, turn, 0), 1.0)
        b_next = jnp.where(there, pltpu.roll(b, turn, 0), 0.0)
        b = a * b_next + b
        a = a * a_next
        step *= 2
    starts = list(range(0, rows, group))
    done = {}
    for start in reversed(starts) if later else starts:
        states = a[start : start + group] * carry + b[start : start + group]
        done[start] = states
        carry = states[:1] if later else states[group - 1 :]
    return jnp.concatenate([done[start] for start in starts], axis=0)


def in_time(value, core):
    rows = value.shape[0] // 2
    near, far = value[:rows], value[rows:]
    odd = core == 1
    return jnp.concatenate([jnp.where(odd, far, near), jnp.where(odd, near, far)], axis=0)


def by_core(value, ref, core):
    rows = value.shape[0] // 2
    first, second = value[:rows], value[rows:]
    odd = core == 1
    ref[0] = jnp.where(odd, second, first).astype(ref.dtype)
    ref[1] = jnp.where(odd, first, second).astype(ref.dtype)


def tables_kernel(starts_ref, taps_ref, conv_ref, decay_ref, input_ref, param_ref, chan_ref, age_ref):
    chan_ref[...] = jnp.zeros_like(chan_ref)
    chan_ref[0:4, :] = taps_ref[...]
    chan_ref[4:5, :] = conv_ref[...]
    chan_ref[5:6, :] = decay_ref[...]
    chan_ref[6:7, :] = input_ref[...]
    small = jnp.exp(-param_ref[...])
    series = small * (
        1.0
        - small * (1 / 2 - small * (1 / 3 - small * (1 / 4 - small * (1 / 5 - small * (1 / 6)))))
    )
    chan_ref[7:8, :] = jnp.where(small < 0.1, series, jnp.log(1.0 + small))
    chan_ref[8:9, :] = small / (1.0 + small)
    positions = lax.broadcasted_iota(jnp.int32, age_ref.shape, 0)
    begin = jnp.zeros(age_ref.shape, jnp.int32)
    for j in range(starts_ref.shape[0]):
        start = starts_ref[j]
        begin = jnp.maximum(begin, jnp.where(start <= positions, start, 0))
    age_ref[...] = (positions - begin).astype(jnp.float32)


def tables(starts, taps, conv_bias, decay_bias, input_bias, param, length):
    channels = taps.shape[1]
    whole = pl.BlockSpec(memory_space=pltpu.VMEM)
    return pl.pallas_call(
        tables_kernel,
        in_specs=[pl.BlockSpec(memory_space=pltpu.SMEM)] + [whole] * 5,
        out_specs=[whole] * 2,
        out_shape=[
            jax.ShapeDtypeStruct((16, channels), jnp.float32),
            jax.ShapeDtypeStruct((length, 1), jnp.float32),
        ],
        name="tables",
    )(starts, taps, conv_bias[None], decay_bias[None], input_bias[None], param[None])


def mix_forward_kernel(
    seq_ref,
    near_ref,
    far_ref,
    age_ref,
    chan_ref,
    keep_ref,
    got_ref,
    merged_ref,
    middle_near_ref,
    middle_far_ref,
    branch_ref,
    conv_ref,
    gelu_ref,
    gelu_grad_ref,
    decay_ref,
    input_ref,
    direct_ref,
    sig_ref,
    decay_grad_ref,
    weights_ref,
    extended,
    carry,
):
    place = seq_ref[0]
    chips = keep_ref.shape[0]
    step = pl.program_id(0)
    chip, core = place // 2, place % 2
    rows, width = branch_ref.shape
    model = middle_near_ref.shape[1]
    piece = keep_ref.shape[1]

    @pl.when(step == 0)
    def _():
        extended[pl.ds(0, 8), :] = jnp.zeros((8, width), jnp.float32)
        carry[...] = jnp.zeros_like(carry)
        for k in range(chips):
            home = pl.multiple_of(piece * 2 * (chip ^ k) + piece * core, piece)
            away = pl.multiple_of(piece * 2 * (chip ^ k) + piece * (1 - core), piece)
            weights_ref[pl.ds(home, piece), :] = keep_ref[k]
            weights_ref[pl.ds(away, piece), :] = got_ref[k]

    @pl.when(step > 0)
    def _():
        extended[pl.ds(0, 8), :] = extended[pl.ds(rows, 8), :]

    pre = in_time(jnp.concatenate([near_ref[...], far_ref[...]], axis=0), core)
    branch = pre[:, :width].astype(jnp.bfloat16)
    gelu_pre = pre[:, width:]
    branch_ref[...] = branch
    extended[pl.ds(8, rows), :] = branch.astype(jnp.float32)
    age = age_ref[...]
    total = jnp.zeros((rows, width), jnp.float32) + chan_ref[4:5, :]
    for k in range(4):
        shifted = extended[pl.ds(8 - k, rows), :]
        total = total + chan_ref[k : k + 1, :] * shifted * jnp.where(age >= k, 1.0, 0.0)
    conv_low = total.astype(jnp.bfloat16)
    conv = conv_low.astype(jnp.float32)
    conv_ref[...] = conv_low
    decay_pre = dot_nn(conv_low, weights_ref[:, model : model + width]) + chan_ref[5:6, :]
    input_pre = dot_nn(conv_low, weights_ref[:, model + width :]) + chan_ref[6:7, :]
    sig_d, sig_i = sigmoid(decay_pre), sigmoid(input_pre)
    soft = chan_ref[7:8, :]
    log_a = -8.0 * sig_d * soft
    reset = age < 0.5
    open_room = one_less_exp(2.0 * log_a)
    root = jnp.sqrt(jnp.maximum(open_room, mult_floor))
    factor = jnp.where(reset, 1.0, root)
    a = jnp.exp(log_a)
    decay = jnp.where(reset, 0.0, a)
    passed = sig_i * conv
    before = carry[0:1, :]
    states = scan_rows(decay, passed * factor, before, False)
    carry[0:1, :] = states[rows - 1 :, :]
    row = lax.broadcasted_iota(jnp.int32, states.shape, 0)
    prior = jnp.where(row == 0, before, pltpu.roll(states, 1, 0))
    low = states.astype(jnp.bfloat16).astype(jnp.float32)
    value, slope = gelu_parts(gelu_pre)
    by_core(low * value, merged_ref, core)
    product = dot_nn(merged_ref[...].reshape(rows, width), weights_ref[:, :model])
    middle_near_ref[...] = product[: rows // 2].astype(jnp.bfloat16)
    middle_far_ref[...] = product[rows // 2 :].astype(jnp.bfloat16)
    gelu_ref[...] = value
    gelu_grad_ref[...] = low * slope
    decay_ref[...] = decay
    input_ref[...] = passed * (1.0 - sig_i) * factor
    direct_ref[...] = sig_i * factor
    through_room = jnp.where(open_room > mult_floor, a * a * passed / root, 0.0)
    sig_grad = jnp.where(reset, 0.0, (prior * a - through_room) * sig_d)
    sig_ref[...] = sig_grad
    decay_grad_ref[...] = -8.0 * soft * (1.0 - sig_d) * sig_grad


def mix_forward(place, near, far, age, chan, keep, got):
    chips, rows, both = near.shape
    width = both // 2
    model = keep.shape[2] - both
    length = 2 * chips * rows
    chunk = 2 * rows
    columns = keep.shape[2]
    one_block = lambda i, s: (i ^ (s[0] // 2), 0, 0)
    time_block = lambda i, s: (i, 0)
    token_block = lambda i, s: (0, i ^ (s[0] // 2), 0, 0)
    saved = lambda dtype: jax.ShapeDtypeStruct((length, width), dtype)
    spec = pl.BlockSpec((chunk, width), time_block)
    fixed = lambda shape: pl.BlockSpec(shape, lambda i, s: (0,) * len(shape))
    return pl.pallas_call(
        mix_forward_kernel,
        grid_spec=pltpu.PrefetchScalarGridSpec(
            num_scalar_prefetch=1,
            grid=(chips,),
            in_specs=[
                pl.BlockSpec((None, rows, both), one_block),
                pl.BlockSpec((None, rows, both), one_block),
                pl.BlockSpec((chunk, 1), time_block),
                pl.BlockSpec((chan.shape[0], width), lambda i, s: (0, s[0])),
                fixed(keep.shape),
                fixed(got.shape),
            ],
            out_specs=[pl.BlockSpec((2, None, rows, width), token_block)]
            + [pl.BlockSpec((None, rows, model), one_block)] * 2
            + [spec] * 9
            + [fixed((width, columns))],
            scratch_shapes=[
                pltpu.VMEM((chunk + 8, width), jnp.float32),
                pltpu.VMEM((8, width), jnp.float32),
            ],
        ),
        out_shape=[
            jax.ShapeDtypeStruct((2, chips, rows, width), jnp.bfloat16),
            jax.ShapeDtypeStruct((chips, rows, model), jnp.bfloat16),
            jax.ShapeDtypeStruct((chips, rows, model), jnp.bfloat16),
            saved(jnp.bfloat16),
            saved(jnp.bfloat16),
        ]
        + [saved(jnp.float32)] * 7
        + [jax.ShapeDtypeStruct((width, columns), jnp.bfloat16)],
        compiler_params=pltpu.CompilerParams(vmem_limit_bytes=56 * 1024 * 1024),
        name="mix_forward",
    )(place, near, far, age, chan, keep, got)


def mix_backward_kernel(
    seq_ref,
    near_ref,
    far_ref,
    age_ref,
    chan_ref,
    weights_ref,
    in_ref,
    merged_ref,
    branch_ref,
    conv_ref,
    gelu_ref,
    gelu_grad_ref,
    decay_ref,
    input_ref,
    direct_ref,
    sig_ref,
    decay_grad_ref,
    both_ref,
    small_ref,
    back_near_ref,
    back_far_ref,
    *rest,
):
    place = seq_ref[0]
    chips = near_ref.shape[0]
    row_refs, (out_grad, gate_grads, ahead, carry) = rest[:chips], rest[chips:]
    step = pl.program_id(0)
    chip, core = place // 2, place % 2
    rows, width = branch_ref.shape
    model = near_ref.shape[-1]

    @pl.when(step == 0)
    def _():
        carry[...] = jnp.zeros_like(carry)
        ahead[:, pl.ds(rows, 8), :] = jnp.zeros((3, 8, width), jnp.float32)
        small_ref[...] = jnp.zeros_like(small_ref)
        gate_grads[...] = jnp.zeros_like(gate_grads)
        out_grad[...] = jnp.zeros_like(out_grad)

    @pl.when(step > 0)
    def _():
        ahead[:, pl.ds(rows, 8), :] = ahead[:, pl.ds(0, 8), :]

    turn = (chips - 1 - step) ^ chip
    mixer_grad = jnp.concatenate([near_ref[turn], far_ref[turn]], axis=0)
    merged_grad = in_time(dot_nt(mixer_grad, weights_ref[:, :model]), core)
    age = age_ref[...]
    out_grad[...] += dot_tn(mixer_grad, merged_ref[...].reshape(rows, width))
    state_grad = (merged_grad * gelu_ref[...]).astype(jnp.bfloat16).astype(jnp.float32)
    gelu_pre_grad = merged_grad * gelu_grad_ref[...]
    decay = decay_ref[...]
    conv_low = conv_ref[...]
    row = lax.broadcasted_iota(jnp.int32, (rows, width), 0)
    next_decay = jnp.where(row == rows - 1, carry[0:1, :], pltpu.roll(decay, rows - 1, 0))
    carried = scan_rows(next_decay, state_grad, carry[1:2, :], True)
    carry[0:1, :] = decay[0:1, :]
    carry[1:2, :] = carried[0:1, :]
    gate_conv_grad = carried * direct_ref[...]
    input_low = (carried * input_ref[...]).astype(jnp.bfloat16)
    decay_low = (carried * decay_grad_ref[...]).astype(jnp.bfloat16)
    sig_grad = carried * sig_ref[...]
    conv_grad = (
        gate_conv_grad
        + dot_nt(decay_low, weights_ref[:, model : model + width])
        + dot_nt(input_low, weights_ref[:, model + width :])
    )
    gate_grads[0] += dot_tn(decay_low, conv_low)
    gate_grads[1] += dot_tn(input_low, conv_low)
    branch = branch_ref[...].astype(jnp.float32)
    branch_grad = chan_ref[0:1, :] * conv_grad
    small_ref[0:1, :] += jnp.sum(conv_grad * branch, axis=0, keepdims=True)
    for k in range(1, 4):
        ahead[k - 1, pl.ds(0, rows), :] = conv_grad * jnp.where(age >= k, 1.0, 0.0)
        shifted = ahead[k - 1, pl.ds(k, rows), :]
        branch_grad = branch_grad + chan_ref[k : k + 1, :] * shifted
        small_ref[k : k + 1, :] += jnp.sum(shifted * branch, axis=0, keepdims=True)
    small_ref[4:5, :] += jnp.sum(conv_grad, axis=0, keepdims=True)
    small_ref[5:6, :] += jnp.sum(decay_low.astype(jnp.float32), axis=0, keepdims=True)
    small_ref[6:7, :] += jnp.sum(input_low.astype(jnp.float32), axis=0, keepdims=True)
    small_ref[7:8, :] += 8.0 * chan_ref[8:9, :] * jnp.sum(sig_grad, axis=0, keepdims=True)
    by_core(jnp.concatenate([branch_grad, gelu_pre_grad], axis=1), both_ref, core)
    both = both_ref[...].reshape(rows, 2 * width)
    back = dot_nt(both, in_ref[...].reshape(model, 2 * width)).astype(jnp.bfloat16)
    back_near_ref[...] = back[: rows // 2]
    back_far_ref[...] = back[rows // 2 :]

    @pl.when(step == chips - 1)
    def _():
        slim, piece = model // (2 * chips), width // (2 * chips)
        for k in range(chips):
            for e in range(2):
                target = 2 * (chip ^ k) + (core ^ e)
                rows = pl.ds(pl.multiple_of(target * slim, slim), slim)
                row_refs[k][e, pl.ds(0, slim), :] = out_grad[rows, :].astype(jnp.bfloat16)
                rows = pl.ds(pl.multiple_of(target * piece, piece), piece)
                for j in range(2):
                    row_refs[k][e, pl.ds(slim + j * piece, piece), :] = gate_grads[j, rows, :].astype(
                        jnp.bfloat16
                    )


def mix_backward(place, near, far, age, chan, weights, pack, merged, saved):
    planes, _, both = pack.shape
    chips, rows, model = near.shape
    width, columns = weights.shape
    tall = (model + 2 * width) // (2 * chips)
    chunk = 2 * rows
    last = chips - 1
    time_block = lambda i, s: (last - i, 0)
    token_block = lambda i, s: (0, (last - i) ^ (s[0] // 2), 0, 0)
    spec = pl.BlockSpec((chunk, width), time_block)
    back = pl.BlockSpec((None, rows, model), lambda i, s: ((last - i) ^ (s[0] // 2), 0, 0))
    fixed = lambda shape: pl.BlockSpec(shape, lambda i, s: (0,) * len(shape))
    return pl.pallas_call(
        mix_backward_kernel,
        grid_spec=pltpu.PrefetchScalarGridSpec(
            num_scalar_prefetch=1,
            grid=(chips,),
            in_specs=[
                fixed(near.shape),
                fixed(far.shape),
                pl.BlockSpec((chunk, 1), time_block),
                pl.BlockSpec((chan.shape[0], width), lambda i, s: (0, s[0])),
                fixed((width, columns)),
                fixed((planes, model // planes, both)),
                pl.BlockSpec((2, None, rows, width), token_block),
            ]
            + [spec] * 9,
            out_specs=[
                pl.BlockSpec((2, None, rows, 2 * width), token_block),
                fixed((8, width)),
                back,
                back,
            ]
            + [fixed((2, tall, width))] * chips,
            scratch_shapes=[
                pltpu.VMEM((model, width), jnp.float32),
                pltpu.VMEM((2, width, width), jnp.float32),
                pltpu.VMEM((3, chunk + 8, width), jnp.float32),
                pltpu.VMEM((8, width), jnp.float32),
            ],
        ),
        out_shape=[
            jax.ShapeDtypeStruct((2, chips, rows, 2 * width), jnp.bfloat16),
            jax.ShapeDtypeStruct((8, width), jnp.float32),
            jax.ShapeDtypeStruct(near.shape, jnp.bfloat16),
            jax.ShapeDtypeStruct(near.shape, jnp.bfloat16),
        ]
        + [jax.ShapeDtypeStruct((2, tall, width), jnp.bfloat16)] * chips,
        compiler_params=pltpu.CompilerParams(vmem_limit_bytes=50 * 1024 * 1024),
        cost_estimate=pl.CostEstimate(
            flops=10**9, bytes_accessed=24 * 10**6, transcendentals=0
        ),
        name="mix_backward",
    )(place, near, far, age, chan, weights, pack, merged, *saved)


def unit_kernel(
    near_ref,
    far_ref,
    cot_near_ref,
    cot_far_ref,
    pack_ref,
    back_near_out,
    back_far_out,
    mixed_near_out,
    mixed_far_out,
    grads_out,
    normed,
    cot,
    gate_up,
    down,
    pair,
    hidden,
    pair_t,
    hidden_t,
    grads,
    back,
    mixed,
    in_sems,
    out_sems,
):
    bf16 = jnp.bfloat16
    chips, rows, _ = near_ref.shape
    planes, tall, near_model = pack_ref.shape
    both = pair.shape[1]
    part = both // 2
    span = part // planes
    side = near_model // 2
    spare = down.shape[0] - part
    half = chips * rows
    incoming, outgoing = [], []

    def fetch(source, target):
        copy = pltpu.make_async_copy(source, target, in_sems.at[len(incoming)])
        copy.start()
        incoming.append(copy)
        return copy

    def send(source, target):
        copy = pltpu.make_async_copy(source, target, out_sems.at[len(outgoing)])
        copy.start()
        outgoing.append(copy)

    def fetch_half(source, target, i):
        return [
            fetch(source.at[k], target.at[pl.ds(i * half + k * rows, rows), :]) for k in range(chips)
        ]

    gate_up_copies = [
        fetch(
            pack_ref.at[z, pl.ds(j * near_model, near_model), :],
            gate_up.at[pl.ds(z * near_model, near_model), pl.ds(j * near_model, near_model)],
        )
        for z in range(planes)
        for j in range(3)
    ]
    normed_copies = [fetch_half(near_ref, normed, 0)]
    down_copies = [
        fetch(
            pack_ref.at[z, pl.ds(3 * near_model + j * span, span), :],
            down.at[pl.ds(z * span, span), pl.ds(j * near_model, near_model)],
        )
        for z in range(planes)
        for j in range(planes)
    ]
    cot_copies = [fetch_half(cot_near_ref, cot, 0)]
    for copy in gate_up_copies + normed_copies[0]:
        copy.wait()
    normed_copies.append(fetch_half(far_ref, normed, 1))
    cot_copies.append(fetch_half(cot_far_ref, cot, 1))
    chunk = 2 * rows
    first_unit, mid_unit, last_unit = (pl.ds(j * near_model, near_model) for j in range(3))
    for i in range(chips):
        here = pl.ds(i * chunk, chunk)
        if i * chunk == half:
            for copy in normed_copies[1] + cot_copies[1]:
                copy.wait()
        pre = dot_nn(normed[here, :], gate_up[...])
        if i == 0:
            for copy in down_copies + cot_copies[0]:
                copy.wait()
            down[pl.ds(part, spare), :] = jnp.zeros((spare, down.shape[1]), bf16)
        above = dot_nt(cot[here, :], down[...])
        up = pre[:, 2 * near_model :]
        value, slope = gelu_parts(pre[:, :near_model])
        grad = above[:, :near_model]
        hidden[here, first_unit] = (value * up).astype(bf16)
        pair[here, first_unit] = (grad * up * slope).astype(bf16)
        pair[here, last_unit] = (grad * value).astype(bf16)
        mid = pre[:, near_model : 2 * near_model]
        broad = side + spare
        up = pltpu.roll(mid, side, 1)[:, :broad]
        value, slope = gelu_parts(mid[:, :broad])
        grad = above[:, near_model:]
        hidden[here, pl.ds(near_model, side)] = (value * up)[:, :side].astype(bf16)
        left, right = grad * up * slope, grad * value
        left = jnp.concatenate([left, left[:, : near_model - broad]], axis=1)
        right = jnp.concatenate([right, right[:, : near_model - broad]], axis=1)
        lane = lax.broadcasted_iota(jnp.int32, left.shape, 1)
        pair[here, mid_unit] = jnp.where(lane < side, left, pltpu.roll(right, side, 1)).astype(bf16)
        pair_t[:, here] = pair[here, :].T
        hidden_t[:, here] = hidden[here, :].T
    def unit_rows(start):
        pieces, stop = [], start + span
        if start < near_model:
            pieces.append((2 * near_model + start, min(stop, near_model) - start))
        if stop > near_model:
            first = max(start, near_model)
            pieces.append((part + first - near_model, stop - first))
        return pieces

    for first_z in range(0, planes, 2):
        here = pl.ds(first_z * near_model, 2 * near_model)
        grad = dot_nn(hidden_t[...], cot[:, here]).astype(bf16)
        for z in (first_z, first_z + 1):
            columns = slice((z - first_z) * near_model, (z - first_z + 1) * near_model)
            for j in range(planes):
                grads[j, pl.ds((3 * z + 2) * span, span), :] = grad[
                    j * span : (j + 1) * span, columns
                ]
    for first_z in range(0, planes, 2):
        here = pl.ds(first_z * near_model, 2 * near_model)
        grad = dot_nn(pair_t[...], normed[:, here]).astype(bf16)
        for z in (first_z, first_z + 1):
            columns = slice((z - first_z) * near_model, (z - first_z + 1) * near_model)
            for j in range(planes):
                row = 3 * j * span
                grads[z, pl.ds(row, span), :] = grad[j * span : (j + 1) * span, columns]
                row += span
                for first, count in unit_rows(j * span):
                    grads[z, pl.ds(row, count), :] = grad[first : first + count, columns]
                    row += count
            send(grads.at[z], grads_out.at[z])
    for i, out in ((0, mixed_near_out), (1, mixed_far_out)):
        here = pl.ds(i * half, half)
        mixed[here, :] = dot_nn(hidden[here, :], down[pl.ds(0, part), :]).astype(bf16)
        for k in range(chips):
            send(mixed.at[pl.ds(i * half + k * rows, rows), :], out.at[k])
    for i, out in ((1, back_far_out), (0, back_near_out)):
        for k in range(0, chips, 2):
            first_row = i * half + k * rows
            here = pl.ds(first_row, chunk)
            back[here, :] = dot_nt(pair[here, :], gate_up[...]).astype(bf16)
            for e in range(2):
                send(back.at[pl.ds(first_row + e * rows, rows), :], out.at[k + e])
    for copy in outgoing:
        copy.wait()


def unit_back_and_forth(near, far, cot_near, cot_far, pack, part):
    chips, rows, model = near.shape
    length = 2 * chips * rows
    planes, _, near_model = pack.shape
    bf16 = jnp.bfloat16
    there = pl.BlockSpec(memory_space=pl.ANY)
    return pl.pallas_call(
        unit_kernel,
        in_specs=[there] * 5,
        out_specs=[there] * 5,
        scratch_shapes=[
            pltpu.VMEM((length, model), bf16),
            pltpu.VMEM((length, model), bf16),
            pltpu.VMEM((model, 2 * part), bf16),
            pltpu.VMEM((pl.cdiv(part, 128) * 128, model), bf16),
            pltpu.VMEM((length, 2 * part), bf16),
            pltpu.VMEM((length, part), bf16),
            pltpu.VMEM((2 * part, length), bf16),
            pltpu.VMEM((part, length), bf16),
            pltpu.VMEM(pack.shape, bf16),
            pltpu.VMEM((length, model), bf16),
            pltpu.VMEM((length, model), bf16),
            pltpu.SemaphoreType.DMA((4 * chips + planes * (3 + planes),)),
            pltpu.SemaphoreType.DMA((4 * chips + planes,)),
        ],
        out_shape=[jax.ShapeDtypeStruct(near.shape, bf16)] * 4
        + [jax.ShapeDtypeStruct(pack.shape, bf16)],
        compiler_params=pltpu.CompilerParams(vmem_limit_bytes=58 * 1024 * 1024),
        name="unit_back_and_forth",
    )(near, far, cot_near, cot_far, pack)


def mix_pack_kernel(
    place_ref, input_ref, gelu_ref, out_ref, decay_ref, gate_ref, in_own_ref, rows_ref
):
    width, model = input_ref.shape[1], out_ref.shape[2]
    in_own_ref[:, pl.ds(0, width)] = input_ref[...]
    in_own_ref[:, pl.ds(width, width)] = gelu_ref[...]
    rows_ref[:, :, pl.ds(0, model)] = out_ref[...]
    rows_ref[:, :, pl.ds(model, width)] = decay_ref[...]
    rows_ref[:, :, pl.ds(model + width, width)] = gate_ref[...]


def own_mix_pack(place, input_proj, gelu_proj, output_proj, decay_gate, input_gate):
    near_model, channels = input_proj.shape
    width = decay_gate.shape[1]
    heads = decay_gate.shape[0] // width
    model = output_proj.shape[1]
    piece = width // (channels // width)
    mine = pl.BlockSpec((near_model, width), lambda i, s: (0, s[0]))
    rows = lambda columns: pl.BlockSpec((heads, piece, columns), lambda i, s: (0, s[0], 0))
    shapes = [(near_model, 2 * width), (heads, piece, model + 2 * width)]
    return pl.pallas_call(
        mix_pack_kernel,
        grid_spec=pltpu.PrefetchScalarGridSpec(
            num_scalar_prefetch=1,
            grid=(1,),
            in_specs=[mine, mine, rows(model), rows(width), rows(width)],
            out_specs=[
                pl.BlockSpec(shape, lambda i, s, zeros=(0,) * len(shape): zeros) for shape in shapes
            ],
        ),
        out_shape=[jax.ShapeDtypeStruct(shape, input_proj.dtype) for shape in shapes],
        name="own_mix_pack",
    )(
        place,
        input_proj,
        gelu_proj,
        output_proj.reshape(heads, width, model),
        decay_gate.reshape(heads, width, width),
        input_gate.reshape(heads, width, width),
    )


def unit_pack_kernel(place_ref, gate_ref, up_ref, down_ref, pack_ref, windows, sems):
    place = place_ref[0]
    near_model, deep = gate_ref.shape
    planes = windows.shape[1]
    tile = 128
    span = (pack_ref.shape[0] - 3 * near_model) // planes
    extra = span - tile
    copies = []

    def fetch(source, target):
        copies.append(pltpu.make_async_copy(source, target, sems.at[len(copies)]))
        copies[-1].start()

    for i, ref in enumerate((gate_ref, up_ref)):
        for z in range(planes):
            start = pl.multiple_of(z * (deep // planes) + place * tile, tile)
            fetch(ref.at[:, pl.ds(start, 2 * tile)], windows.at[i, z])
    rows = pl.ds(pl.multiple_of(place * span, 16), span)
    for j in range(planes):
        fetch(
            down_ref.at[rows, pl.ds(j * near_model, near_model)],
            pack_ref.at[pl.ds(3 * near_model + j * span, span), :],
        )
    lane = lax.broadcasted_iota(jnp.int32, (near_model, tile), 1)

    def tiles(i):
        parts = []
        for z in range(planes):
            copies[i * planes + z].wait()
            turn = lax.rem((z - place) * extra + 2 * tile, 2 * tile)
            parts.append(pltpu.roll(windows[i, z].astype(jnp.float32), turn, 1))
        found = [parts[0][:, :tile]]
        for z in range(1, planes):
            found.append(jnp.where(lane < z * extra, parts[z - 1][:, tile:], parts[z][:, :tile]))
        return found + [parts[planes - 1][:, tile:]]

    gate, up = tiles(0), tiles(1)
    half = tile // 2
    turned = [pltpu.roll(up[j], half, 1) for j in (3, 4)]
    mid = [
        gate[3],
        jnp.where(lane < half, gate[4], turned[0]),
        jnp.where(lane < half, turned[0], turned[1]),
    ]
    for block, found in enumerate((gate[:3], mid, up[:3])):
        for j in range(3):
            pack_ref[pl.ds(block * near_model, near_model), pl.ds(j * tile, tile)] = found[
                j
            ].astype(pack_ref.dtype)
    for copy in copies[2 * planes :]:
        copy.wait()


def own_unit_pack(place, mlp_gate, mlp_up, mlp_down, planes, span):
    near_model = mlp_gate.shape[0]
    tall = 3 * near_model + planes * span
    there = pl.BlockSpec(memory_space=pl.ANY)
    return pl.pallas_call(
        unit_pack_kernel,
        grid_spec=pltpu.PrefetchScalarGridSpec(
            num_scalar_prefetch=1,
            grid=(1,),
            in_specs=[there] * 3,
            out_specs=pl.BlockSpec((tall, near_model), lambda i, s: (0, 0)),
            scratch_shapes=[
                pltpu.VMEM((2, planes, near_model, 256), mlp_gate.dtype),
                pltpu.SemaphoreType.DMA((3 * planes,)),
            ],
        ),
        out_shape=jax.ShapeDtypeStruct((tall, near_model), mlp_gate.dtype),
        compiler_params=pltpu.CompilerParams(vmem_limit_bytes=48 * 1024 * 1024),
        cost_estimate=pl.CostEstimate(flops=0, bytes_accessed=5 << 20, transcendentals=0),
        name="own_unit_pack",
    )(place, mlp_gate, mlp_up, mlp_down)


def in_grads_kernel(
    place_ref,
    near_ref,
    far_ref,
    both_ref,
    back_near_ref,
    back_far_ref,
    gain_ref,
    later_gain_ref,
    small_ref,
    grads_ref,
    sums_ref,
):
    place = place_ref[0]
    chips, rows, model = near_ref.shape
    planes, near_model, _ = grads_ref.shape
    taken, width = small_ref.shape
    near = near_ref[...].reshape(chips * rows, model)
    far = far_ref[...].reshape(chips * rows, model)
    for z in range(planes):
        here = slice(z * near_model, (z + 1) * near_model)
        total = dot_tn(near[:, here], both_ref[0].reshape(chips * rows, -1))
        total = total + dot_tn(far[:, here], both_ref[1].reshape(chips * rows, -1))
        grads_ref[z] = total.astype(grads_ref.dtype)
    gain_sum = jnp.zeros((1, model), jnp.float32)
    for ref, back_ref in ((near_ref, back_near_ref), (far_ref, back_far_ref)):
        for k in range(chips):
            product = ref[k].astype(jnp.float32) * back_ref[k].astype(jnp.float32)
            gain_sum = gain_sum + jnp.sum(product, axis=0, keepdims=True)
    sums_ref[...] = jnp.zeros_like(sums_ref)
    across = model // width
    row = pl.multiple_of(taken * (place // across), taken)
    column = pl.multiple_of(width * lax.rem(place, across), width)
    sums_ref[pl.ds(row, taken), pl.ds(column, width)] = small_ref[...]
    band = model // 3
    for j in range(3):
        here = slice(j * band, (j + 1) * band)
        sums_ref[pl.ds(taken + j, 1), pl.ds(band, band)] = gain_sum[:, here] / gain_ref[:, here]
        sums_ref[pl.ds(taken + 3 + j, 1), pl.ds(band, band)] = later_gain_ref[:, here]


def in_grads(place, near, far, both, back_near, back_far, gain, later_gain, small, planes):
    chips, rows, model = near.shape
    columns = both.shape[-1]
    whole = lambda shape: pl.BlockSpec(shape, lambda i, s: (0,) * len(shape))
    inputs = (near, far, both, back_near, back_far, gain[None], later_gain, small)
    shapes = [
        jax.ShapeDtypeStruct((planes, model // planes, columns), jnp.bfloat16),
        jax.ShapeDtypeStruct((16, model), jnp.float32),
    ]
    return pl.pallas_call(
        in_grads_kernel,
        grid_spec=pltpu.PrefetchScalarGridSpec(
            num_scalar_prefetch=1,
            grid=(1,),
            in_specs=[whole(x.shape) for x in inputs],
            out_specs=[whole(x.shape) for x in shapes],
        ),
        out_shape=shapes,
        compiler_params=pltpu.CompilerParams(vmem_limit_bytes=24 * 1024 * 1024),
        name="in_grads",
    )(place, *inputs)


def payload_kernel(*refs):
    near_ref, got_ref, *extra_refs = refs[: -near_count(refs)]
    own_ref, *out_refs = refs[-near_count(refs) :]
    chips, rows, _ = near_ref.shape
    for k in range(chips):
        total = near_ref[k].astype(jnp.float32) + got_ref[k].astype(jnp.float32)
        if k == 0:
            own_ref[...] = total
        else:
            out_refs[k - 1][pl.ds(0, rows), :] = total.astype(jnp.bfloat16)
            for ref in extra_refs:
                out_refs[k - 1][pl.ds(rows, ref.shape[0]), :] = ref[...]


def near_count(refs):
    return refs[0].shape[0]


def payloads(near, got, extra):
    chips, rows, model = near.shape
    tall = rows + extra.shape[0]
    whole = pl.BlockSpec(memory_space=pltpu.VMEM)
    inputs = (near, got) + ((extra,) if extra.shape[0] else ())
    return pl.pallas_call(
        payload_kernel,
        in_specs=[whole] * len(inputs),
        out_specs=[whole] * chips,
        out_shape=[jax.ShapeDtypeStruct((rows, model), jnp.float32)]
        + [jax.ShapeDtypeStruct((tall, model), jnp.bfloat16)] * (chips - 1),
        compiler_params=pltpu.CompilerParams(vmem_limit_bytes=20 * 1024 * 1024),
        cost_estimate=little,
        name="payloads",
    )(*inputs)


def middle_kernel(tokens_ref, gain_ref, *refs):
    *parts, middle_ref, normed_ref = refs
    total = tokens_ref[...].astype(jnp.float32)
    for ref in parts:
        total = total + ref[...].astype(jnp.float32)
    middle_ref[...] = total
    scale = lax.rsqrt(jnp.mean(total * total, axis=-1, keepdims=True) + norm_eps)
    normed_ref[...] = (total * scale * gain_ref[...]).astype(jnp.bfloat16)


def middle_and_normed(tokens, gain, parts):
    rows, model = tokens.shape
    whole = pl.BlockSpec(memory_space=pltpu.VMEM)
    return pl.pallas_call(
        middle_kernel,
        in_specs=[whole] * (2 + len(parts)),
        out_specs=[whole] * 2,
        out_shape=[
            jax.ShapeDtypeStruct((rows, model), jnp.float32),
            jax.ShapeDtypeStruct((rows, model), jnp.bfloat16),
        ],
        cost_estimate=little,
        name="middle_and_normed",
    )(tokens, gain[None], *parts)


def middle_back_kernel(cot_ref, middle_ref, gain_ref, *refs):
    *parts, grad_ref, low_ref, gain_grad_ref = refs
    middle, gain = middle_ref[...], gain_ref[...]
    upper = parts[0][...]
    for ref in parts[1:]:
        upper = upper + ref[...].astype(jnp.float32)
    scale = lax.rsqrt(jnp.mean(middle * middle, axis=-1, keepdims=True) + norm_eps)
    gain_grad_ref[...] = jnp.sum(upper * middle * scale, axis=0, keepdims=True)
    scaled = gain * upper
    inner = jnp.mean(scaled * middle, axis=-1, keepdims=True)
    grad = cot_ref[...].astype(jnp.float32) + scale * scaled - middle * (scale * scale * scale) * inner
    grad_ref[...] = grad
    low_ref[...] = grad.astype(jnp.bfloat16)


def middle_back(cotangent, middle, gain, parts):
    rows, model = middle.shape
    whole = pl.BlockSpec(memory_space=pltpu.VMEM)
    return pl.pallas_call(
        middle_back_kernel,
        in_specs=[whole] * (3 + len(parts)),
        out_specs=[whole] * 3,
        out_shape=[
            jax.ShapeDtypeStruct((rows, model), jnp.float32),
            jax.ShapeDtypeStruct((rows, model), jnp.bfloat16),
            jax.ShapeDtypeStruct((1, model), jnp.float32),
        ],
        cost_estimate=little,
        name="middle_back",
    )(cotangent, middle, gain[None], *parts)


def halves(value, wanted):
    side = value.shape[1] // 2
    return jnp.where(wanted == 1, pltpu.roll(value, side, 1), value)


def unit_give_kernel(place_ref, *refs):
    *piece_refs, give_ref = refs
    place = place_ref[0]
    chip, core = place // 2, place % 2
    turn = core ^ (chip // 2)
    span = piece_refs[0].shape[0] // 3
    for e in range(2):
        first, second = (piece_refs[i][pl.ds(0, 2 * span), :] for i in (e, 2 + e))
        give_ref[pl.ds(2 * e * span, 2 * span), :] = jnp.where(turn == 0, second, first)
    for e in range(2):
        first, second = (
            halves(piece_refs[2 * e + i][pl.ds(2 * span, span), :].astype(jnp.float32), 1 - core)
            for i in range(2)
        )
        side = first.shape[1] // 2
        lane = lax.broadcasted_iota(jnp.int32, first.shape, 1)
        give_ref[pl.ds((4 + e) * span, span), :] = jnp.where(
            lane < side, first, pltpu.roll(second, side, 1)
        ).astype(give_ref.dtype)


def unit_finish_kernel(place_ref, *refs):
    *piece_refs, got_ref, gate_ref, up_ref, down_ref, down = refs
    place = place_ref[0]
    chip, core = place // 2, place % 2
    turn = core ^ (chip // 2)
    span = piece_refs[0].shape[0] // 3
    side = piece_refs[0].shape[1] // 2
    for e in range(2):
        first, second = (piece_refs[i][pl.ds(0, 2 * span), :] for i in (e, 2 + e))
        mine = jnp.where(turn == 0, first, second).astype(jnp.float32)
        away = got_ref[pl.ds(2 * e * span, 2 * span), :].astype(jnp.float32)
        column = 2 * ((chip % 2) ^ e)
        for value, at in ((mine, column + core), (away, column + 1 - core)):
            rows = pl.ds(pl.multiple_of(at * span, span), span)
            gate_ref[rows, :] = value[:span]
            up_ref[rows, :] = value[span:]
    for k in range(4):
        mine = halves(piece_refs[k][pl.ds(2 * span, span), :].astype(jnp.float32), core)
        away = halves(got_ref[pl.ds((4 + k // 2) * span, span), :].astype(jnp.float32), k % 2)
        for value, at in ((mine, core), (away, 1 - core)):
            row = pl.multiple_of((2 * (chip ^ k) + at) * span, span)
            down[pl.ds(row, span), :] = value[:, :side]
    down_ref[...] = down[...].T


def unit_pieces(total, chip):
    chips = total.shape[0]
    pieces = [
        lax.dynamic_index_in_dim(total, chip ^ k, 0, keepdims=False) for k in range(chips)
    ]
    return [pieces[0]] + [chip_swap(pieces[k], k) for k in range(1, chips)]


def unit_exchange(place, pieces):
    chips = len(pieces)
    tall, cols = pieces[0].shape
    span = tall // 3
    fixed = lambda shape: pl.BlockSpec(shape, lambda i, s: (0,) * len(shape))
    give = pl.pallas_call(
        unit_give_kernel,
        grid_spec=pltpu.PrefetchScalarGridSpec(
            num_scalar_prefetch=1,
            grid=(1,),
            in_specs=[fixed((tall, cols))] * chips,
            out_specs=fixed((6 * span, cols)),
        ),
        out_shape=jax.ShapeDtypeStruct((6 * span, cols), pieces[0].dtype),
        name="unit_give",
    )(place, *pieces)
    shapes = [(4 * span, cols), (4 * span, cols), (cols // 2, 2 * chips * span)]
    grads = pl.pallas_call(
        unit_finish_kernel,
        grid_spec=pltpu.PrefetchScalarGridSpec(
            num_scalar_prefetch=1,
            grid=(1,),
            in_specs=[fixed((tall, cols))] * chips + [fixed((6 * span, cols))],
            out_specs=[fixed(shape) for shape in shapes],
            scratch_shapes=[pltpu.VMEM((2 * chips * span, cols // 2), jnp.float32)],
        ),
        out_shape=[jax.ShapeDtypeStruct(shape, jnp.float32) for shape in shapes],
        compiler_params=pltpu.CompilerParams(vmem_limit_bytes=32 * 1024 * 1024),
        name="unit_finish",
    )(place, *pieces, core_swap(give))
    return [grad.T for grad in grads]


def grad_pack_kernel(place_ref, in_ref, *refs):
    *blocks, pack_ref = refs
    place = place_ref[0]
    chips = len(blocks) // 2
    chip, core = place // 2, place % 2
    near_model, both = in_ref.shape[1:]
    tall, width = blocks[0].shape
    pack_ref[:, pl.ds(0, near_model), :] = in_ref[...]
    for k in range(chips):
        home, away = blocks[k][...], blocks[chips + k][...]
        odd = core == 1
        pack_ref[chip ^ k, pl.ds(near_model, tall), pl.ds(0, width)] = jnp.where(odd, away, home)
        pack_ref[chip ^ k, pl.ds(near_model, tall), pl.ds(width, width)] = jnp.where(odd, home, away)


def grad_pack(place, in_grad, home, away):
    planes, near_model, both = in_grad.shape
    tall, width = home[0].shape
    return pl.pallas_call(
        grad_pack_kernel,
        grid_spec=pltpu.PrefetchScalarGridSpec(
            num_scalar_prefetch=1,
            grid=(1,),
            in_specs=[pl.BlockSpec(in_grad.shape, lambda i, s: (0, 0, 0))]
            + [pl.BlockSpec((tall, width), lambda i, s: (0, 0))] * (2 * len(home)),
            out_specs=pl.BlockSpec((planes, near_model + tall, both), lambda i, s: (0, 0, 0)),
        ),
        out_shape=jax.ShapeDtypeStruct((planes, near_model + tall, both), jnp.bfloat16),
        compiler_params=pltpu.CompilerParams(vmem_limit_bytes=16 * 1024 * 1024),
        name="grad_pack",
    )(place, in_grad, *home, *away)


def mix_results_kernel(sum_ref, *refs):
    row = 0
    width = sum_ref.shape[1] // 2
    for j, ref in enumerate(refs):
        rows = ref.shape[0]
        if j < 2:
            ref[...] = sum_ref[pl.ds(0, rows), pl.ds(j * width, width)].astype(jnp.float32)
            row = rows
        else:
            ref[...] = sum_ref[pl.ds(row, rows), :].astype(jnp.float32)
            row += rows


def mix_results(total, near_model, slim):
    tall, both = total.shape
    piece = (tall - near_model - slim) // 2
    shapes = [(near_model, both // 2)] * 2 + [(slim, both), (piece, both), (piece, both)]
    whole = pl.BlockSpec(memory_space=pltpu.VMEM)
    found = pl.pallas_call(
        mix_results_kernel,
        in_specs=[whole],
        out_specs=[whole] * len(shapes),
        out_shape=[jax.ShapeDtypeStruct(shape, jnp.float32) for shape in shapes],
        name="mix_results",
    )(total)
    return [*found[:2], *[grad.T for grad in found[2:]]]


def norm_back(values, scale, gain, grad):
    inner = jnp.mean(gain * grad * values, axis=-1, keepdims=True)
    return scale * gain * grad - values * (scale * scale * scale) * inner


def narrow_shards(
    tokens,
    cotangent,
    doc_starts,
    mix_gain,
    input_proj,
    gelu_proj,
    conv_taps,
    conv_bias,
    decay_gate,
    decay_bias,
    input_gate,
    input_bias,
    decay_param,
    output_proj,
    mlp_gain,
    mlp_gate,
    mlp_up,
    mlp_down,
):
    f32, bf16 = jnp.float32, jnp.bfloat16
    devices, planes = lax.axis_size("seq"), lax.axis_size("fsdp")
    chips = devices // 2
    place, plane = lax.axis_index("seq"), lax.axis_index("fsdp")
    chip, core = place // 2, place % 2
    rows, model = tokens.shape[1:]
    length = rows * devices
    channels = conv_taps.shape[1]
    width = decay_gate.shape[1]
    deep = mlp_gate.shape[1]
    heads = output_proj.shape[0] // width
    piece = width // devices
    span = deep // (planes * devices)
    part = deep // devices
    near_model = model // planes

    def along_fsdp(x):
        return lax.all_gather(x, "fsdp", axis=0, tiled=True)

    def columns(x, start, size):
        return lax.dynamic_slice_in_dim(x, start, size, axis=1)

    place_arg = place.astype(jnp.int32)[None]
    in_own, rowset = own_mix_pack(
        place_arg, input_proj, gelu_proj, output_proj, decay_gate, input_gate
    )
    in_own, rowset, tokens = tie(in_own, rowset, tokens)
    in_weights = lax.all_gather(in_own, "fsdp", axis=0)
    by_plane = [plane_swap(rowset, k) for k in range(planes)]

    values = tokens[0].astype(f32)
    scale1 = lax.rsqrt(jnp.mean(values * values, axis=-1, keepdims=True) + norm_eps)
    normed_own, mlp_gate, mlp_up, mlp_down = tie(
        (values * scale1 * mix_gain).astype(bf16), mlp_gate, mlp_up, mlp_down
    )
    normed_near, normed_far = gather_blocks(normed_own)
    unit_pack = own_unit_pack(place_arg, mlp_gate, mlp_up, mlp_down, planes, span)
    unit_pack, normed_near, normed_far = tie(unit_pack, normed_near, normed_far)
    unit_pack = lax.all_gather(unit_pack, "fsdp", axis=0)
    chan, age = tables(
        doc_starts[0], conv_taps, conv_bias, decay_bias, input_bias, decay_param, length
    )
    normed_near, normed_far, out_grad = tie(normed_near, normed_far, cotangent[0])
    cot_got = [chip_swap(out_grad, k) for k in range(1, chips)]
    held = tie(normed_near, normed_far, chan, age, *by_plane, *cot_got)
    normed_near, normed_far, chan, age = held[:4]
    by_plane, cot_got = held[4 : 4 + planes], held[4 + planes :]

    pre_near, pre_far = (
        dot_nn(x.reshape(-1, model), in_weights.reshape(model, 2 * width)).reshape(
            chips, rows, 2 * width
        )
        for x in (normed_near, normed_far)
    )
    keep, got, pre_near, pre_far = exchange(
        jnp.stack(by_plane), chip, core, plane, [pre_near, pre_far]
    )
    merged, middle_near, middle_far, *saved, weights = mix_forward(
        place_arg, pre_near, pre_far, age, chan, keep, got
    )
    cot_near = jnp.stack([out_grad, *cot_got])
    cot_far = core_swap(cot_near)
    middle, normed2 = middle_and_normed(
        tokens[0], mlp_gain, spread_pairs(*pair_blocks(middle_near, middle_far))
    )

    near, far = gather_blocks(normed2)
    back_near, back_far, mixed_near, mixed_far, unit_grads = unit_back_and_forth(
        near, far, cot_near, cot_far, unit_pack, part
    )
    unit_sum = lax.psum_scatter(unit_grads, "fsdp", scatter_dimension=0, tiled=False)

    middle_grad, middle_low, mlp_gain_term = middle_back(
        out_grad, middle, mlp_gain, spread_pairs(*pair_blocks(back_near, back_far))
    )
    middle_low, mixed_near, mixed_far = tie(middle_low, mixed_near, mixed_far)
    mixed_own, *mixed_low = pair_blocks(mixed_near, mixed_far)
    first, *others = [chip_swap(middle_low, k) for k in range(1, chips)]
    first, mixed_own, *mixed_low = tie(first, mixed_own, *mixed_low)
    near = jnp.stack([middle_low, first, *others])
    far = core_swap(near)

    both, small, back_near, back_far, *by_chip = mix_backward(
        place_arg, near, far, age, chan, weights, in_weights, merged, saved
    )
    mixed_got = [chip_swap(block, k + 1) for k, block in enumerate(mixed_low)]
    held = tie(*mixed_got, *by_chip)
    mixed_got, by_chip = held[: chips - 1], held[chips - 1 :]
    arrived = [by_chip[0]] + [chip_swap(by_chip[k], k) for k in range(1, chips)]
    arrived[1], both, back_near, back_far, small = tie(
        arrived[1], both, back_near, back_far, small
    )
    in_pack, sums = in_grads(
        place_arg,
        normed_near,
        normed_far,
        both,
        back_near,
        back_far,
        mix_gain,
        mlp_gain_term,
        small,
        planes,
    )
    sums = sums + core_swap(sums)
    *arrived, in_pack = tie(*arrived, in_pack)
    away = core_swap(jnp.stack([block[1] for block in arrived]))
    pack, unit_sum, back_near, back_far, *mixed_got = tie(
        grad_pack(
            place_arg,
            in_pack,
            [block[0] for block in arrived],
            [away[k] for k in range(chips)],
        ),
        unit_sum,
        back_near,
        back_far,
        *mixed_got,
    )
    normed_own, *normed_low = pair_blocks(back_near, back_far)
    mixed = mixed_own
    for got in mixed_got:
        mixed = mixed + got.astype(f32)
    mixed = (middle + mixed).astype(bf16)
    mix_sum = lax.psum_scatter(pack, "fsdp", scatter_dimension=0, tiled=False)
    (
        input_proj_grad,
        gelu_proj_grad,
        output_proj_grad,
        decay_gate_grad,
        input_gate_grad,
    ) = mix_results(mix_sum, near_model, model // devices)

    pieces = unit_pieces(unit_sum.reshape(planes, 3 * span, near_model), chip)
    pieces[1], sums, *normed_low = tie(pieces[1], sums, *normed_low)
    normed_grad = normed_own
    for k in range(1, chips):
        normed_grad = normed_grad + chip_swap(normed_low[k - 1], k).astype(f32)
    values_part = norm_back(values, scale1, mix_gain, normed_grad)
    tokens_grad = (middle_grad + values_part).astype(bf16)

    low = sums.astype(bf16)
    for k in range(1, chips):
        sums = sums + chip_swap(low, k).astype(f32)
    sums = over_planes(sums)
    sums, *pieces = tie(sums, *pieces)
    channel_sums = jnp.concatenate([sums[:8], sums[8:, : channels - model]], axis=1)
    band = model // 3
    gain_sums = sums[8:14, band : 2 * band].reshape(2, model)
    mlp_gate_grad, mlp_up_grad, mlp_down_grad = unit_exchange(place_arg, pieces)

    return (
        mixed[None],
        tokens_grad[None],
        gain_sums[0],
        input_proj_grad,
        gelu_proj_grad,
        channel_sums[:4],
        channel_sums[4],
        decay_gate_grad,
        channel_sums[5],
        input_gate_grad,
        channel_sums[6],
        channel_sums[7],
        output_proj_grad,
        gain_sums[1],
        mlp_gate_grad,
        mlp_up_grad,
        mlp_down_grad,
    )


def choose_plan(mesh):
    devices, planes = mesh.shape["seq"], mesh.shape["fsdp"]

    def plan(*args):
        channels, width = args[6].shape[1], args[8].shape[1]
        if channels == width * devices and devices == 2 * planes and planes == 4:
            return narrow_shards(*args)
        return wide_shards(*args)

    return plan


def solution(mesh):
    return jax.shard_map(
        choose_plan(mesh),
        mesh=mesh,
        in_specs=(
            P("fsdp", "seq", None),
            P("fsdp", "seq", None),
            P("fsdp", None),
            P(),
            P("fsdp", None),
            P("fsdp", None),
            P(),
            P(),
            P("fsdp", None),
            P(),
            P("fsdp", None),
            P(),
            P(),
            P("fsdp", None),
            P(),
            P("fsdp", None),
            P("fsdp", None),
            P("fsdp", None),
        ),
        out_specs=(
            P("fsdp", "seq", None),
            P("fsdp", "seq", None),
            P(),
            P("fsdp", "seq"),
            P("fsdp", "seq"),
            P(),
            P(),
            P("fsdp", "seq"),
            P(),
            P("fsdp", "seq"),
            P(),
            P(),
            P("fsdp", "seq"),
            P(),
            P("fsdp", "seq"),
            P("fsdp", "seq"),
            P("fsdp", "seq"),
        ),
        check_vma=False,
    )
```

```python
import functools

import jax
import jax.numpy as jnp
from jax import lax
from jax.experimental import pallas as pl
from jax.experimental.pallas import tpu as pltpu
from jax.sharding import PartitionSpec as P

norm_eps = 1e-06
mult_floor = 0.0001


def from_behind(x, axis, by):
    devices = lax.axis_size(axis)
    pairs = [(i, i + by) for i in range(devices) if 0 <= i + by < devices]
    return lax.ppermute(x, axis, pairs)


def rms_scale(values, gain):
    scale = lax.rsqrt(jnp.mean(values * values, axis=-1, keepdims=True) + norm_eps)
    return values * scale * gain


def smooth_gelu(values):
    return jax.nn.gelu(values, approximate=True)


def gated_unit(gate, up_val):
    return smooth_gelu(gate) * up_val


def affine_pair(earlier, later):
    return (earlier[0] * later[0], earlier[1] * later[0] + later[1])


def decay_terms(conv_out, decay_pre, input_pre, decay_param, resets):
    log_a = -8.0 * jax.nn.sigmoid(decay_pre) * jax.nn.softplus(-decay_param)
    room = jnp.maximum(-jnp.expm1(2.0 * log_a), mult_floor)
    factor = jnp.where(resets, 1.0, jnp.sqrt(room))
    decay = jnp.where(resets, 0.0, jnp.exp(log_a))
    return (decay, jax.nn.sigmoid(input_pre) * conv_out * factor)


def conv_apply(extended, taps_w, bias, masks):
    taps = taps_w.shape[0]
    rows = masks.shape[1]
    total = jnp.zeros((rows, taps_w.shape[1]), jnp.float32) + bias
    for shift_k in range(taps):
        begin_row = taps - 1 - shift_k
        total = total + taps_w[shift_k] * extended[begin_row : begin_row + rows] * masks[shift_k]
    return total


def block_product(left, weight):
    width = weight.shape[1]
    blocks = weight.shape[0] // width
    result = jnp.einsum(
        "nhk,hkj->nhj",
        left.reshape(left.shape[0], blocks, width),
        weight.reshape(blocks, width, width),
        preferred_element_type=jnp.float32,
    )
    return result.reshape(left.shape[0], -1)


def block_back(grad, weight):
    width = weight.shape[1]
    blocks = weight.shape[0] // width
    result = jnp.einsum(
        "nhj,hkj->nhk",
        grad.reshape(grad.shape[0], blocks, width),
        weight.reshape(blocks, width, width),
        preferred_element_type=jnp.float32,
    )
    return result.reshape(grad.shape[0], -1)


def block_weight_grad(left, grad, width):
    blocks = left.shape[1] // width
    result = jnp.einsum(
        "nhk,nhj->hkj",
        left.reshape(left.shape[0], blocks, width),
        grad.reshape(grad.shape[0], blocks, width),
        preferred_element_type=jnp.float32,
    )
    return result.reshape(blocks * width, width)


def wide_shards(
    tokens,
    cotangent,
    doc_starts,
    mix_gain,
    input_proj,
    gelu_proj,
    conv_taps,
    conv_bias,
    decay_gate,
    decay_bias,
    input_gate,
    input_bias,
    decay_param,
    output_proj,
    mlp_gain,
    mlp_gate,
    mlp_up,
    mlp_down,
):
    rows = tokens.shape[1]
    taps = conv_taps.shape[0]
    width = decay_gate.shape[1]
    input_w, gelu_w, output_w, decay_w, inputg_w, gate_w, up_w, down_w = (
        lax.all_gather(input_proj, "fsdp", axis=0, tiled=True),
        lax.all_gather(gelu_proj, "fsdp", axis=0, tiled=True),
        lax.all_gather(output_proj, "fsdp", axis=0, tiled=True),
        lax.all_gather(decay_gate, "fsdp", axis=0, tiled=True),
        lax.all_gather(input_gate, "fsdp", axis=0, tiled=True),
        lax.all_gather(mlp_gate, "fsdp", axis=0, tiled=True),
        lax.all_gather(mlp_up, "fsdp", axis=0, tiled=True),
        lax.all_gather(mlp_down, "fsdp", axis=0, tiled=True),
    )
    channels = input_w.shape[1]
    first = lax.axis_index("seq") * rows
    positions = first + jnp.arange(rows, dtype=jnp.int32)
    starts = doc_starts[0]
    begin = jnp.max(jnp.where(starts[None, :] <= positions[:, None], starts[None, :], 0), axis=1)
    resets = (begin == positions)[:, None]
    masks = jnp.stack([(positions - k >= begin)[:, None] for k in range(taps)]).astype(jnp.float32)
    values = tokens[0].astype(jnp.float32)
    normed = rms_scale(values, mix_gain).astype(jnp.bfloat16)
    branch = jnp.dot(normed, input_w, preferred_element_type=jnp.float32).astype(jnp.bfloat16)
    gelu_pre = jnp.dot(normed, gelu_w, preferred_element_type=jnp.float32)
    gelu_out = smooth_gelu(gelu_pre)
    previous = from_behind(branch[rows - (taps - 1) :], "seq", 1)
    extended = jnp.concatenate([previous, branch], axis=0).astype(jnp.float32)
    conv_f = conv_apply(extended, conv_taps, conv_bias, masks).astype(jnp.bfloat16)
    conv_val = conv_f.astype(jnp.float32)
    decay_pre = block_product(conv_f, decay_w) + decay_bias
    input_pre = block_product(conv_f, inputg_w) + input_bias
    decay, driven = decay_terms(conv_val, decay_pre, input_pre, decay_param, resets)
    decay_cols, driven_cols = (
        lax.all_to_all(decay, "seq", split_axis=1, concat_axis=0, tiled=True),
        lax.all_to_all(driven, "seq", split_axis=1, concat_axis=0, tiled=True),
    )
    states_cols = lax.associative_scan(affine_pair, (decay_cols, driven_cols), axis=0)[1]
    states_low = lax.all_to_all(
        states_cols.astype(jnp.bfloat16), "seq", split_axis=0, concat_axis=1, tiled=True
    )
    states_val = states_low.astype(jnp.float32)
    merged = (states_val * gelu_out).astype(jnp.bfloat16)
    middle = values + jnp.dot(merged, output_w, preferred_element_type=jnp.float32)
    normed2 = rms_scale(middle, mlp_gain).astype(jnp.bfloat16)
    gate = jnp.dot(normed2, gate_w, preferred_element_type=jnp.float32)
    up_val = jnp.dot(normed2, up_w, preferred_element_type=jnp.float32)
    hidden = gated_unit(gate, up_val).astype(jnp.bfloat16)
    mixed = (middle + jnp.dot(hidden, down_w, preferred_element_type=jnp.float32)).astype(
        jnp.bfloat16
    )
    out_grad = cotangent[0]
    down_grad = jnp.einsum("tf,td->fd", hidden, out_grad, preferred_element_type=jnp.float32)
    hidden_grad = jnp.einsum("td,fd->tf", out_grad, down_w, preferred_element_type=jnp.float32)
    unit_pull = jax.vjp(gated_unit, gate, up_val)[1]
    gate_grad, up_grad = unit_pull(hidden_grad)
    gate_low = gate_grad.astype(jnp.bfloat16)
    up_low = up_grad.astype(jnp.bfloat16)
    gate_w_grad = jnp.einsum("td,tf->df", normed2, gate_low, preferred_element_type=jnp.float32)
    up_w_grad = jnp.einsum("td,tf->df", normed2, up_low, preferred_element_type=jnp.float32)
    mlp_terms = (
        lax.psum_scatter(gate_w_grad, "seq", scatter_dimension=1, tiled=True),
        lax.psum_scatter(up_w_grad, "seq", scatter_dimension=1, tiled=True),
        lax.psum_scatter(down_grad, "seq", scatter_dimension=1, tiled=True),
    )
    mlp_gate_grad, mlp_up_grad, mlp_down_grad = (
        lax.psum_scatter(mlp_terms[0], "fsdp", scatter_dimension=0, tiled=True),
        lax.psum_scatter(mlp_terms[1], "fsdp", scatter_dimension=0, tiled=True),
        lax.psum_scatter(mlp_terms[2], "fsdp", scatter_dimension=0, tiled=True),
    )
    normed2_grad = jnp.einsum(
        "tf,df->td", gate_low, gate_w, preferred_element_type=jnp.float32
    ) + jnp.einsum("tf,df->td", up_low, up_w, preferred_element_type=jnp.float32)
    norm2_pull = jax.vjp(rms_scale, middle, mlp_gain)[1]
    middle_part, mlp_gain_term = norm2_pull(normed2_grad)
    middle_grad = out_grad.astype(jnp.float32) + middle_part
    mixer_grad = middle_grad.astype(jnp.bfloat16)
    output_w_grad = jnp.einsum("tr,td->rd", merged, mixer_grad, preferred_element_type=jnp.float32)
    merged_grad = jnp.einsum("td,rd->tr", mixer_grad, output_w, preferred_element_type=jnp.float32)
    state_low = (merged_grad * gelu_out).astype(jnp.bfloat16)
    gelu_pull = jax.vjp(smooth_gelu, gelu_pre)[1]
    gelu_pre_low = gelu_pull(merged_grad * states_val)[0].astype(jnp.bfloat16)
    grad_cols = lax.all_to_all(state_low, "seq", split_axis=1, concat_axis=0, tiled=True).astype(
        jnp.float32
    )
    width_cols = grad_cols.shape[1]
    next_decay = jnp.concatenate([decay_cols[1:], jnp.zeros((1, width_cols), jnp.float32)], axis=0)
    carried = lax.associative_scan(affine_pair, (next_decay, grad_cols), reverse=True, axis=0)[1]
    prior = jnp.concatenate([jnp.zeros((1, width_cols), jnp.float32), states_cols[:-1]], axis=0)
    decay_grad, driven_grad = (
        lax.all_to_all(carried * prior, "seq", split_axis=0, concat_axis=1, tiled=True),
        lax.all_to_all(carried, "seq", split_axis=0, concat_axis=1, tiled=True),
    )
    terms_pull = jax.vjp(
        lambda conv_in, dpre, ipre, dparam: decay_terms(conv_in, dpre, ipre, dparam, resets),
        conv_val,
        decay_pre,
        input_pre,
        decay_param,
    )[1]
    gate_conv_grad, dpre_grad, ipre_grad, decay_param_term = terms_pull((decay_grad, driven_grad))
    dpre_low = dpre_grad.astype(jnp.bfloat16)
    ipre_low = ipre_grad.astype(jnp.bfloat16)
    decay_w_grad = block_weight_grad(conv_f, dpre_low, width)
    inputg_w_grad = block_weight_grad(conv_f, ipre_low, width)
    conv_grad = gate_conv_grad + block_back(dpre_low, decay_w) + block_back(ipre_low, inputg_w)
    conv_pull = jax.vjp(
        lambda ext, taps_w, bias: conv_apply(ext, taps_w, bias, masks),
        extended,
        conv_taps,
        conv_bias,
    )[1]
    extended_grad, taps_term, conv_bias_term = conv_pull(conv_grad)
    returned = from_behind(extended_grad[: taps - 1], "seq", -1)
    branch_grad = extended_grad[taps - 1 :] + jnp.concatenate(
        [jnp.zeros((rows - (taps - 1), channels), jnp.float32), returned], axis=0
    )
    branch_low = branch_grad.astype(jnp.bfloat16)
    input_w_grad = jnp.einsum("td,tr->dr", normed, branch_low, preferred_element_type=jnp.float32)
    gelu_w_grad = jnp.einsum("td,tr->dr", normed, gelu_pre_low, preferred_element_type=jnp.float32)
    mix_terms = (
        lax.psum_scatter(input_w_grad, "seq", scatter_dimension=1, tiled=True),
        lax.psum_scatter(gelu_w_grad, "seq", scatter_dimension=1, tiled=True),
        lax.psum_scatter(output_w_grad, "seq", scatter_dimension=1, tiled=True),
        lax.psum_scatter(decay_w_grad, "seq", scatter_dimension=1, tiled=True),
        lax.psum_scatter(inputg_w_grad, "seq", scatter_dimension=1, tiled=True),
    )
    input_proj_grad, gelu_proj_grad, output_proj_grad, decay_gate_grad, input_gate_grad = (
        lax.psum_scatter(mix_terms[0], "fsdp", scatter_dimension=0, tiled=True),
        lax.psum_scatter(mix_terms[1], "fsdp", scatter_dimension=0, tiled=True),
        lax.psum_scatter(mix_terms[2], "fsdp", scatter_dimension=0, tiled=True),
        lax.psum_scatter(mix_terms[3], "fsdp", scatter_dimension=0, tiled=True),
        lax.psum_scatter(mix_terms[4], "fsdp", scatter_dimension=0, tiled=True),
    )
    normed_grad = jnp.einsum(
        "tr,dr->td", branch_low, input_w, preferred_element_type=jnp.float32
    ) + jnp.einsum("tr,dr->td", gelu_pre_low, gelu_w, preferred_element_type=jnp.float32)
    norm1_pull = jax.vjp(rms_scale, values, mix_gain)[1]
    values_part, mix_gain_term = norm1_pull(normed_grad)
    tokens_grad = (middle_grad + values_part).astype(jnp.bfloat16)
    (
        mix_gain_grad,
        conv_taps_grad,
        conv_bias_grad,
        decay_bias_grad,
        input_bias_grad,
        decay_param_grad,
        mlp_gain_grad,
    ) = lax.psum(
        (
            mix_gain_term,
            taps_term,
            conv_bias_term,
            jnp.sum(dpre_low.astype(jnp.float32), axis=0),
            jnp.sum(ipre_low.astype(jnp.float32), axis=0),
            decay_param_term,
            mlp_gain_term,
        ),
        ("seq", "fsdp"),
    )
    return (
        mixed[None],
        tokens_grad[None],
        mix_gain_grad,
        input_proj_grad,
        gelu_proj_grad,
        conv_taps_grad,
        conv_bias_grad,
        decay_gate_grad,
        decay_bias_grad,
        input_gate_grad,
        input_bias_grad,
        decay_param_grad,
        output_proj_grad,
        mlp_gain_grad,
        mlp_gate_grad,
        mlp_up_grad,
        mlp_down_grad,
    )


def chip_swap(x, k):
    devices = lax.axis_size("seq")
    return lax.ppermute(x, "seq", [(i, i ^ (2 * k)) for i in range(devices)])


def core_swap(x):
    devices = lax.axis_size("seq")
    return lax.ppermute(x, "seq", [(i, i ^ 1) for i in range(devices)])


def gather_blocks(x):
    chips = lax.axis_size("seq") // 2
    near = jnp.stack([x] + [chip_swap(x, k) for k in range(1, chips)])
    return near, core_swap(near)


def tie(*arrays):
    return lax.optimization_barrier(arrays)


def pair_blocks(near, far, extra=None):
    if extra is None:
        extra = jnp.zeros((0, near.shape[2]), jnp.bfloat16)
    return payloads(near, core_swap(far), extra)


def spread_pairs(own, *low):
    return own, *[chip_swap(block, k + 1) for k, block in enumerate(low)]


def plane_swap(x, k):
    if k == 0:
        return x
    return lax.ppermute(x, "fsdp", [(i, i ^ k) for i in range(lax.axis_size("fsdp"))])


def exchange(x, chip, core, turn, beside):
    chips = x.shape[0]
    parts = [
        lax.dynamic_index_in_dim(x, chip ^ k ^ turn, 0, keepdims=False) for k in range(chips)
    ]
    got = [chip_swap(parts[k], k) for k in range(1, chips)]
    got[0], *beside = tie(got[0], *beside)
    got = jnp.stack([parts[0], *got])
    keep = lax.dynamic_index_in_dim(got, core, 1, keepdims=False)
    give = lax.dynamic_index_in_dim(got, 1 - core, 1, keepdims=False)
    return keep, core_swap(give), *beside


def over_planes(x):
    planes = lax.axis_size("fsdp")
    total = x
    for k in range(1, planes):
        got = lax.ppermute(x.astype(jnp.bfloat16), "fsdp", [(i, i ^ k) for i in range(planes)])
        total = total + got.astype(jnp.float32)
    return total


little = pl.CostEstimate(flops=0, bytes_accessed=0, transcendentals=0)


def gelu_parts(v):
    root = 0.7978845608028654
    square = v * v
    h = 0.5 + 0.5 * jnp.tanh(v * (root + root * 0.044715 * square))
    value = v * h
    return value, h + value * (1.0 - h) * (2.0 * root + root * 0.26829 * square)


def sigmoid(v):
    return 1.0 / (1.0 + jnp.exp(-v))


def one_less_exp(v):
    series = -v * (1.0 + v * (0.5 + v * (1.0 / 6.0 + v * (1.0 / 24.0 + v * (1.0 / 120.0)))))
    return jnp.where(v > -0.1, series, 1.0 - jnp.exp(v))


def dot_nn(a, b):
    return lax.dot_general(a, b, (((1,), (0,)), ((), ())), preferred_element_type=jnp.float32)


def dot_nt(a, b):
    return lax.dot_general(a, b, (((1,), (1,)), ((), ())), preferred_element_type=jnp.float32)


def dot_tn(a, b):
    return lax.dot_general(a, b, (((0,), (0,)), ((), ())), preferred_element_type=jnp.float32)


def scan_rows(a, b, carry, later):
    rows = a.shape[0]
    group = 8
    row = lax.broadcasted_iota(jnp.int32, a.shape, 0) % group
    step = 1
    while step < group:
        turn = rows - step if later else step
        there = (row < group - step) if later else (row >= step)
        a_next = jnp.where(there, pltpu.roll(a, turn, 0), 1.0)
        b_next = jnp.where(there, pltpu.roll(b, turn, 0), 0.0)
        b = a * b_next + b
        a = a * a_next
        step *= 2
    starts = list(range(0, rows, group))
    done = {}
    for start in reversed(starts) if later else starts:
        states = a[start : start + group] * carry + b[start : start + group]
        done[start] = states
        carry = states[:1] if later else states[group - 1 :]
    return jnp.concatenate([done[start] for start in starts], axis=0)


def in_time(value, core):
    rows = value.shape[0] // 2
    near, far = value[:rows], value[rows:]
    odd = core == 1
    return jnp.concatenate([jnp.where(odd, far, near), jnp.where(odd, near, far)], axis=0)


def by_core(value, ref, core):
    rows = value.shape[0] // 2
    first, second = value[:rows], value[rows:]
    odd = core == 1
    ref[0] = jnp.where(odd, second, first).astype(ref.dtype)
    ref[1] = jnp.where(odd, first, second).astype(ref.dtype)


def tables_kernel(starts_ref, taps_ref, conv_ref, decay_ref, input_ref, param_ref, chan_ref, age_ref):
    chan_ref[...] = jnp.zeros_like(chan_ref)
    chan_ref[0:4, :] = taps_ref[...]
    chan_ref[4:5, :] = conv_ref[...]
    chan_ref[5:6, :] = decay_ref[...]
    chan_ref[6:7, :] = input_ref[...]
    small = jnp.exp(-param_ref[...])
    series = small * (
        1.0
        - small * (1 / 2 - small * (1 / 3 - small * (1 / 4 - small * (1 / 5 - small * (1 / 6)))))
    )
    chan_ref[7:8, :] = jnp.where(small < 0.1, series, jnp.log(1.0 + small))
    chan_ref[8:9, :] = small / (1.0 + small)
    positions = lax.broadcasted_iota(jnp.int32, age_ref.shape, 0)
    begin = jnp.zeros(age_ref.shape, jnp.int32)
    for j in range(starts_ref.shape[0]):
        start = starts_ref[j]
        begin = jnp.maximum(begin, jnp.where(start <= positions, start, 0))
    age_ref[...] = (positions - begin).astype(jnp.float32)


def tables(starts, taps, conv_bias, decay_bias, input_bias, param, length):
    channels = taps.shape[1]
    whole = pl.BlockSpec(memory_space=pltpu.VMEM)
    return pl.pallas_call(
        tables_kernel,
        in_specs=[pl.BlockSpec(memory_space=pltpu.SMEM)] + [whole] * 5,
        out_specs=[whole] * 2,
        out_shape=[
            jax.ShapeDtypeStruct((16, channels), jnp.float32),
            jax.ShapeDtypeStruct((length, 1), jnp.float32),
        ],
        name="tables",
    )(starts, taps, conv_bias[None], decay_bias[None], input_bias[None], param[None])


def mix_forward_kernel(
    seq_ref,
    near_ref,
    far_ref,
    age_ref,
    chan_ref,
    keep_ref,
    got_ref,
    merged_ref,
    middle_near_ref,
    middle_far_ref,
    branch_ref,
    conv_ref,
    gelu_ref,
    gelu_grad_ref,
    decay_ref,
    input_ref,
    direct_ref,
    sig_ref,
    decay_grad_ref,
    weights_ref,
    extended,
    carry,
):
    place = seq_ref[0]
    chips = keep_ref.shape[0]
    step = pl.program_id(0)
    chip, core = place // 2, place % 2
    rows, width = branch_ref.shape
    model = middle_near_ref.shape[1]
    piece = keep_ref.shape[1]

    @pl.when(step == 0)
    def _():
        extended[pl.ds(0, 8), :] = jnp.zeros((8, width), jnp.float32)
        carry[...] = jnp.zeros_like(carry)
        for k in range(chips):
            home = pl.multiple_of(piece * 2 * (chip ^ k) + piece * core, piece)
            away = pl.multiple_of(piece * 2 * (chip ^ k) + piece * (1 - core), piece)
            weights_ref[pl.ds(home, piece), :] = keep_ref[k]
            weights_ref[pl.ds(away, piece), :] = got_ref[k]

    @pl.when(step > 0)
    def _():
        extended[pl.ds(0, 8), :] = extended[pl.ds(rows, 8), :]

    pre = in_time(jnp.concatenate([near_ref[...], far_ref[...]], axis=0), core)
    branch = pre[:, :width].astype(jnp.bfloat16)
    gelu_pre = pre[:, width:]
    branch_ref[...] = branch
    extended[pl.ds(8, rows), :] = branch.astype(jnp.float32)
    age = age_ref[...]
    total = jnp.zeros((rows, width), jnp.float32) + chan_ref[4:5, :]
    for k in range(4):
        shifted = extended[pl.ds(8 - k, rows), :]
        total = total + chan_ref[k : k + 1, :] * shifted * jnp.where(age >= k, 1.0, 0.0)
    conv_low = total.astype(jnp.bfloat16)
    conv = conv_low.astype(jnp.float32)
    conv_ref[...] = conv_low
    decay_pre = dot_nn(conv_low, weights_ref[:, model : model + width]) + chan_ref[5:6, :]
    input_pre = dot_nn(conv_low, weights_ref[:, model + width :]) + chan_ref[6:7, :]
    sig_d, sig_i = sigmoid(decay_pre), sigmoid(input_pre)
    soft = chan_ref[7:8, :]
    log_a = -8.0 * sig_d * soft
    reset = age < 0.5
    open_room = one_less_exp(2.0 * log_a)
    root = jnp.sqrt(jnp.maximum(open_room, mult_floor))
    factor = jnp.where(reset, 1.0, root)
    a = jnp.exp(log_a)
    decay = jnp.where(reset, 0.0, a)
    passed = sig_i * conv
    before = carry[0:1, :]
    states = scan_rows(decay, passed * factor, before, False)
    carry[0:1, :] = states[rows - 1 :, :]
    row = lax.broadcasted_iota(jnp.int32, states.shape, 0)
    prior = jnp.where(row == 0, before, pltpu.roll(states, 1, 0))
    low = states.astype(jnp.bfloat16).astype(jnp.float32)
    value, slope = gelu_parts(gelu_pre)
    by_core(low * value, merged_ref, core)
    product = dot_nn(merged_ref[...].reshape(rows, width), weights_ref[:, :model])
    middle_near_ref[...] = product[: rows // 2].astype(jnp.bfloat16)
    middle_far_ref[...] = product[rows // 2 :].astype(jnp.bfloat16)
    gelu_ref[...] = value
    gelu_grad_ref[...] = low * slope
    decay_ref[...] = decay
    input_ref[...] = passed * (1.0 - sig_i) * factor
    direct_ref[...] = sig_i * factor
    through_room = jnp.where(open_room > mult_floor, a * a * passed / root, 0.0)
    sig_grad = jnp.where(reset, 0.0, (prior * a - through_room) * sig_d)
    sig_ref[...] = sig_grad
    decay_grad_ref[...] = -8.0 * soft * (1.0 - sig_d) * sig_grad


def mix_forward(place, near, far, age, chan, keep, got):
    chips, rows, both = near.shape
    width = both // 2
    model = keep.shape[2] - both
    length = 2 * chips * rows
    chunk = 2 * rows
    columns = keep.shape[2]
    one_block = lambda i, s: (i ^ (s[0] // 2), 0, 0)
    time_block = lambda i, s: (i, 0)
    token_block = lambda i, s: (0, i ^ (s[0] // 2), 0, 0)
    saved = lambda dtype: jax.ShapeDtypeStruct((length, width), dtype)
    spec = pl.BlockSpec((chunk, width), time_block)
    fixed = lambda shape: pl.BlockSpec(shape, lambda i, s: (0,) * len(shape))
    return pl.pallas_call(
        mix_forward_kernel,
        grid_spec=pltpu.PrefetchScalarGridSpec(
            num_scalar_prefetch=1,
            grid=(chips,),
            in_specs=[
                pl.BlockSpec((None, rows, both), one_block),
                pl.BlockSpec((None, rows, both), one_block),
                pl.BlockSpec((chunk, 1), time_block),
                pl.BlockSpec((chan.shape[0], width), lambda i, s: (0, s[0])),
                fixed(keep.shape),
                fixed(got.shape),
            ],
            out_specs=[pl.BlockSpec((2, None, rows, width), token_block)]
            + [pl.BlockSpec((None, rows, model), one_block)] * 2
            + [spec] * 9
            + [fixed((width, columns))],
            scratch_shapes=[
                pltpu.VMEM((chunk + 8, width), jnp.float32),
                pltpu.VMEM((8, width), jnp.float32),
            ],
        ),
        out_shape=[
            jax.ShapeDtypeStruct((2, chips, rows, width), jnp.bfloat16),
            jax.ShapeDtypeStruct((chips, rows, model), jnp.bfloat16),
            jax.ShapeDtypeStruct((chips, rows, model), jnp.bfloat16),
            saved(jnp.bfloat16),
            saved(jnp.bfloat16),
        ]
        + [saved(jnp.float32)] * 7
        + [jax.ShapeDtypeStruct((width, columns), jnp.bfloat16)],
        compiler_params=pltpu.CompilerParams(vmem_limit_bytes=56 * 1024 * 1024),
        name="mix_forward",
    )(place, near, far, age, chan, keep, got)


def mix_backward_kernel(
    seq_ref,
    near_ref,
    far_ref,
    age_ref,
    chan_ref,
    weights_ref,
    in_ref,
    merged_ref,
    branch_ref,
    conv_ref,
    gelu_ref,
    gelu_grad_ref,
    decay_ref,
    input_ref,
    direct_ref,
    sig_ref,
    decay_grad_ref,
    both_ref,
    small_ref,
    back_near_ref,
    back_far_ref,
    *rest,
):
    place = seq_ref[0]
    chips = near_ref.shape[0]
    row_refs, (out_grad, gate_grads, ahead, carry) = rest[:chips], rest[chips:]
    step = pl.program_id(0)
    chip, core = place // 2, place % 2
    rows, width = branch_ref.shape
    model = near_ref.shape[-1]

    @pl.when(step == 0)
    def _():
        carry[...] = jnp.zeros_like(carry)
        ahead[:, pl.ds(rows, 8), :] = jnp.zeros((3, 8, width), jnp.float32)
        small_ref[...] = jnp.zeros_like(small_ref)
        gate_grads[...] = jnp.zeros_like(gate_grads)
        out_grad[...] = jnp.zeros_like(out_grad)

    @pl.when(step > 0)
    def _():
        ahead[:, pl.ds(rows, 8), :] = ahead[:, pl.ds(0, 8), :]

    turn = (chips - 1 - step) ^ chip
    mixer_grad = jnp.concatenate([near_ref[turn], far_ref[turn]], axis=0)
    merged_grad = in_time(dot_nt(mixer_grad, weights_ref[:, :model]), core)
    age = age_ref[...]
    out_grad[...] += dot_tn(mixer_grad, merged_ref[...].reshape(rows, width))
    state_grad = (merged_grad * gelu_ref[...]).astype(jnp.bfloat16).astype(jnp.float32)
    gelu_pre_grad = merged_grad * gelu_grad_ref[...]
    decay = decay_ref[...]
    conv_low = conv_ref[...]
    row = lax.broadcasted_iota(jnp.int32, (rows, width), 0)
    next_decay = jnp.where(row == rows - 1, carry[0:1, :], pltpu.roll(decay, rows - 1, 0))
    carried = scan_rows(next_decay, state_grad, carry[1:2, :], True)
    carry[0:1, :] = decay[0:1, :]
    carry[1:2, :] = carried[0:1, :]
    gate_conv_grad = carried * direct_ref[...]
    input_low = (carried * input_ref[...]).astype(jnp.bfloat16)
    decay_low = (carried * decay_grad_ref[...]).astype(jnp.bfloat16)
    sig_grad = carried * sig_ref[...]
    conv_grad = (
        gate_conv_grad
        + dot_nt(decay_low, weights_ref[:, model : model + width])
        + dot_nt(input_low, weights_ref[:, model + width :])
    )
    gate_grads[0] += dot_tn(decay_low, conv_low)
    gate_grads[1] += dot_tn(input_low, conv_low)
    branch = branch_ref[...].astype(jnp.float32)
    branch_grad = chan_ref[0:1, :] * conv_grad
    small_ref[0:1, :] += jnp.sum(conv_grad * branch, axis=0, keepdims=True)
    for k in range(1, 4):
        ahead[k - 1, pl.ds(0, rows), :] = conv_grad * jnp.where(age >= k, 1.0, 0.0)
        shifted = ahead[k - 1, pl.ds(k, rows), :]
        branch_grad = branch_grad + chan_ref[k : k + 1, :] * shifted
        small_ref[k : k + 1, :] += jnp.sum(shifted * branch, axis=0, keepdims=True)
    small_ref[4:5, :] += jnp.sum(conv_grad, axis=0, keepdims=True)
    small_ref[5:6, :] += jnp.sum(decay_low.astype(jnp.float32), axis=0, keepdims=True)
    small_ref[6:7, :] += jnp.sum(input_low.astype(jnp.float32), axis=0, keepdims=True)
    small_ref[7:8, :] += 8.0 * chan_ref[8:9, :] * jnp.sum(sig_grad, axis=0, keepdims=True)
    by_core(jnp.concatenate([branch_grad, gelu_pre_grad], axis=1), both_ref, core)
    both = both_ref[...].reshape(rows, 2 * width)
    back = dot_nt(both, in_ref[...].reshape(model, 2 * width)).astype(jnp.bfloat16)
    back_near_ref[...] = back[: rows // 2]
    back_far_ref[...] = back[rows // 2 :]

    @pl.when(step == chips - 1)
    def _():
        slim, piece = model // (2 * chips), width // (2 * chips)
        for k in range(chips):
            for e in range(2):
                target = 2 * (chip ^ k) + (core ^ e)
                rows = pl.ds(pl.multiple_of(target * slim, slim), slim)
                row_refs[k][e, pl.ds(0, slim), :] = out_grad[rows, :].astype(jnp.bfloat16)
                rows = pl.ds(pl.multiple_of(target * piece, piece), piece)
                for j in range(2):
                    row_refs[k][e, pl.ds(slim + j * piece, piece), :] = gate_grads[j, rows, :].astype(
                        jnp.bfloat16
                    )


def mix_backward(place, near, far, age, chan, weights, pack, merged, saved):
    planes, _, both = pack.shape
    chips, rows, model = near.shape
    width, columns = weights.shape
    tall = (model + 2 * width) // (2 * chips)
    chunk = 2 * rows
    last = chips - 1
    time_block = lambda i, s: (last - i, 0)
    token_block = lambda i, s: (0, (last - i) ^ (s[0] // 2), 0, 0)
    spec = pl.BlockSpec((chunk, width), time_block)
    back = pl.BlockSpec((None, rows, model), lambda i, s: ((last - i) ^ (s[0] // 2), 0, 0))
    fixed = lambda shape: pl.BlockSpec(shape, lambda i, s: (0,) * len(shape))
    return pl.pallas_call(
        mix_backward_kernel,
        grid_spec=pltpu.PrefetchScalarGridSpec(
            num_scalar_prefetch=1,
            grid=(chips,),
            in_specs=[
                fixed(near.shape),
                fixed(far.shape),
                pl.BlockSpec((chunk, 1), time_block),
                pl.BlockSpec((chan.shape[0], width), lambda i, s: (0, s[0])),
                fixed((width, columns)),
                fixed((planes, model // planes, both)),
                pl.BlockSpec((2, None, rows, width), token_block),
            ]
            + [spec] * 9,
            out_specs=[
                pl.BlockSpec((2, None, rows, 2 * width), token_block),
                fixed((8, width)),
                back,
                back,
            ]
            + [fixed((2, tall, width))] * chips,
            scratch_shapes=[
                pltpu.VMEM((model, width), jnp.float32),
                pltpu.VMEM((2, width, width), jnp.float32),
                pltpu.VMEM((3, chunk + 8, width), jnp.float32),
                pltpu.VMEM((8, width), jnp.float32),
            ],
        ),
        out_shape=[
            jax.ShapeDtypeStruct((2, chips, rows, 2 * width), jnp.bfloat16),
            jax.ShapeDtypeStruct((8, width), jnp.float32),
            jax.ShapeDtypeStruct(near.shape, jnp.bfloat16),
            jax.ShapeDtypeStruct(near.shape, jnp.bfloat16),
        ]
        + [jax.ShapeDtypeStruct((2, tall, width), jnp.bfloat16)] * chips,
        compiler_params=pltpu.CompilerParams(vmem_limit_bytes=50 * 1024 * 1024),
        cost_estimate=pl.CostEstimate(
            flops=10**9, bytes_accessed=24 * 10**6, transcendentals=0
        ),
        name="mix_backward",
    )(place, near, far, age, chan, weights, pack, merged, *saved)


def unit_kernel(
    near_ref,
    far_ref,
    cot_near_ref,
    cot_far_ref,
    pack_ref,
    back_near_out,
    back_far_out,
    hidden_out,
    down_out,
    grads_out,
    normed,
    cot,
    gate_up,
    down,
    pair,
    hidden,
    pair_t,
    hidden_t,
    grads,
    back,
    in_sems,
    out_sems,
):
    bf16 = jnp.bfloat16
    chips, rows, _ = near_ref.shape
    planes, tall, near_model = pack_ref.shape
    both = pair.shape[1]
    part = both // 2
    span = part // planes
    side = near_model // 2
    spare = down.shape[0] - part
    half = chips * rows
    incoming, outgoing = [], []

    def fetch(source, target):
        copy = pltpu.make_async_copy(source, target, in_sems.at[len(incoming)])
        copy.start()
        incoming.append(copy)
        return copy

    def send(source, target):
        copy = pltpu.make_async_copy(source, target, out_sems.at[len(outgoing)])
        copy.start()
        outgoing.append(copy)

    def fetch_half(source, target, i):
        return [
            fetch(source.at[k], target.at[pl.ds(i * half + k * rows, rows), :]) for k in range(chips)
        ]

    gate_up_copies = [
        fetch(
            pack_ref.at[z, pl.ds(j * near_model, near_model), :],
            gate_up.at[pl.ds(z * near_model, near_model), pl.ds(j * near_model, near_model)],
        )
        for z in range(planes)
        for j in range(3)
    ]
    normed_copies = [fetch_half(near_ref, normed, 0)]
    down_copies = [
        fetch(
            pack_ref.at[z, pl.ds(3 * near_model + j * span, span), :],
            down.at[pl.ds(z * span, span), pl.ds(j * near_model, near_model)],
        )
        for z in range(planes)
        for j in range(planes)
    ]
    cot_copies = [fetch_half(cot_near_ref, cot, 0)]
    for copy in gate_up_copies + normed_copies[0]:
        copy.wait()
    normed_copies.append(fetch_half(far_ref, normed, 1))
    cot_copies.append(fetch_half(cot_far_ref, cot, 1))
    chunk = 2 * rows
    first_unit, mid_unit, last_unit = (pl.ds(j * near_model, near_model) for j in range(3))
    for i in range(chips):
        here = pl.ds(i * chunk, chunk)
        if i * chunk == half:
            for copy in normed_copies[1] + cot_copies[1]:
                copy.wait()
        pre = dot_nn(normed[here, :], gate_up[...])
        if i == 0:
            for copy in down_copies + cot_copies[0]:
                copy.wait()
            down[pl.ds(part, spare), :] = jnp.zeros((spare, down.shape[1]), bf16)
        above = dot_nt(cot[here, :], down[...])
        up = pre[:, 2 * near_model :]
        value, slope = gelu_parts(pre[:, :near_model])
        grad = above[:, :near_model]
        hidden[here, first_unit] = (value * up).astype(bf16)
        pair[here, first_unit] = (grad * up * slope).astype(bf16)
        pair[here, last_unit] = (grad * value).astype(bf16)
        mid = pre[:, near_model : 2 * near_model]
        broad = side + spare
        up = pltpu.roll(mid, side, 1)[:, :broad]
        value, slope = gelu_parts(mid[:, :broad])
        grad = above[:, near_model:]
        hidden[here, pl.ds(near_model, side)] = (value * up)[:, :side].astype(bf16)
        left, right = grad * up * slope, grad * value
        left = jnp.concatenate([left, left[:, : near_model - broad]], axis=1)
        right = jnp.concatenate([right, right[:, : near_model - broad]], axis=1)
        lane = lax.broadcasted_iota(jnp.int32, left.shape, 1)
        pair[here, mid_unit] = jnp.where(lane < side, left, pltpu.roll(right, side, 1)).astype(bf16)
        pair_t[:, here] = pair[here, :].T
        hidden_t[:, here] = hidden[here, :].T
    def unit_rows(start):
        pieces, stop = [], start + span
        if start < near_model:
            pieces.append((2 * near_model + start, min(stop, near_model) - start))
        if stop > near_model:
            first = max(start, near_model)
            pieces.append((part + first - near_model, stop - first))
        return pieces

    for first_z in range(0, planes, 2):
        here = pl.ds(first_z * near_model, 2 * near_model)
        grad = dot_nn(hidden_t[...], cot[:, here]).astype(bf16)
        for z in (first_z, first_z + 1):
            columns = slice((z - first_z) * near_model, (z - first_z + 1) * near_model)
            for j in range(planes):
                grads[j, pl.ds((3 * z + 2) * span, span), :] = grad[
                    j * span : (j + 1) * span, columns
                ]
    for first_z in range(0, planes, 2):
        here = pl.ds(first_z * near_model, 2 * near_model)
        grad = dot_nn(pair_t[...], normed[:, here]).astype(bf16)
        for z in (first_z, first_z + 1):
            columns = slice((z - first_z) * near_model, (z - first_z + 1) * near_model)
            for j in range(planes):
                row = 3 * j * span
                grads[z, pl.ds(row, span), :] = grad[j * span : (j + 1) * span, columns]
                row += span
                for first, count in unit_rows(j * span):
                    grads[z, pl.ds(row, count), :] = grad[first : first + count, columns]
                    row += count
            send(grads.at[z], grads_out.at[z])
    send(hidden, hidden_out)
    send(down.at[pl.ds(0, part), :], down_out)
    for i, out in ((1, back_far_out), (0, back_near_out)):
        for k in range(0, chips, 2):
            first_row = i * half + k * rows
            here = pl.ds(first_row, chunk)
            back[here, :] = dot_nt(pair[here, :], gate_up[...]).astype(bf16)
            for e in range(2):
                send(back.at[pl.ds(first_row + e * rows, rows), :], out.at[k + e])
    for copy in outgoing:
        copy.wait()


def unit_back_and_forth(near, far, cot_near, cot_far, pack, part):
    chips, rows, model = near.shape
    length = 2 * chips * rows
    planes, _, near_model = pack.shape
    bf16 = jnp.bfloat16
    there = pl.BlockSpec(memory_space=pl.ANY)
    return pl.pallas_call(
        unit_kernel,
        in_specs=[there] * 5,
        out_specs=[there] * 5,
        scratch_shapes=[
            pltpu.VMEM((length, model), bf16),
            pltpu.VMEM((length, model), bf16),
            pltpu.VMEM((model, 2 * part), bf16),
            pltpu.VMEM((pl.cdiv(part, 128) * 128, model), bf16),
            pltpu.VMEM((length, 2 * part), bf16),
            pltpu.VMEM((length, part), bf16),
            pltpu.VMEM((2 * part, length), bf16),
            pltpu.VMEM((part, length), bf16),
            pltpu.VMEM(pack.shape, bf16),
            pltpu.VMEM((length, model), bf16),
            pltpu.SemaphoreType.DMA((4 * chips + planes * (3 + planes),)),
            pltpu.SemaphoreType.DMA((4 * chips + planes,)),
        ],
        out_shape=[jax.ShapeDtypeStruct(near.shape, bf16)] * 2
        + [
            jax.ShapeDtypeStruct((length, part), bf16),
            jax.ShapeDtypeStruct((part, model), bf16),
            jax.ShapeDtypeStruct(pack.shape, bf16),
        ],
        compiler_params=pltpu.CompilerParams(vmem_limit_bytes=58 * 1024 * 1024),
        name="unit_back_and_forth",
    )(near, far, cot_near, cot_far, pack)


def mixed_kernel(hidden_ref, down_ref, near_ref, far_ref):
    chips, rows, model = near_ref.shape
    for i, ref in enumerate((near_ref, far_ref)):
        here = pl.ds(i * chips * rows, chips * rows)
        product = dot_nn(hidden_ref[here, :], down_ref[...])
        ref[...] = product.reshape(chips, rows, model).astype(ref.dtype)


def mixed_parts(hidden, down, chips):
    length, model = hidden.shape[0], down.shape[1]
    whole = pl.BlockSpec(memory_space=pltpu.VMEM)
    shape = jax.ShapeDtypeStruct((chips, length // (2 * chips), model), jnp.bfloat16)
    return pl.pallas_call(
        mixed_kernel,
        in_specs=[whole] * 2,
        out_specs=[whole] * 2,
        out_shape=[shape] * 2,
        compiler_params=pltpu.CompilerParams(vmem_limit_bytes=24 * 1024 * 1024),
        cost_estimate=little,
        name="mixed_parts",
    )(hidden, down)


def mix_pack_kernel(
    place_ref, input_ref, gelu_ref, out_ref, decay_ref, gate_ref, in_own_ref, rows_ref
):
    width, model = input_ref.shape[1], out_ref.shape[2]
    in_own_ref[:, pl.ds(0, width)] = input_ref[...]
    in_own_ref[:, pl.ds(width, width)] = gelu_ref[...]
    rows_ref[:, :, pl.ds(0, model)] = out_ref[...]
    rows_ref[:, :, pl.ds(model, width)] = decay_ref[...]
    rows_ref[:, :, pl.ds(model + width, width)] = gate_ref[...]


def own_mix_pack(place, input_proj, gelu_proj, output_proj, decay_gate, input_gate):
    near_model, channels = input_proj.shape
    width = decay_gate.shape[1]
    heads = decay_gate.shape[0] // width
    model = output_proj.shape[1]
    piece = width // (channels // width)
    mine = pl.BlockSpec((near_model, width), lambda i, s: (0, s[0]))
    rows = lambda columns: pl.BlockSpec((heads, piece, columns), lambda i, s: (0, s[0], 0))
    shapes = [(near_model, 2 * width), (heads, piece, model + 2 * width)]
    return pl.pallas_call(
        mix_pack_kernel,
        grid_spec=pltpu.PrefetchScalarGridSpec(
            num_scalar_prefetch=1,
            grid=(1,),
            in_specs=[mine, mine, rows(model), rows(width), rows(width)],
            out_specs=[
                pl.BlockSpec(shape, lambda i, s, zeros=(0,) * len(shape): zeros) for shape in shapes
            ],
        ),
        out_shape=[jax.ShapeDtypeStruct(shape, input_proj.dtype) for shape in shapes],
        name="own_mix_pack",
    )(
        place,
        input_proj,
        gelu_proj,
        output_proj.reshape(heads, width, model),
        decay_gate.reshape(heads, width, width),
        input_gate.reshape(heads, width, width),
    )


def unit_pack_kernel(place_ref, gate_ref, up_ref, down_ref, pack_ref, windows, sems):
    place = place_ref[0]
    near_model, deep = gate_ref.shape
    planes = windows.shape[1]
    tile = 128
    span = (pack_ref.shape[0] - 3 * near_model) // planes
    extra = span - tile
    copies = []

    def fetch(source, target):
        copies.append(pltpu.make_async_copy(source, target, sems.at[len(copies)]))
        copies[-1].start()

    for i, ref in enumerate((gate_ref, up_ref)):
        for z in range(planes):
            start = pl.multiple_of(z * (deep // planes) + place * tile, tile)
            fetch(ref.at[:, pl.ds(start, 2 * tile)], windows.at[i, z])
    rows = pl.ds(pl.multiple_of(place * span, 16), span)
    for j in range(planes):
        fetch(
            down_ref.at[rows, pl.ds(j * near_model, near_model)],
            pack_ref.at[pl.ds(3 * near_model + j * span, span), :],
        )
    lane = lax.broadcasted_iota(jnp.int32, (near_model, tile), 1)

    def tiles(i):
        parts = []
        for z in range(planes):
            copies[i * planes + z].wait()
            turn = lax.rem((z - place) * extra + 2 * tile, 2 * tile)
            parts.append(pltpu.roll(windows[i, z].astype(jnp.float32), turn, 1))
        found = [parts[0][:, :tile]]
        for z in range(1, planes):
            found.append(jnp.where(lane < z * extra, parts[z - 1][:, tile:], parts[z][:, :tile]))
        return found + [parts[planes - 1][:, tile:]]

    gate, up = tiles(0), tiles(1)
    half = tile // 2
    turned = [pltpu.roll(up[j], half, 1) for j in (3, 4)]
    mid = [
        gate[3],
        jnp.where(lane < half, gate[4], turned[0]),
        jnp.where(lane < half, turned[0], turned[1]),
    ]
    for block, found in enumerate((gate[:3], mid, up[:3])):
        for j in range(3):
            pack_ref[pl.ds(block * near_model, near_model), pl.ds(j * tile, tile)] = found[
                j
            ].astype(pack_ref.dtype)
    for copy in copies[2 * planes :]:
        copy.wait()


def own_unit_pack(place, mlp_gate, mlp_up, mlp_down, planes, span):
    near_model = mlp_gate.shape[0]
    tall = 3 * near_model + planes * span
    there = pl.BlockSpec(memory_space=pl.ANY)
    return pl.pallas_call(
        unit_pack_kernel,
        grid_spec=pltpu.PrefetchScalarGridSpec(
            num_scalar_prefetch=1,
            grid=(1,),
            in_specs=[there] * 3,
            out_specs=pl.BlockSpec((tall, near_model), lambda i, s: (0, 0)),
            scratch_shapes=[
                pltpu.VMEM((2, planes, near_model, 256), mlp_gate.dtype),
                pltpu.SemaphoreType.DMA((3 * planes,)),
            ],
        ),
        out_shape=jax.ShapeDtypeStruct((tall, near_model), mlp_gate.dtype),
        compiler_params=pltpu.CompilerParams(vmem_limit_bytes=48 * 1024 * 1024),
        cost_estimate=pl.CostEstimate(flops=0, bytes_accessed=5 << 20, transcendentals=0),
        name="own_unit_pack",
    )(place, mlp_gate, mlp_up, mlp_down)


def in_grads_kernel(
    place_ref,
    near_ref,
    far_ref,
    both_ref,
    back_near_ref,
    back_far_ref,
    gain_ref,
    later_gain_ref,
    small_ref,
    grads_ref,
    sums_ref,
):
    place = place_ref[0]
    chips, rows, model = near_ref.shape
    planes, near_model, _ = grads_ref.shape
    taken, width = small_ref.shape
    near = near_ref[...].reshape(chips * rows, model)
    far = far_ref[...].reshape(chips * rows, model)
    for z in range(planes):
        here = slice(z * near_model, (z + 1) * near_model)
        total = dot_tn(near[:, here], both_ref[0].reshape(chips * rows, -1))
        total = total + dot_tn(far[:, here], both_ref[1].reshape(chips * rows, -1))
        grads_ref[z] = total.astype(grads_ref.dtype)
    gain_sum = jnp.zeros((1, model), jnp.float32)
    for ref, back_ref in ((near_ref, back_near_ref), (far_ref, back_far_ref)):
        for k in range(chips):
            product = ref[k].astype(jnp.float32) * back_ref[k].astype(jnp.float32)
            gain_sum = gain_sum + jnp.sum(product, axis=0, keepdims=True)
    sums_ref[...] = jnp.zeros_like(sums_ref)
    across = model // width
    row = pl.multiple_of(taken * (place // across), taken)
    column = pl.multiple_of(width * lax.rem(place, across), width)
    sums_ref[pl.ds(row, taken), pl.ds(column, width)] = small_ref[...]
    band = model // 3
    for j in range(3):
        here = slice(j * band, (j + 1) * band)
        sums_ref[pl.ds(taken + j, 1), pl.ds(band, band)] = gain_sum[:, here] / gain_ref[:, here]
        sums_ref[pl.ds(taken + 3 + j, 1), pl.ds(band, band)] = later_gain_ref[:, here]


def in_grads(place, near, far, both, back_near, back_far, gain, later_gain, small, planes):
    chips, rows, model = near.shape
    columns = both.shape[-1]
    whole = lambda shape: pl.BlockSpec(shape, lambda i, s: (0,) * len(shape))
    inputs = (near, far, both, back_near, back_far, gain[None], later_gain, small)
    shapes = [
        jax.ShapeDtypeStruct((planes, model // planes, columns), jnp.bfloat16),
        jax.ShapeDtypeStruct((16, model), jnp.float32),
    ]
    return pl.pallas_call(
        in_grads_kernel,
        grid_spec=pltpu.PrefetchScalarGridSpec(
            num_scalar_prefetch=1,
            grid=(1,),
            in_specs=[whole(x.shape) for x in inputs],
            out_specs=[whole(x.shape) for x in shapes],
        ),
        out_shape=shapes,
        compiler_params=pltpu.CompilerParams(vmem_limit_bytes=24 * 1024 * 1024),
        name="in_grads",
    )(place, *inputs)


def payload_kernel(*refs):
    near_ref, got_ref, *extra_refs = refs[: -near_count(refs)]
    own_ref, *out_refs = refs[-near_count(refs) :]
    chips, rows, _ = near_ref.shape
    for k in range(chips):
        total = near_ref[k].astype(jnp.float32) + got_ref[k].astype(jnp.float32)
        if k == 0:
            own_ref[...] = total
        else:
            out_refs[k - 1][pl.ds(0, rows), :] = total.astype(jnp.bfloat16)
            for ref in extra_refs:
                out_refs[k - 1][pl.ds(rows, ref.shape[0]), :] = ref[...]


def near_count(refs):
    return refs[0].shape[0]


def payloads(near, got, extra):
    chips, rows, model = near.shape
    tall = rows + extra.shape[0]
    whole = pl.BlockSpec(memory_space=pltpu.VMEM)
    inputs = (near, got) + ((extra,) if extra.shape[0] else ())
    return pl.pallas_call(
        payload_kernel,
        in_specs=[whole] * len(inputs),
        out_specs=[whole] * chips,
        out_shape=[jax.ShapeDtypeStruct((rows, model), jnp.float32)]
        + [jax.ShapeDtypeStruct((tall, model), jnp.bfloat16)] * (chips - 1),
        compiler_params=pltpu.CompilerParams(vmem_limit_bytes=20 * 1024 * 1024),
        cost_estimate=little,
        name="payloads",
    )(*inputs)


def middle_kernel(tokens_ref, gain_ref, *refs):
    *parts, middle_ref, normed_ref = refs
    total = tokens_ref[...].astype(jnp.float32)
    for ref in parts:
        total = total + ref[...].astype(jnp.float32)
    middle_ref[...] = total
    scale = lax.rsqrt(jnp.mean(total * total, axis=-1, keepdims=True) + norm_eps)
    normed_ref[...] = (total * scale * gain_ref[...]).astype(jnp.bfloat16)


def middle_and_normed(tokens, gain, parts):
    rows, model = tokens.shape
    whole = pl.BlockSpec(memory_space=pltpu.VMEM)
    return pl.pallas_call(
        middle_kernel,
        in_specs=[whole] * (2 + len(parts)),
        out_specs=[whole] * 2,
        out_shape=[
            jax.ShapeDtypeStruct((rows, model), jnp.float32),
            jax.ShapeDtypeStruct((rows, model), jnp.bfloat16),
        ],
        cost_estimate=little,
        name="middle_and_normed",
    )(tokens, gain[None], *parts)


def middle_back_kernel(cot_ref, middle_ref, gain_ref, *refs):
    *parts, grad_ref, low_ref, gain_grad_ref = refs
    middle, gain = middle_ref[...], gain_ref[...]
    upper = parts[0][...]
    for ref in parts[1:]:
        upper = upper + ref[...].astype(jnp.float32)
    scale = lax.rsqrt(jnp.mean(middle * middle, axis=-1, keepdims=True) + norm_eps)
    gain_grad_ref[...] = jnp.sum(upper * middle * scale, axis=0, keepdims=True)
    scaled = gain * upper
    inner = jnp.mean(scaled * middle, axis=-1, keepdims=True)
    grad = cot_ref[...].astype(jnp.float32) + scale * scaled - middle * (scale * scale * scale) * inner
    grad_ref[...] = grad
    low_ref[...] = grad.astype(jnp.bfloat16)


def middle_back(cotangent, middle, gain, parts):
    rows, model = middle.shape
    whole = pl.BlockSpec(memory_space=pltpu.VMEM)
    return pl.pallas_call(
        middle_back_kernel,
        in_specs=[whole] * (3 + len(parts)),
        out_specs=[whole] * 3,
        out_shape=[
            jax.ShapeDtypeStruct((rows, model), jnp.float32),
            jax.ShapeDtypeStruct((rows, model), jnp.bfloat16),
            jax.ShapeDtypeStruct((1, model), jnp.float32),
        ],
        cost_estimate=little,
        name="middle_back",
    )(cotangent, middle, gain[None], *parts)


def halves(value, wanted):
    side = value.shape[1] // 2
    return jnp.where(wanted == 1, pltpu.roll(value, side, 1), value)


def unit_give_kernel(place_ref, *refs):
    *piece_refs, give_ref = refs
    place = place_ref[0]
    chip, core = place // 2, place % 2
    turn = core ^ (chip // 2)
    span = piece_refs[0].shape[0] // 3
    for e in range(2):
        first, second = (piece_refs[i][pl.ds(0, 2 * span), :] for i in (e, 2 + e))
        give_ref[pl.ds(2 * e * span, 2 * span), :] = jnp.where(turn == 0, second, first)
    for e in range(2):
        first, second = (
            halves(piece_refs[2 * e + i][pl.ds(2 * span, span), :].astype(jnp.float32), 1 - core)
            for i in range(2)
        )
        side = first.shape[1] // 2
        lane = lax.broadcasted_iota(jnp.int32, first.shape, 1)
        give_ref[pl.ds((4 + e) * span, span), :] = jnp.where(
            lane < side, first, pltpu.roll(second, side, 1)
        ).astype(give_ref.dtype)


def unit_finish_kernel(place_ref, *refs):
    *piece_refs, got_ref, gate_ref, up_ref, down_ref, down = refs
    place = place_ref[0]
    chip, core = place // 2, place % 2
    turn = core ^ (chip // 2)
    span = piece_refs[0].shape[0] // 3
    side = piece_refs[0].shape[1] // 2
    for e in range(2):
        first, second = (piece_refs[i][pl.ds(0, 2 * span), :] for i in (e, 2 + e))
        mine = jnp.where(turn == 0, first, second).astype(jnp.float32)
        away = got_ref[pl.ds(2 * e * span, 2 * span), :].astype(jnp.float32)
        column = 2 * ((chip % 2) ^ e)
        for value, at in ((mine, column + core), (away, column + 1 - core)):
            rows = pl.ds(pl.multiple_of(at * span, span), span)
            gate_ref[rows, :] = value[:span]
            up_ref[rows, :] = value[span:]
    for k in range(4):
        mine = halves(piece_refs[k][pl.ds(2 * span, span), :].astype(jnp.float32), core)
        away = halves(got_ref[pl.ds((4 + k // 2) * span, span), :].astype(jnp.float32), k % 2)
        for value, at in ((mine, core), (away, 1 - core)):
            row = pl.multiple_of((2 * (chip ^ k) + at) * span, span)
            down[pl.ds(row, span), :] = value[:, :side]
    down_ref[...] = down[...].T


def unit_pieces(total, chip):
    chips = total.shape[0]
    pieces = [
        lax.dynamic_index_in_dim(total, chip ^ k, 0, keepdims=False) for k in range(chips)
    ]
    return [pieces[0]] + [chip_swap(pieces[k], k) for k in range(1, chips)]


def unit_exchange(place, pieces):
    chips = len(pieces)
    tall, cols = pieces[0].shape
    span = tall // 3
    fixed = lambda shape: pl.BlockSpec(shape, lambda i, s: (0,) * len(shape))
    give = pl.pallas_call(
        unit_give_kernel,
        grid_spec=pltpu.PrefetchScalarGridSpec(
            num_scalar_prefetch=1,
            grid=(1,),
            in_specs=[fixed((tall, cols))] * chips,
            out_specs=fixed((6 * span, cols)),
        ),
        out_shape=jax.ShapeDtypeStruct((6 * span, cols), pieces[0].dtype),
        name="unit_give",
    )(place, *pieces)
    shapes = [(4 * span, cols), (4 * span, cols), (cols // 2, 2 * chips * span)]
    grads = pl.pallas_call(
        unit_finish_kernel,
        grid_spec=pltpu.PrefetchScalarGridSpec(
            num_scalar_prefetch=1,
            grid=(1,),
            in_specs=[fixed((tall, cols))] * chips + [fixed((6 * span, cols))],
            out_specs=[fixed(shape) for shape in shapes],
            scratch_shapes=[pltpu.VMEM((2 * chips * span, cols // 2), jnp.float32)],
        ),
        out_shape=[jax.ShapeDtypeStruct(shape, jnp.float32) for shape in shapes],
        compiler_params=pltpu.CompilerParams(vmem_limit_bytes=32 * 1024 * 1024),
        name="unit_finish",
    )(place, *pieces, core_swap(give))
    return [grad.T for grad in grads]


def grad_pack_kernel(place_ref, in_ref, *refs):
    *blocks, pack_ref = refs
    place = place_ref[0]
    chips = len(blocks) // 2
    chip, core = place // 2, place % 2
    near_model, both = in_ref.shape[1:]
    tall, width = blocks[0].shape
    pack_ref[:, pl.ds(0, near_model), :] = in_ref[...]
    for k in range(chips):
        home, away = blocks[k][...], blocks[chips + k][...]
        odd = core == 1
        pack_ref[chip ^ k, pl.ds(near_model, tall), pl.ds(0, width)] = jnp.where(odd, away, home)
        pack_ref[chip ^ k, pl.ds(near_model, tall), pl.ds(width, width)] = jnp.where(odd, home, away)


def grad_pack(place, in_grad, home, away):
    planes, near_model, both = in_grad.shape
    tall, width = home[0].shape
    return pl.pallas_call(
        grad_pack_kernel,
        grid_spec=pltpu.PrefetchScalarGridSpec(
            num_scalar_prefetch=1,
            grid=(1,),
            in_specs=[pl.BlockSpec(in_grad.shape, lambda i, s: (0, 0, 0))]
            + [pl.BlockSpec((tall, width), lambda i, s: (0, 0))] * (2 * len(home)),
            out_specs=pl.BlockSpec((planes, near_model + tall, both), lambda i, s: (0, 0, 0)),
        ),
        out_shape=jax.ShapeDtypeStruct((planes, near_model + tall, both), jnp.bfloat16),
        compiler_params=pltpu.CompilerParams(vmem_limit_bytes=16 * 1024 * 1024),
        name="grad_pack",
    )(place, in_grad, *home, *away)


def mix_results_kernel(sum_ref, *refs):
    row = 0
    width = sum_ref.shape[1] // 2
    for j, ref in enumerate(refs):
        rows = ref.shape[0]
        if j < 2:
            ref[...] = sum_ref[pl.ds(0, rows), pl.ds(j * width, width)].astype(jnp.float32)
            row = rows
        else:
            ref[...] = sum_ref[pl.ds(row, rows), :].astype(jnp.float32)
            row += rows


def mix_results(total, near_model, slim):
    tall, both = total.shape
    piece = (tall - near_model - slim) // 2
    shapes = [(near_model, both // 2)] * 2 + [(slim, both), (piece, both), (piece, both)]
    whole = pl.BlockSpec(memory_space=pltpu.VMEM)
    found = pl.pallas_call(
        mix_results_kernel,
        in_specs=[whole],
        out_specs=[whole] * len(shapes),
        out_shape=[jax.ShapeDtypeStruct(shape, jnp.float32) for shape in shapes],
        name="mix_results",
    )(total)
    return [*found[:2], *[grad.T for grad in found[2:]]]


def norm_back(values, scale, gain, grad):
    inner = jnp.mean(gain * grad * values, axis=-1, keepdims=True)
    return scale * gain * grad - values * (scale * scale * scale) * inner


def narrow_shards(
    tokens,
    cotangent,
    doc_starts,
    mix_gain,
    input_proj,
    gelu_proj,
    conv_taps,
    conv_bias,
    decay_gate,
    decay_bias,
    input_gate,
    input_bias,
    decay_param,
    output_proj,
    mlp_gain,
    mlp_gate,
    mlp_up,
    mlp_down,
):
    f32, bf16 = jnp.float32, jnp.bfloat16
    devices, planes = lax.axis_size("seq"), lax.axis_size("fsdp")
    chips = devices // 2
    place, plane = lax.axis_index("seq"), lax.axis_index("fsdp")
    chip, core = place // 2, place % 2
    rows, model = tokens.shape[1:]
    length = rows * devices
    channels = conv_taps.shape[1]
    width = decay_gate.shape[1]
    deep = mlp_gate.shape[1]
    heads = output_proj.shape[0] // width
    piece = width // devices
    span = deep // (planes * devices)
    part = deep // devices
    near_model = model // planes

    def along_fsdp(x):
        return lax.all_gather(x, "fsdp", axis=0, tiled=True)

    def columns(x, start, size):
        return lax.dynamic_slice_in_dim(x, start, size, axis=1)

    place_arg = place.astype(jnp.int32)[None]
    in_own, rowset = own_mix_pack(
        place_arg, input_proj, gelu_proj, output_proj, decay_gate, input_gate
    )
    in_own, rowset, tokens = tie(in_own, rowset, tokens)
    in_weights = lax.all_gather(in_own, "fsdp", axis=0)
    by_plane = [plane_swap(rowset, k) for k in range(planes)]

    values = tokens[0].astype(f32)
    scale1 = lax.rsqrt(jnp.mean(values * values, axis=-1, keepdims=True) + norm_eps)
    normed_own, mlp_gate, mlp_up, mlp_down = tie(
        (values * scale1 * mix_gain).astype(bf16), mlp_gate, mlp_up, mlp_down
    )
    normed_near, normed_far = gather_blocks(normed_own)
    unit_pack = own_unit_pack(place_arg, mlp_gate, mlp_up, mlp_down, planes, span)
    unit_pack, normed_near, normed_far = tie(unit_pack, normed_near, normed_far)
    unit_pack = lax.all_gather(unit_pack, "fsdp", axis=0)
    chan, age = tables(
        doc_starts[0], conv_taps, conv_bias, decay_bias, input_bias, decay_param, length
    )
    normed_near, normed_far, out_grad = tie(normed_near, normed_far, cotangent[0])
    cot_got = [chip_swap(out_grad, k) for k in range(1, chips)]
    held = tie(normed_near, normed_far, chan, age, *by_plane, *cot_got)
    normed_near, normed_far, chan, age = held[:4]
    by_plane, cot_got = held[4 : 4 + planes], held[4 + planes :]

    pre_near, pre_far = (
        dot_nn(x.reshape(-1, model), in_weights.reshape(model, 2 * width)).reshape(
            chips, rows, 2 * width
        )
        for x in (normed_near, normed_far)
    )
    keep, got, pre_near, pre_far = exchange(
        jnp.stack(by_plane), chip, core, plane, [pre_near, pre_far]
    )
    merged, middle_near, middle_far, *saved, weights = mix_forward(
        place_arg, pre_near, pre_far, age, chan, keep, got
    )
    cot_near = jnp.stack([out_grad, *cot_got])
    cot_far = core_swap(cot_near)
    middle, normed2 = middle_and_normed(
        tokens[0], mlp_gain, spread_pairs(*pair_blocks(middle_near, middle_far))
    )

    near, far = gather_blocks(normed2)
    back_near, back_far, hidden, down, unit_grads = unit_back_and_forth(
        near, far, cot_near, cot_far, unit_pack, part
    )
    unit_sum = lax.psum_scatter(unit_grads, "fsdp", scatter_dimension=0, tiled=False)

    middle_grad, middle_low, mlp_gain_term = middle_back(
        out_grad, middle, mlp_gain, spread_pairs(*pair_blocks(back_near, back_far))
    )
    middle_low, hidden, down = tie(middle_low, hidden, down)
    mixed_near, mixed_far = mixed_parts(hidden, down, chips)
    mixed_own, *mixed_low = pair_blocks(mixed_near, mixed_far)
    first, *others = [chip_swap(middle_low, k) for k in range(1, chips)]
    first, mixed_own, *mixed_low = tie(first, mixed_own, *mixed_low)
    near = jnp.stack([middle_low, first, *others])
    far = core_swap(near)

    both, small, back_near, back_far, *by_chip = mix_backward(
        place_arg, near, far, age, chan, weights, in_weights, merged, saved
    )
    mixed_got = [chip_swap(block, k + 1) for k, block in enumerate(mixed_low)]
    held = tie(*mixed_got, *by_chip)
    mixed_got, by_chip = held[: chips - 1], held[chips - 1 :]
    arrived = [by_chip[0]] + [chip_swap(by_chip[k], k) for k in range(1, chips)]
    arrived[1], both, back_near, back_far, small = tie(
        arrived[1], both, back_near, back_far, small
    )
    in_pack, sums = in_grads(
        place_arg,
        normed_near,
        normed_far,
        both,
        back_near,
        back_far,
        mix_gain,
        mlp_gain_term,
        small,
        planes,
    )
    sums = sums + core_swap(sums)
    *arrived, in_pack = tie(*arrived, in_pack)
    away = core_swap(jnp.stack([block[1] for block in arrived]))
    pack, unit_sum, back_near, back_far, *mixed_got = tie(
        grad_pack(
            place_arg,
            in_pack,
            [block[0] for block in arrived],
            [away[k] for k in range(chips)],
        ),
        unit_sum,
        back_near,
        back_far,
        *mixed_got,
    )
    normed_own, *normed_low = pair_blocks(back_near, back_far)
    mixed = mixed_own
    for got in mixed_got:
        mixed = mixed + got.astype(f32)
    mixed = (middle + mixed).astype(bf16)
    mix_sum = lax.psum_scatter(pack, "fsdp", scatter_dimension=0, tiled=False)
    (
        input_proj_grad,
        gelu_proj_grad,
        output_proj_grad,
        decay_gate_grad,
        input_gate_grad,
    ) = mix_results(mix_sum, near_model, model // devices)

    pieces = unit_pieces(unit_sum.reshape(planes, 3 * span, near_model), chip)
    pieces[1], sums, *normed_low = tie(pieces[1], sums, *normed_low)
    normed_grad = normed_own
    for k in range(1, chips):
        normed_grad = normed_grad + chip_swap(normed_low[k - 1], k).astype(f32)
    values_part = norm_back(values, scale1, mix_gain, normed_grad)
    tokens_grad = (middle_grad + values_part).astype(bf16)

    low = sums.astype(bf16)
    for k in range(1, chips):
        sums = sums + chip_swap(low, k).astype(f32)
    sums = over_planes(sums)
    sums, *pieces = tie(sums, *pieces)
    channel_sums = jnp.concatenate([sums[:8], sums[8:, : channels - model]], axis=1)
    band = model // 3
    gain_sums = sums[8:14, band : 2 * band].reshape(2, model)
    mlp_gate_grad, mlp_up_grad, mlp_down_grad = unit_exchange(place_arg, pieces)

    return (
        mixed[None],
        tokens_grad[None],
        gain_sums[0],
        input_proj_grad,
        gelu_proj_grad,
        channel_sums[:4],
        channel_sums[4],
        decay_gate_grad,
        channel_sums[5],
        input_gate_grad,
        channel_sums[6],
        channel_sums[7],
        output_proj_grad,
        gain_sums[1],
        mlp_gate_grad,
        mlp_up_grad,
        mlp_down_grad,
    )


def choose_plan(mesh):
    devices, planes = mesh.shape["seq"], mesh.shape["fsdp"]

    def plan(*args):
        channels, width = args[6].shape[1], args[8].shape[1]
        if channels == width * devices and devices == 2 * planes and planes == 4:
            return narrow_shards(*args)
        return wide_shards(*args)

    return plan


def solution(mesh):
    return jax.shard_map(
        choose_plan(mesh),
        mesh=mesh,
        in_specs=(
            P("fsdp", "seq", None),
            P("fsdp", "seq", None),
            P("fsdp", None),
            P(),
            P("fsdp", None),
            P("fsdp", None),
            P(),
            P(),
            P("fsdp", None),
            P(),
            P("fsdp", None),
            P(),
            P(),
            P("fsdp", None),
            P(),
            P("fsdp", None),
            P("fsdp", None),
            P("fsdp", None),
        ),
        out_specs=(
            P("fsdp", "seq", None),
            P("fsdp", "seq", None),
            P(),
            P("fsdp", "seq"),
            P("fsdp", "seq"),
            P(),
            P(),
            P("fsdp", "seq"),
            P(),
            P("fsdp", "seq"),
            P(),
            P(),
            P("fsdp", "seq"),
            P(),
            P("fsdp", "seq"),
            P("fsdp", "seq"),
            P("fsdp", "seq"),
        ),
        check_vma=False,
    )
```
